512 devices in a mesh: gx: 64 (over y, z), gy: 8 (over x, core).
Axes of the slice: x: 4, y: 8, z: 8, core: 2. Of those that a mesh axis runs over, the one named last changes fastest.
Arguments:
- velocity: float32 [2048, 256, 128], P('gx', 'gy'), may hold values from -6 to 6
Outputs:
- coefficients: float32 [2048, 256, 128], P('gx', 'gy')
The draws below stay inside these ranges and needn't reach their ends.
All inputs are finite; a program needn't handle non-finite values.
Results may differ from the reference program's by a relative error of at most 0.00002.
Values sent between devices are 32-bit elements; how exact they have to be, the bound alone decides.
A program may use at most 128 MiB of HBM per device.

```python
import jax
import jax.numpy as jnp
from jax import lax

NZ = 128
LEVELS = 4
NX = 2048
NY = 256


def shard_levels(rng, extent, shards, least, high):
    level, own = 1.0, jax.random.fold_in(rng, 6)
    for dim, shards_of in shards:
        draws = jnp.exp(jax.random.uniform(jax.random.fold_in(own, dim), (shards_of,), jnp.float32, least / len(shards), high / len(shards)))
        level = level * jnp.repeat(draws, extent[dim] // shards_of).reshape([-1 if axis == dim else 1 for axis in range(len(extent))])
    return level


def normal_values(stream_key, dims, spread, bound, shards=(), dtype=jnp.bfloat16):
    result = jax.random.normal(stream_key, dims, jnp.float32) * spread
    if len(shards) > 0:
        result = shard_levels(stream_key, dims, shards, -0.22, 0.18) * result
    return jnp.clip(result, min=-bound, max=bound).astype(dtype)


def setup_inputs(seed: int = 0) -> dict:
    key_of = jax.random.split(jax.random.key(seed), 2)
    velocity = normal_values(key_of[0], (NX, NY, NZ), 1.0, 6.0, ((0, 64), (1, 8)), jnp.float32)
    return dict(velocity=velocity)


lift_alpha = -1.586134342
lift_beta = -0.05298011854
lift_gamma = 0.8829110762
lift_delta = 0.4435068522
lift_scale = 1.149604398


def lift_core(even, odd, forward, backward):
    odd = odd + lift_alpha * (even + forward(even))
    even = even + lift_beta * (backward(odd) + odd)
    odd = odd + lift_gamma * (even + forward(even))
    even = even + lift_delta * (backward(odd) + odd)
    return even / lift_scale, odd * lift_scale


def periodic_split(array, axis):
    count = array.shape[axis]
    even = lax.slice_in_dim(array, 0, count, 2, axis)
    odd = lax.slice_in_dim(array, 1, count, 2, axis)

    def forward(values):
        return jnp.roll(values, -1, axis)

    def backward(values):
        return jnp.roll(values, 1, axis)

    return lift_core(even, odd, forward, backward)


def split_level(array):
    low, high = periodic_split(array, 0)
    bands = jnp.stack([low, high])
    low, high = periodic_split(bands, 2)
    bands = jnp.stack([low, high])
    low, high = periodic_split(bands, 4)
    return jnp.stack([low, high])


def alternate(bands):
    size_x, size_y, size_z = bands.shape[3], bands.shape[4], bands.shape[5]
    return jnp.transpose(bands, (3, 2, 4, 1, 5, 0)).reshape(2 * size_x, 2 * size_y, 2 * size_z)


def decompose(array, level):
    bands = split_level(array)
    if level < LEVELS:
        coarse = decompose(bands[0, 0, 0], level + 1)
        bands = bands.at[0, 0, 0].set(coarse)
    return alternate(bands)


def reference(velocity):
    return decompose(velocity, 1)
```

```python
import jax
import jax.numpy as jnp
import numpy as np
from jax import lax
from jax.experimental import pallas as pl
from jax.experimental.pallas import tpu as pltpu
from jax.sharding import PartitionSpec as P

LIFT_A, LIFT_B, LIFT_C, LIFT_D = -1.586134342, -0.05298011854, 0.8829110762, 0.4435068522
LIFT_K = 1.149604398
MESH = pl.DeviceIdType.MESH
HIGHEST = lax.Precision.HIGHEST
F32 = jnp.float32

X_COUNT = {0: 20, -1: 8, 1: 8, -2: 2, 2: 2}
X_PAIR = {0: (0, 10), -1: (10, 4), 1: (14, 4), -2: (18, 1), 2: (19, 1)}
Y_ROWS = {0: (0, 24), -1: (24, 8), 1: (32, 8), -2: (40, 8), 2: (48, 8)}
PAIRS, ROWS = 20, 56
OTHERS = [(dx, dy) for dx in (-1, 1, 0, -2, 2) for dy in (0, -1, 1, -2, 2) if (dx, dy) != (0, 0)]


def lift_1d(v):
    even, odd = v[0::2], v[1::2]
    odd = odd + LIFT_A * (even + np.roll(even, -1, 0))
    even = even + LIFT_B * (np.roll(odd, 1, 0) + odd)
    odd = odd + LIFT_C * (even + np.roll(even, -1, 0))
    even = even + LIFT_D * (np.roll(odd, 1, 0) + odd)
    return even / LIFT_K, odd * LIFT_K


def interleave(low, high):
    out = np.empty((2 * low.shape[0], low.shape[1]))
    out[0::2], out[1::2] = low, high
    return out


def operators():
    n, blocks, mid = 32, 16, 8
    low, levels = np.eye(n * blocks), {}
    for level in range(1, 5):
        low, high = lift_1d(low)
        m = n >> level
        levels[level] = interleave(low[mid * m:(mid + 1) * m], high[mid * m:(mid + 1) * m])
    upper = np.concatenate([levels[2], levels[3], levels[4]])
    functional, combine = {}, {}
    for offset, count in X_COUNT.items():
        part = upper[:, (mid + offset) * n:(mid + offset + 1) * n]
        basis = np.linalg.svd(part)[2][:count]
        functional[offset], combine[offset] = basis, part @ basis.T
    fx = np.concatenate([functional[o][h * c // 2:(h + 1) * c // 2] for h in (0, 1) for o, c in X_COUNT.items()])
    cx = np.concatenate([combine[o][:, h * c // 2:(h + 1) * c // 2] for h in (0, 1) for o, c in X_COUNT.items()], 1)
    kx = np.kron(fx, np.eye(8))
    fy, cy = np.zeros((ROWS, 32)), np.zeros((28, ROWS))
    for offset, count in X_COUNT.items():
        at = Y_ROWS[offset][0]
        fy[at:at + count], cy[:, at:at + count] = functional[offset], combine[offset]
    ty = np.zeros((32, ROWS))
    ty[0:8], ty[8:16], ty[16:24], ty[24:32:2] = cy[0:16:2], cy[1:16:2], cy[16:24], cy[24:28]
    tx = [np.stack([np.kron(cx[rows, h * PAIRS:(h + 1) * PAIRS], np.eye(8)) for h in (0, 1)]) for rows in (slice(0, 16), slice(16, 24), slice(24, 28))]
    low, high = lift_1d(np.eye(128))
    z1, zl = interleave(low, high).T, low.T
    zp = np.zeros((2, 128, 128))
    zp[0, :, :64], zp[1, :, 64:] = zl, zl
    low, zu = np.eye(64), np.zeros((3, 2, 128, 128))
    for level in range(3):
        low, high = lift_1d(low)
        for h in (0, 1):
            zu[level, h, 64 * h:64 * (h + 1), ::2 << level] = interleave(low, high).T
    return [np.asarray(m, np.float32) for m in (kx, fy, z1, zp, ty, *tx, zu)]


def dot(a, b):
    return lax.dot_general(a, b, (((1,), (0,)), ((), ())), precision=HIGHEST, preferred_element_type=F32)


def states(s):
    a = s(31) + LIFT_A * s(30)
    b = s(30) + LIFT_B * (s(29) + LIFT_A * (s(28) + s(30)))
    c = s(0)
    d = s(0) + LIFT_B * (s(1) + LIFT_A * (s(0) + s(2)))
    return a, b, c, d


def prepare(v_ref, kx_ref, fy_ref, z1_ref, zp_ref, zt_ref, vo_ref, xh_ref, yh_ref, ch_ref, xf_ref):
    for t in range(4):
        block = v_ref[:, 8 * t:8 * t + 8, :].reshape(256, 128)
        xf_ref[:, 8 * t:8 * t + 8, :] = dot(kx_ref[...], block).reshape(2 * PAIRS, 8, 128)
        zt_ref[:, 8 * t:8 * t + 8, :] = dot(block, z1_ref[...]).reshape(32, 8, 128)
    packed = dot(xf_ref[:PAIRS].reshape(PAIRS * 32, 128), zp_ref[0]) + dot(xf_ref[PAIRS:].reshape(PAIRS * 32, 128), zp_ref[1])
    packed = packed.reshape(PAIRS, 32, 128)
    for p in range(PAIRS):
        vo_ref[p] = dot(fy_ref[...], packed[p])
    for q, plane in enumerate(states(lambda x: zt_ref[x])):
        xh_ref[q] = plane
    for q, rows in enumerate(states(lambda y: zt_ref[:, y, :])):
        yh_ref[q] = rows
    for q in range(4):
        for p, row in enumerate(states(lambda y: xh_ref[q, y:y + 1, :])):
            at = (q // 2) * 2 + p // 2
            ch_ref[at, (q % 2) * 2 + p % 2:(q % 2) * 2 + p % 2 + 1, :] = row
    ch_ref[:, 4:8, :] = jnp.zeros((4, 4, 128), F32)


def exchange(nx, ny, vo_ref, xh_ref, yh_ref, ch_ref, vi_ref, xi_ref, yi_ref, ci_ref, send, recv):
    x, y = lax.axis_index("gx"), lax.axis_index("gy")

    def device(dx, dy):
        return lax.rem(x + dx + nx, nx), lax.rem(y + dy + ny, ny)

    barrier = pltpu.get_barrier_semaphore()
    for dx, dy in OTHERS:
        pl.semaphore_signal(barrier, inc=1, device_id=device(dx, dy), device_id_type=MESH)
    pl.semaphore_wait(barrier, len(OTHERS))
    moves = []
    for dx, dy in OTHERS:
        pieces = []
        if abs(dx) + abs(dy) == 1:
            source, target = (xh_ref, xi_ref) if dx else (yh_ref, yi_ref)
            piece = pl.ds(0 if dx + dy < 0 else 2, 2)
            pieces.append((source.at[piece], target.at[piece]))
        elif abs(dx) == 1 and abs(dy) == 1:
            piece = (dx + 1) + (dy + 1) // 2
            pieces.append((ch_ref.at[piece], ci_ref.at[piece]))
        (p, np_), (r, nr) = X_PAIR[dx], Y_ROWS[dy]
        pieces.append((vo_ref.at[pl.ds(p, np_), pl.ds(r, nr)], vi_ref.at[pl.ds(p, np_), pl.ds(r, nr)]))
        moves += [(source, target, device(-dx, -dy)) for source, target in pieces]
    copies = []
    for i, (source, target, to) in enumerate(moves):
        copy = pltpu.make_async_remote_copy(
            src_ref=source, dst_ref=target, send_sem=send.at[i], recv_sem=recv.at[i], device_id=to, device_id_type=MESH)
        copy.start()
        copies.append(copy)
    for copy in copies:
        copy.wait_recv()
    for copy in copies:
        copy.wait_send()


N_COPIES = 24 + 8


def split_y(p, halo, first, last):
    a, b, c, d = halo
    p0, p1, p2, p3 = p

    def following(v, edge):
        return jnp.where(last, edge, pltpu.roll(v, 7, 0))

    def preceding(v, edge):
        return jnp.where(first, edge, pltpu.roll(v, 1, 0))

    o0 = p1 + LIFT_A * (p0 + p2)
    o1 = p3 + LIFT_A * (p2 + following(p0, c))
    before = a + LIFT_A * p0
    e0 = p0 + LIFT_B * (preceding(o1, before) + o0)
    e1 = p2 + LIFT_B * (o0 + o1)
    q0 = o0 + LIFT_C * (e0 + e1)
    q1 = o1 + LIFT_C * (e1 + following(e0, d + LIFT_B * o1))
    before = before + LIFT_C * (b + LIFT_B * before + e0)
    f0 = e0 + LIFT_D * (preceding(q1, before) + q0)
    f1 = e1 + LIFT_D * (q0 + q1)
    return f0 * (1 / LIFT_K), q0 * LIFT_K, f1 * (1 / LIFT_K), q1 * LIFT_K


def finish(zt_ref, vo_ref, vi_ref, xi_ref, yi_ref, ci_ref, ty_ref, t2_ref, t3_ref, t4_ref, zu_ref, out_ref, ys, tt, up, done, sems):
    sub = lax.broadcasted_iota(jnp.int32, (8, 128), 0)
    lane = lax.broadcasted_iota(jnp.int32, (8, 128), 1)
    first, last = sub == 0, sub == 7

    def row(ref, *at):
        return jnp.broadcast_to(ref[(*at[:-1], pl.ds(at[-1], 1), slice(None))], (8, 128))

    own_p, own_r = X_PAIR[0][1], Y_ROWS[0][1]
    for p in range(PAIRS):
        if p < own_p:
            v = jnp.concatenate([vo_ref[p, 0:own_r, :], vi_ref[p, own_r:ROWS, :]], 0)
        else:
            v = vi_ref[p]
        r = dot(ty_ref[...], v)
        for t in range(4):
            tt[t, p] = r[8 * t:8 * t + 8]

    def upper(t_ref, t, level):
        v = tt[t].reshape(PAIRS * 8, 128)
        return dot(dot(t_ref[0], v), zu_ref[level, 0]) + dot(dot(t_ref[1], v), zu_ref[level, 1])

    l2 = [upper(t2_ref, t, 0).reshape(16, 8, 128) for t in (0, 1)]
    l3 = upper(t3_ref, 2, 1).reshape(8, 8, 128)
    l4 = upper(t4_ref, 3, 2).reshape(4, 8, 128)
    for i in range(16):
        for t in (0, 1):
            v = l2[t][i]
            if i % 2 == 0 and t == 0:
                w = l3[i // 2]
                if i % 4 == 0:
                    w = jnp.where((lane % 8 == 0) & (sub % 2 == 0), l4[i // 4], w)
                v = jnp.where(lane % 4 == 0, w, v)
            up[i, t] = v

    for x in range(36):
        if 2 <= x < 34:
            p = [zt_ref[x - 2, pl.ds(r, 8, 4), :] for r in range(4)]
            halo = [row(yi_ref, q, x - 2) for q in range(4)]
        else:
            q = x if x < 2 else x - 32
            p = [xi_ref[q, pl.ds(r, 8, 4), :] for r in range(4)]
            at = 2 * (q // 2)
            halo = [row(ci_ref, at + k // 2, (q % 2) * 2 + k % 2) for k in range(4)]
        for r, v in enumerate(split_y(p, halo, first, last)):
            ys[x, r] = v

    odd_lane = lane % 2 == 1
    state = {}
    copies = []
    for r in range(4):
        before = ys[0, r] + LIFT_A * ys[2, r]
        state[r] = (before, ys[1, r] + LIFT_B * before, None)
    for i in range(17):
        for r in range(4):
            o, e, q = state[r]
            if i < 16:
                p = ys[2 + 2 * i, r]
                o_now = ys[3 + 2 * i, r] + LIFT_A * (p + ys[4 + 2 * i, r])
                e_now = p + LIFT_B * (o + o_now)
            else:
                o_now, e_now = None, ys[35, r] + LIFT_B * o
            q_now = o + LIFT_C * (e + e_now)
            if i > 0:
                low = (e + LIFT_D * (q + q_now)) * (1 / LIFT_K)
                if r % 2 == 0:
                    low = jnp.where(odd_lane, low, up[i - 1, r // 2])
                done[2 * i - 2, pl.ds(r, 8, 4), :] = low
                done[2 * i - 1, pl.ds(r, 8, 4), :] = q_now * LIFT_K
            state[r] = (o_now, e_now, q_now)
        if i in (4, 8, 12, 16):
            piece = pl.ds(2 * i - 8, 8)
            copy = pltpu.make_async_copy(done.at[piece], out_ref.at[piece], sems.at[i // 4 - 1])
            copy.start()
            copies.append(copy)
    for copy in copies:
        copy.wait()


def solution(mesh):
    nx, ny = mesh.shape["gx"], mesh.shape["gy"]
    kx, fy, z1, zp, ty, t2, t3, t4, zu = operators()
    vmem = pl.BlockSpec(memory_space=pltpu.VMEM)
    limit = 24 * 1024 * 1024
    halos = [(PAIRS, ROWS, 128), (4, 32, 128), (4, 32, 128), (4, 8, 128)]

    def local(v):
        zt, vo, xh, yh, ch = pl.pallas_call(
            prepare,
            out_shape=[KEEP(s, F32) for s in [(32, 32, 128), *halos]],
            in_specs=[vmem] * 5, out_specs=[vmem] * 5,
            scratch_shapes=[pltpu.VMEM((2 * PAIRS, 32, 128), F32)],
            compiler_params=pltpu.CompilerParams(vmem_limit_bytes=limit),
        )(v, kx, fy, z1, zp)
        vi, xi, yi, ci = pl.pallas_call(
            lambda *refs: exchange(nx, ny, *refs),
            out_shape=[KEEP(s, F32) for s in halos],
            in_specs=[vmem] * 4, out_specs=[vmem] * 4,
            scratch_shapes=[pltpu.SemaphoreType.DMA((N_COPIES,)), pltpu.SemaphoreType.DMA((N_COPIES,))],
            compiler_params=pltpu.CompilerParams(collective_id=0, has_side_effects=True, vmem_limit_bytes=limit),
        )(vo, xh, yh, ch)
        return pl.pallas_call(
            finish,
            out_shape=jax.ShapeDtypeStruct((32, 32, 128), F32),
            in_specs=[vmem] * 11, out_specs=pl.BlockSpec(memory_space=pl.ANY),
            scratch_shapes=[
                pltpu.VMEM((36, 4, 8, 128), F32), pltpu.VMEM((4, PAIRS, 8, 128), F32), pltpu.VMEM((16, 2, 8, 128), F32),
                pltpu.VMEM((32, 32, 128), F32), pltpu.SemaphoreType.DMA((4,))],
            compiler_params=pltpu.CompilerParams(vmem_limit_bytes=limit),
        )(zt, vo, vi, xi, yi, ci, ty, t2, t3, t4, zu)

    spec = P("gx", "gy", None)
    return jax.shard_map(local, mesh=mesh, in_specs=(spec,), out_specs=spec, check_vma=False)


def KEEP(shape, dtype):
    return pltpu.VMEM(shape, dtype)
```

```python
import functools

import jax
import jax.numpy as jnp
import ml_dtypes
import numpy as np
from jax import lax
from jax.experimental import pallas as pl
from jax.experimental.pallas import tpu as pltpu
from jax.sharding import PartitionSpec as P

LIFT_A, LIFT_B, LIFT_C, LIFT_D = -1.586134342, -0.05298011854, 0.8829110762, 0.4435068522
LIFT_K = 1.149604398
MESH = pl.DeviceIdType.MESH
F32, BF16 = jnp.float32, jnp.bfloat16

COUNT = {0: 20, 1: 8, 2: 2, -1: 8, -2: 2}
X_AT = {0: 0, 1: 18, 2: 24, -1: 25, -2: 31}
Y_AT = {0: 0, -1: 32, 1: 40, -2: 48, 2: 56}
ENTRIES, ROWS = 32, 64
PAIRS = [X_AT[o] + p for o, c in COUNT.items() for p in range(c // 2)]
EARLY = 15
Y_STATES = 10
X_STATES = {1: 22, -1: 29}
OFFSETS = (0, -1, 1, -2, 2)
GROUP = {dx: [(dx, dy) for dy in OFFSETS if (dx, dy) != (0, 0)] for dx in OFFSETS}


def pieces(dx, dy):
    rows = (Y_AT[dy], 8)
    if dx == 0:
        return [((0, 18 if abs(dy) == 1 else 2), rows)]
    if abs(dx) == 2:
        return [((X_AT[dx], 1), rows)]
    if dy == 0:
        return [((X_STATES[dx], 2), (0, 32)), ((X_AT[dx], 4), (0, 24))]
    return [((X_AT[dx], 5 if abs(dy) == 1 else 2), rows)]


MOVES = [(o, piece) for dx in OFFSETS for o in GROUP[dx] for piece in pieces(*o)]


def lift_1d(v):
    even, odd = v[0::2], v[1::2]
    odd = odd + LIFT_A * (even + np.roll(even, -1, 0))
    even = even + LIFT_B * (np.roll(odd, 1, 0) + odd)
    odd = odd + LIFT_C * (even + np.roll(even, -1, 0))
    even = even + LIFT_D * (np.roll(odd, 1, 0) + odd)
    return even / LIFT_K, odd * LIFT_K


def interleave(low, high):
    out = np.empty((2 * low.shape[0], low.shape[1]))
    out[0::2], out[1::2] = low, high
    return out


def row_space(parts, count):
    basis = np.zeros((0, parts[0].shape[1]))
    for part in parts:
        rest = part - part @ basis.T @ basis
        size, rows = np.linalg.svd(rest)[1:]
        basis = np.concatenate([basis, rows[:int((size > 1e-9).sum())]])
    return np.concatenate([basis, np.zeros((count - len(basis), basis.shape[1]))])


def halves(matrix):
    high = np.asarray(matrix, np.float32).astype(ml_dtypes.bfloat16)
    return high, (np.asarray(matrix, np.float32) - high.astype(np.float32)).astype(ml_dtypes.bfloat16)


def operators():
    n, blocks, mid = 32, 16, 8
    low, levels = np.eye(n * blocks), {}
    for level in range(1, 5):
        low, high = lift_1d(low)
        m = n >> level
        levels[level] = interleave(low[mid * m:(mid + 1) * m], high[mid * m:(mid + 1) * m])
    functional, combine = {}, {}
    for offset, count in COUNT.items():
        parts = [levels[level][:, (mid + offset) * n:(mid + offset + 1) * n] for level in (4, 3, 2)]
        functional[offset] = row_space(parts, count)
        combine[offset] = np.concatenate(parts[::-1]) @ functional[offset].T
    fx = np.concatenate([functional[o][h::2] for h in (0, 1) for o in COUNT])
    kx = np.stack(halves(np.kron(fx, np.eye(8))))
    cx = [np.concatenate([combine[o][:, h::2] for o in COUNT], 1) for h in (0, 1)]
    early, late = [np.stack([np.kron(c[:, part], np.eye(8)) for c in cx]) for part in (slice(0, EARLY), slice(EARLY, None))]
    (high, low), (late_high, late_low) = halves(early), halves(late)
    early = np.stack([np.concatenate([high, high], 2), np.concatenate([low, np.zeros_like(low)], 2)])
    late = np.concatenate([late_high, late_high, late_low], 2)
    fy, cy = np.zeros((ROWS, 32)), np.zeros((28, ROWS))
    for offset, count in COUNT.items():
        at = Y_AT[offset]
        fy[at:at + count], cy[:, at:at + count] = functional[offset], combine[offset]
    ty = np.zeros((32, ROWS))
    ty[0:8], ty[8:16], ty[16:24], ty[24:32:2] = cy[0:16:2], cy[1:16:2], cy[16:24], cy[24:28]
    fy, ty = [np.concatenate([h, h, l], 1) for h, l in (halves(fy), halves(ty))]
    low, high = lift_1d(np.eye(128))
    z1 = wide(interleave(low, high).T)
    zp = np.concatenate(halves(np.kron(np.eye(2), low.T)), 1)
    low, zu = np.eye(64), np.zeros((3, 64, 128))
    for level in range(3):
        low, high = lift_1d(low)
        zu[level, :, ::2 << level] = interleave(low, high).T
    zu = np.stack([wide(np.concatenate([m, m])) for m in zu])
    return [tiles(m) for m in (kx, fy, z1, zp, ty, early, late, zu)]


def wide(matrix):
    high, low = halves(matrix)
    return np.concatenate([np.concatenate([high, high]), np.concatenate([low, np.zeros_like(low)])], 1)


def tiles(matrix):
    columns = -(-matrix.shape[-1] // 128) * 128
    padded = np.zeros((*matrix.shape[:-1], columns), matrix.dtype)
    padded[..., :matrix.shape[-1]] = matrix
    return np.moveaxis(padded.reshape(*matrix.shape[:-1], columns // 128, 128), -2, -3)


def whole(ref, *at, rows=slice(None), columns=None):
    count = ref.shape[len(at)]
    out = ref[(*at, 0, rows)] if count == 1 else jnp.concatenate([ref[(*at, i, rows)] for i in range(count)], 1)
    return out if columns is None else out[:, :columns]


def dot(a, b):
    return lax.dot_general(a, b, (((1,), (0,)), ((), ())), preferred_element_type=F32)


def split(v):
    high = v.astype(BF16)
    return high, (v - high.astype(F32)).astype(BF16)


def stacked(v):
    high, low = split(v)
    return jnp.concatenate([high, low, high], 0)


def wide_dot(v, ref, *at):
    v = dot(jnp.concatenate(split(v), 1), whole(ref, *at))
    return v[:, :128] + v[:, 128:]


def states(s):
    a = s(31) + LIFT_A * s(30)
    b = s(30) + LIFT_B * (s(29) + LIFT_A * (s(28) + s(30)))
    c = s(0)
    d = s(0) + LIFT_B * (s(1) + LIFT_A * (s(0) + s(2)))
    return a, b, c, d


def prepare(v_hbm, kx_hbm, fy_hbm, z1_hbm, zp_hbm, v_ref, vo_ref, kx_ref, fy_ref, z1_ref, zp_ref, xh, sems):
    loads = [pltpu.make_async_copy(v_hbm.at[:, pl.ds(8 * t, 8)], v_ref.at[:, pl.ds(8 * t, 8)], sems.at[t]) for t in range(4)]
    for i, (source, target) in enumerate(((kx_hbm, kx_ref), (zp_hbm, zp_ref), (fy_hbm, fy_ref), (z1_hbm, z1_ref))):
        loads.append(pltpu.make_async_copy(source, target, sems.at[4 + i]))
    for i in (4, 0, 1, 2, 3, 5, 6, 7):
        loads[i].start()
    loads[4].wait()
    parts = [[], []]
    for t in (0, 2):
        loads[t].wait()
        loads[t + 1].wait()
        high, low = split(jnp.concatenate([v_ref[:, 8 * u:8 * u + 8, :].reshape(256, 128) for u in (t, t + 1)], 1))
        x = dot(whole(kx_ref, 0), high) + dot(whole(kx_ref, 0), low) + dot(whole(kx_ref, 1), high)
        for u in (0, 1):
            for h in (0, 1):
                parts[h].append(x[160 * h:160 * h + 160, 128 * u:128 * u + 128])
    loads[5].wait()
    high, low = split(jnp.concatenate([jnp.concatenate(part, 0) for part in parts], 1))
    packed = dot(high, whole(zp_ref))
    packed = packed[:, :128] + packed[:, 128:] + dot(low, zp_ref[0])
    loads[6].wait()
    for i in range(0, len(PAIRS), 2):
        columns = [stacked(jnp.concatenate([packed[160 * t + 8 * j:160 * t + 8 * j + 8] for t in range(4)], 0)) for j in (i, i + 1)]
        rows = dot(whole(fy_ref, columns=96), jnp.concatenate(columns, 1))
        vo_ref[PAIRS[i]] = rows[:, :128]
        vo_ref[PAIRS[i + 1]] = rows[:, 128:]
    loads[7].wait()
    planes = [*states(lambda x: v_ref[x]), *states(lambda y: v_ref[:, y, :])]
    planes = wide_dot(jnp.concatenate(planes, 0), z1_ref)
    for q in range(4):
        plane, rows = planes[32 * q:32 * q + 32], planes[128 + 32 * q:160 + 32 * q]
        xh[q] = plane
        vo_ref[X_STATES[-1 if q < 2 else 1] + q % 2, 0:32, :] = plane
        at = Y_AT[-1 if q < 2 else 1]
        for t in range(4):
            vo_ref[Y_STATES + 4 * (q % 2) + t, at:at + 8, :] = rows[8 * t:8 * t + 8]
    for q in range(4):
        for p, row in enumerate(states(lambda y: xh[q, y:y + 1, :])):
            at = Y_AT[-1 if p < 2 else 1] + 2 * (q % 2) + p % 2
            vo_ref[X_STATES[-1 if q < 2 else 1], at:at + 1, :] = row
    for e in X_STATES.values():
        for dy in (-1, 1):
            vo_ref[e, Y_AT[dy] + 4:Y_AT[dy] + 8, :] = jnp.zeros((4, 128), F32)


def split_y(p, halo, first, last):
    a, b, c, d = halo
    p0, p1, p2, p3 = p

    def following(v, edge):
        return jnp.where(last, edge, pltpu.roll(v, 7, 0))

    def preceding(v, edge):
        return jnp.where(first, edge, pltpu.roll(v, 1, 0))

    o0 = p1 + LIFT_A * (p0 + p2)
    o1 = p3 + LIFT_A * (p2 + following(p0, c))
    before = a + LIFT_A * p0
    e0 = p0 + LIFT_B * (preceding(o1, before) + o0)
    e1 = p2 + LIFT_B * (o0 + o1)
    q0 = o0 + LIFT_C * (e0 + e1)
    q1 = o1 + LIFT_C * (e1 + following(e0, d + LIFT_B * o1))
    before = before + LIFT_C * (b + LIFT_B * before + e0)
    f0 = e0 + LIFT_D * (preceding(q1, before) + q0)
    f1 = e1 + LIFT_D * (q0 + q1)
    return f0 * (1 / LIFT_K), q0 * LIFT_K, f1 * (1 / LIFT_K), q1 * LIFT_K


def exchange(nx, ny, nz, v_ref, vo_ref, z1_hbm, ty_hbm, te_hbm, tl_hbm, zu_hbm, ys_ref, tl_out, e2_ref, e34_ref, tl_ref, zu_ref,
             vi_ref, z1_ref, ty_ref, te_ref, te_in, zt, send, recv, hello, sems):
    x, y = lax.axis_index("gx"), lax.axis_index("gy")
    z = lax.rem(x, nz)

    def device(dx, dy):
        return lax.rem(x + dx + nx, nx), lax.rem(y + dy + ny, ny)

    copies = {dx: [] for dx in OFFSETS}
    for i, ((dx, dy), ((e, ne), (r, nr))) in enumerate(MOVES):
        at = (pl.ds(e, ne), pl.ds(r, nr))
        copies[dx].append(pltpu.make_async_remote_copy(
            src_ref=vo_ref.at[at], dst_ref=vi_ref.at[at], send_sem=send.at[i], recv_sem=recv.at[i],
            device_id=device(-dx, -dy), device_id_type=MESH))

    def start(dx):
        for copy in copies[dx]:
            copy.start()

    def arrive(dx):
        for copy in copies[dx]:
            copy.wait_recv()

    barrier = pltpu.get_barrier_semaphore()

    def greet(dx):
        for o in GROUP[dx]:
            pl.semaphore_signal(barrier, inc=1, device_id=device(*o), device_id_type=MESH)

    greet(-2)
    pl.when(z != nz - 1)(lambda: greet(-1))
    pl.when(z < nz - 2)(lambda: greet(0))
    pl.when(z < nz - 3)(lambda: greet(1))
    pl.when(z < nz - 4)(lambda: greet(2))
    loads = [pltpu.make_async_copy(a, b, sems.at[i]) for i, (a, b) in enumerate(
        ((z1_hbm, z1_ref), (ty_hbm, ty_ref), (te_hbm, te_ref), (tl_hbm, tl_ref), (zu_hbm, zu_ref)))]
    for load in loads:
        load.start()
    for e in PAIRS:
        if e in (X_AT[2], X_AT[-2]):
            vi_ref[e, 8:24, :] = jnp.zeros((16, 128), F32)
        elif e not in (0, 1, X_AT[1], X_AT[1] + 1, X_AT[-1], X_AT[-1] + 1):
            vi_ref[e, 48:64, :] = jnp.zeros((16, 128), F32)
    greeted = jnp.where(z == 0, 14, jnp.where(z == 1, 19, jnp.where(z < nz - 2, 24, jnp.where(z == nz - 2, 5, 10))))
    pl.semaphore_wait(barrier, greeted)
    pl.when(z != nz - 2)(lambda: start(-1))
    start(-2)

    def say_hello(dx):
        for dy in range(-2, 3):
            pl.semaphore_signal(hello.at[dx - 1], inc=1, device_id=device(dx, dy), device_id_type=MESH)

    pl.when(z == nz - 1)(lambda: say_hello(1))
    pl.when(z >= nz - 2)(lambda: say_hello(2))

    @pl.when(z < nz - 2)
    def _():
        start(0)
        pl.when(z > 0)(lambda: start(1))
        pl.when(z > 1)(lambda: start(2))

    loads[0].wait()
    for t in range(4):
        zt[:, 8 * t:8 * t + 8, :] = wide_dot(v_ref[:, 8 * t:8 * t + 8, :].reshape(256, 128), z1_ref).reshape(32, 8, 128)

    @pl.when(z == nz - 2)
    def _():
        arrive(-1)
        start(-1)
        start(1)
        start(0)
        arrive(-2)
        start(2)

    @pl.when(z == nz - 1)
    def _():
        arrive(-2)
        start(0)
        start(2)
        arrive(-1)
        start(1)

    sub = lax.broadcasted_iota(jnp.int32, (8, 128), 0)
    first, last = sub == 0, sub == 7

    def plane(x):
        if 2 <= x < 34:
            x = x - 2
            p = [zt[x, pl.ds(r, 8, 4), :] for r in range(4)]
            at = [(Y_STATES + 4 * (k % 2) + x // 8, Y_AT[-1 if k < 2 else 1] + x % 8) for k in range(4)]
            x = x + 2
        else:
            dx, q = (-1, x) if x < 2 else (1, x - 34)
            p = [vi_ref[X_STATES[dx] + q, pl.ds(r, 8, 4), :] for r in range(4)]
            at = [(X_STATES[dx], Y_AT[-1 if k < 2 else 1] + 2 * q + k % 2) for k in range(4)]
        halo = [jnp.broadcast_to(vi_ref[e, pl.ds(r, 1), :], (8, 128)) for e, r in at]
        for r, v in enumerate(split_y(p, halo, first, last)):
            ys_ref[x, r] = v

    def upper(first_pair, count, out_ref):
        done = []
        for i in range(first_pair, first_pair + count):
            e = PAIRS[i]
            v = vi_ref[e]
            own = vo_ref[e, 0:32, :] if i < COUNT[0] // 2 else jnp.concatenate([v[0:24], jnp.zeros((8, 128), F32)], 0)
            done.append(stacked(jnp.concatenate([own, v[32:]], 0)))
        for i in range(0, count, 2):
            r = dot(whole(ty_ref, columns=192), jnp.concatenate(done[i:i + 2], 1))
            for j in range(min(2, count - i)):
                for t in range(4):
                    out_ref[t // 2, first_pair % EARLY + i + j, :, 128 * (t % 2):128 * (t % 2) + 128] = r[8 * t:8 * t + 8, 128 * j:128 * j + 128]

    loads[1].wait()
    arrive(0)
    for x in range(2, 34):
        plane(x)
    upper(0, 10, te_in)
    arrive(1)
    plane(34)
    plane(35)
    arrive(2)
    upper(10, 5, te_in)
    loads[2].wait()
    for u, (ref, at, rows) in enumerate(((e2_ref, 0, 128), (e34_ref, 128, 96))):
        high, low = split(te_in[u].reshape(8 * EARLY, 256))
        v = jnp.concatenate([high, low], 0)
        v = [dot(whole(te_ref, 0, h, rows=slice(at, at + rows), columns=240), v)
             + dot(whole(te_ref, 1, h, rows=slice(at, at + rows), columns=120), high) for h in (0, 1)]
        ref[...] = jnp.where(lax.broadcasted_iota(jnp.int32, (rows, 256), 1) % 128 < 64, v[0], v[1])

    @pl.when(z == 0)
    def _():
        pl.semaphore_wait(hello.at[0], 5)
        start(1)

    @pl.when(z < 2)
    def _():
        pl.semaphore_wait(hello.at[1], 5)
        start(2)

    @pl.when(z < nz - 2)
    def _():
        arrive(-1)
        arrive(-2)

    plane(0)
    plane(1)
    upper(15, 5, tl_out)
    loads[3].wait()
    loads[4].wait()
    for dx in OFFSETS:
        for copy in copies[dx]:
            copy.wait_send()


def finish(ys, tl, e2_ref, e34_ref, tl_ref, zu_ref, out_ref, up, done, sems):
    sub = lax.broadcasted_iota(jnp.int32, (8, 128), 0)
    lane = lax.broadcasted_iota(jnp.int32, (8, 128), 1)

    def upper(u, at, rows, early):
        v = stacked(tl[u].reshape(8 * (len(PAIRS) - EARLY), 256))
        v = [dot(whole(tl_ref, h, rows=slice(at, at + rows), columns=120), v) for h in (0, 1)]
        return early + jnp.where(lax.broadcasted_iota(jnp.int32, (rows, 256), 1) % 128 < 64, v[0], v[1])

    v = upper(0, 0, 128, e2_ref[...])
    l2 = wide_dot(jnp.concatenate([v[:, :128], v[:, 128:]], 0), zu_ref, 0).reshape(2, 16, 8, 128)
    v = upper(1, 128, 96, e34_ref[...])
    l3 = wide_dot(v[:64, :128], zu_ref, 1).reshape(8, 8, 128)
    l4 = wide_dot(v[64:, 128:], zu_ref, 2).reshape(4, 8, 128)
    for i in range(16):
        for t in (0, 1):
            v = l2[t][i]
            if i % 2 == 0 and t == 0:
                w = l3[i // 2]
                if i % 4 == 0:
                    w = jnp.where((lane % 8 == 0) & (sub % 2 == 0), l4[i // 4], w)
                v = jnp.where(lane % 4 == 0, w, v)
            up[i, t] = v

    odd_lane = lane % 2 == 1
    state = {}
    copies = []
    for r in range(4):
        before = ys[0, r] + LIFT_A * ys[2, r]
        state[r] = (before, ys[1, r] + LIFT_B * before, None)
    for i in range(17):
        for r in range(4):
            o, e, q = state[r]
            if i < 16:
                p = ys[2 + 2 * i, r]
                o_now = ys[3 + 2 * i, r] + LIFT_A * (p + ys[4 + 2 * i, r])
                e_now = p + LIFT_B * (o + o_now)
            else:
                o_now, e_now = None, ys[35, r] + LIFT_B * o
            q_now = o + LIFT_C * (e + e_now)
            if i > 0:
                low = (e + LIFT_D * (q + q_now)) * (1 / LIFT_K)
                if r % 2 == 0:
                    low = jnp.where(odd_lane, low, up[i - 1, r // 2])
                done[2 * i - 2, pl.ds(r, 8, 4), :] = low
                done[2 * i - 1, pl.ds(r, 8, 4), :] = q_now * LIFT_K
            state[r] = (o_now, e_now, q_now)
        if i in (4, 8, 12, 16):
            piece = pl.ds(2 * i - 8, 8)
            copy = pltpu.make_async_copy(done.at[piece], out_ref.at[piece], sems.at[i // 4 - 1])
            copy.start()
            copies.append(copy)
    for copy in copies:
        copy.wait()


def solution(mesh):
    nx, ny = mesh.shape["gx"], mesh.shape["gy"]
    kx, fy, z1, zp, ty, te, tl, zu = operators()
    vmem, hbm = pl.BlockSpec(memory_space=pltpu.VMEM), pl.BlockSpec(memory_space=pltpu.HBM)
    limit = 24 * 1024 * 1024
    block = (32, 32, 128)
    moves = pltpu.SemaphoreType.DMA((len(MOVES),))

    def kept(*ms):
        return [pltpu.with_memory_space_constraint(jnp.asarray(m), pltpu.HBM) for m in ms]

    def local(v):
        v, vo = pl.pallas_call(
            prepare,
            out_shape=[pltpu.VMEM(block, F32), pltpu.VMEM((ENTRIES, ROWS, 128), F32)],
            in_specs=[hbm] * 5, out_specs=[vmem] * 2,
            scratch_shapes=[*(pltpu.VMEM(m.shape, BF16) for m in (kx, fy, z1, zp)), pltpu.VMEM((4, 32, 128), F32), pltpu.SemaphoreType.DMA((8,))],
            compiler_params=pltpu.CompilerParams(vmem_limit_bytes=limit),
        )(*kept(v, kx, fy, z1, zp))
        parts = pl.pallas_call(
            functools.partial(exchange, nx, ny, 8),
            out_shape=[*(pltpu.VMEM(s, F32) for s in ((36, 4, 8, 128), (2, len(PAIRS) - EARLY, 8, 256), (128, 256), (96, 256))),
                       *(pltpu.VMEM(m.shape, BF16) for m in (tl, zu))],
            in_specs=[vmem] * 2 + [hbm] * 5, out_specs=[vmem] * 6,
            scratch_shapes=[pltpu.VMEM((ENTRIES, ROWS, 128), F32), *(pltpu.VMEM(m.shape, BF16) for m in (z1, ty, te)),
                            pltpu.VMEM((2, EARLY, 8, 256), F32), pltpu.VMEM(block, F32),
                            moves, moves, pltpu.SemaphoreType.REGULAR((2,)), pltpu.SemaphoreType.DMA((5,))],
            compiler_params=pltpu.CompilerParams(collective_id=0, has_side_effects=True, vmem_limit_bytes=limit),
        )(v, vo, *kept(z1, ty, te, tl, zu))
        return pl.pallas_call(
            finish,
            out_shape=jax.ShapeDtypeStruct(block, F32),
            in_specs=[vmem] * 6, out_specs=pl.BlockSpec(memory_space=pl.ANY),
            scratch_shapes=[pltpu.VMEM((16, 2, 8, 128), F32), pltpu.VMEM(block, F32), pltpu.SemaphoreType.DMA((4,))],
            compiler_params=pltpu.CompilerParams(vmem_limit_bytes=limit),
        )(*parts)

    spec = P("gx", "gy", None)
    return jax.shard_map(local, mesh=mesh, in_specs=(spec,), out_specs=spec, check_vma=False)
```

```python
import functools

import jax
import jax.numpy as jnp
import ml_dtypes
import numpy as np
from jax import lax
from jax.experimental import pallas as pl
from jax.experimental.pallas import tpu as pltpu
from jax.sharding import PartitionSpec as P

LIFT_A, LIFT_B, LIFT_C, LIFT_D = -1.586134342, -0.05298011854, 0.8829110762, 0.4435068522
LIFT_K = 1.149604398
MESH = pl.DeviceIdType.MESH
F32, BF16 = jnp.float32, jnp.bfloat16

COUNT = {0: 20, 1: 8, 2: 2, -1: 8, -2: 2}
X_AT = {0: 0, 1: 18, 2: 24, -1: 25, -2: 31}
Y_AT = {0: 0, -1: 32, 1: 40, -2: 48, 2: 56}
ENTRIES, ROWS = 32, 64
PAIRS = [X_AT[o] + p for o, c in COUNT.items() for p in range(c // 2)]
EARLY = 15
Y_STATES = 10
X_STATES = {1: 22, -1: 29}
OFFSETS = (0, -1, 1, -2, 2)
GROUP = {dx: [(dx, dy) for dy in OFFSETS if (dx, dy) != (0, 0)] for dx in OFFSETS}


def pieces(dx, dy):
    rows = (Y_AT[dy], 8)
    if dx == 0:
        return [((0, 18 if abs(dy) == 1 else 10), rows)]
    if abs(dx) == 2:
        return [((X_AT[dx], 1), rows)]
    if dy == 0:
        return [((X_STATES[dx], 2), (0, 32)), ((X_AT[dx], 4), (0, 24))]
    return [((X_AT[dx], 5 if abs(dy) == 1 else 2), rows)]


MOVES = [(o, piece) for dx in OFFSETS for o in GROUP[dx] for piece in pieces(*o)]


def lift_1d(v):
    even, odd = v[0::2], v[1::2]
    odd = odd + LIFT_A * (even + np.roll(even, -1, 0))
    even = even + LIFT_B * (np.roll(odd, 1, 0) + odd)
    odd = odd + LIFT_C * (even + np.roll(even, -1, 0))
    even = even + LIFT_D * (np.roll(odd, 1, 0) + odd)
    return even / LIFT_K, odd * LIFT_K


def interleave(low, high):
    out = np.empty((2 * low.shape[0], low.shape[1]))
    out[0::2], out[1::2] = low, high
    return out


def row_space(parts, count):
    basis = np.zeros((0, parts[0].shape[1]))
    for part in parts:
        rest = part - part @ basis.T @ basis
        size, rows = np.linalg.svd(rest)[1:]
        basis = np.concatenate([basis, rows[:int((size > 1e-9).sum())]])
    return np.concatenate([basis, np.zeros((count - len(basis), basis.shape[1]))])


def thirds(matrix):
    out, rest = [], np.asarray(matrix, np.float64)
    for _ in range(3):
        out.append(rest.astype(ml_dtypes.bfloat16))
        rest = rest - out[-1].astype(np.float64)
    return out


def operators():
    n, blocks, mid = 32, 16, 8
    low, levels = np.eye(n * blocks), {}
    for level in range(1, 5):
        low, high = lift_1d(low)
        m = n >> level
        levels[level] = interleave(low[mid * m:(mid + 1) * m], high[mid * m:(mid + 1) * m])
    functional, combine = {}, {}
    for offset, count in COUNT.items():
        parts = [levels[level][:, (mid + offset) * n:(mid + offset + 1) * n] for level in (4, 3, 2)]
        functional[offset] = row_space(parts, count)
        combine[offset] = np.concatenate(parts[::-1])
    basis = np.stack(own_basis(np.eye(n)))
    inverse = np.linalg.pinv(basis)
    weights = np.concatenate([functional[o] @ inverse for o in COUNT if o])
    cx = [np.concatenate([(combine[o] @ (functional[o].T if o else inverse))[:, h::2] for o in COUNT], 1) for h in (0, 1)]
    early, late = [np.stack([np.kron(c[:, part], np.eye(8)) for c in cx]) for part in (slice(0, EARLY), slice(EARLY, None))]
    high, mid_, low = thirds(early)
    early = np.stack([np.concatenate(m, 2) for m in ((high, high), (mid_, mid_), (low, high))])
    high, mid_, low = thirds(late)
    late = np.concatenate([high, high, high, mid_, mid_, low], 2)
    fy, cy = np.zeros((ROWS, 32)), np.zeros((28, ROWS))
    for offset, count in COUNT.items():
        at = Y_AT[offset]
        fy[at:at + count], cy[:, at:at + count] = functional[offset], combine[offset] @ functional[offset].T
    ty = np.zeros((32, ROWS))
    ty[0:8], ty[8:16], ty[16:24], ty[24:32:2] = cy[0:16:2], cy[1:16:2], cy[16:24], cy[24:28]
    high, mid_, low = thirds(fy)
    fy = np.concatenate([high, high, high, mid_, mid_, low], 1)
    high, mid_, low = thirds(ty)
    ty = np.stack([np.concatenate(m, 1) for m in ((high, high, high), (mid_, mid_, low))])
    low, high = lift_1d(np.eye(128))
    z1 = wide(np.concatenate([interleave(low, high).T, low.T, low.T], 1))
    low, zu = np.eye(64), np.zeros((3, 64, 128))
    for level in range(3):
        low, high = lift_1d(low)
        zu[level, :, ::2 << level] = interleave(low, high).T
    zu = np.stack([wide(np.concatenate([m, m])) for m in zu])
    return weights, [tiles(m) for m in (fy, z1, ty, early, late, zu)]


def wide(matrix):
    high, mid, low = thirds(matrix)
    return np.concatenate([np.concatenate(m) for m in ((high, high), (mid, mid), (low, high))], 1)


def tiles(matrix):
    columns = -(-matrix.shape[-1] // 128) * 128
    padded = np.zeros((*matrix.shape[:-1], columns), matrix.dtype)
    padded[..., :matrix.shape[-1]] = matrix
    return np.moveaxis(padded.reshape(*matrix.shape[:-1], columns // 128, 128), -2, -3)


def whole(ref, *at, rows=slice(None), columns=None):
    count = ref.shape[len(at)]
    out = ref[(*at, 0, rows)] if count == 1 else jnp.concatenate([ref[(*at, i, rows)] for i in range(count)], 1)
    return out if columns is None else out[:, :columns]


def dot(a, b):
    return lax.dot_general(a, b, (((1,), (0,)), ((), ())), preferred_element_type=F32)


def split(v):
    high = v.astype(BF16)
    rest = v - high.astype(F32)
    mid = rest.astype(BF16)
    return high, mid, (rest - mid.astype(F32)).astype(BF16)


def stacked(v):
    high, mid, low = split(v)
    return jnp.concatenate([high, mid, low, high, mid, high], 0)


def wide_dot(v, ref, *at):
    high, mid, low = split(v)
    m = whole(ref, *at)
    n = m.shape[1] // 3
    v = dot(jnp.concatenate([high, mid], 1), m[:, :2 * n])
    return dot(jnp.concatenate([high, low], 1), m[:, 2 * n:]) + v[:, n:] + v[:, :n]


def states(s):
    a = s(31) + LIFT_A * s(30)
    b = s(30) + LIFT_B * (s(29) + LIFT_A * (s(28) + s(30)))
    c = s(0)
    d = s(0) + LIFT_B * (s(1) + LIFT_A * (s(0) + s(2)))
    return a, b, c, d


def own_basis(v):
    out, odd, even, odd3 = [], 0.0, 0.0, 0.0
    for i in range(17):
        if i < 16:
            after = v[2 * i + 2] if i < 15 else 0.0
            odd_now = v[2 * i + 1] + LIFT_A * (v[2 * i] + after)
            even_now = v[2 * i] + LIFT_B * (odd + odd_now)
        else:
            odd_now, even_now = None, LIFT_B * odd
        if i > 0:
            odd3_now = odd + LIFT_C * (even + even_now)
            out.append(even + LIFT_D * (odd3 + odd3_now))
            odd3 = odd3_now
        odd, even = odd_now, even_now
    return [*out, *states(lambda i: v[i])]


def prepare(weights, z1_ref, fy_ref, v_ref, vo_ref, zt, xh, loads):
    half = lax.broadcasted_iota(jnp.int32, (8, 128), 1) < 64
    columns = [[] for _ in PAIRS]
    loads["z1"].wait()
    for t in range(4):
        loads[t].wait()
        v = wide_dot(v_ref[:, 8 * t:8 * t + 8, :].reshape(256, 128), z1_ref)
        zt[:, 8 * t:8 * t + 8, :] = v[:, :128].reshape(32, 8, 128)
        values = own_basis([v[8 * x:8 * x + 8, 128:] for x in range(32)])
        for row in weights:
            terms = [w * value for w, value in zip(row, values[:20]) if abs(w) > 1e-14]
            while len(terms) > 1:
                terms = [sum(terms[k:k + 2][1:], terms[k]) for k in range(0, len(terms), 2)]
            values.append(terms[0] if terms else jnp.zeros((8, 128), F32))
        for i, column in enumerate(columns):
            column.append(jnp.where(half, values[2 * i], values[2 * i + 1]))
    loads["fy"].wait()
    for i in range(0, len(PAIRS), 2):
        two = [stacked(jnp.concatenate(columns[j], 0)) for j in (i, i + 1)]
        rows = dot(whole(fy_ref, columns=192), jnp.concatenate(two, 1))
        vo_ref[PAIRS[i]] = rows[:, :128]
        vo_ref[PAIRS[i + 1]] = rows[:, 128:]
    for q, plane in enumerate(states(lambda x: zt[x])):
        xh[q] = plane
        vo_ref[X_STATES[-1 if q < 2 else 1] + q % 2, 0:32, :] = plane
    for q, rows in enumerate(states(lambda y: zt[:, y, :])):
        at = Y_AT[-1 if q < 2 else 1]
        for t in range(4):
            vo_ref[Y_STATES + 4 * (q % 2) + t, at:at + 8, :] = rows[8 * t:8 * t + 8]
    for q in range(4):
        for p, row in enumerate(states(lambda y: xh[q, y:y + 1, :])):
            at = Y_AT[-1 if p < 2 else 1] + 2 * (q % 2) + p % 2
            vo_ref[X_STATES[-1 if q < 2 else 1], at:at + 1, :] = row
    for e in X_STATES.values():
        for dy in (-1, 1):
            vo_ref[e, Y_AT[dy] + 4:Y_AT[dy] + 8, :] = jnp.zeros((4, 128), F32)


def split_y(p, halo, first, last):
    a, b, c, d = halo
    p0, p1, p2, p3 = p

    def following(v, edge):
        return jnp.where(last, edge, pltpu.roll(v, 7, 0))

    def preceding(v, edge):
        return jnp.where(first, edge, pltpu.roll(v, 1, 0))

    o0 = p1 + LIFT_A * (p0 + p2)
    o1 = p3 + LIFT_A * (p2 + following(p0, c))
    before = a + LIFT_A * p0
    e0 = p0 + LIFT_B * (preceding(o1, before) + o0)
    e1 = p2 + LIFT_B * (o0 + o1)
    q0 = o0 + LIFT_C * (e0 + e1)
    q1 = o1 + LIFT_C * (e1 + following(e0, d + LIFT_B * o1))
    before = before + LIFT_C * (b + LIFT_B * before + e0)
    f0 = e0 + LIFT_D * (preceding(q1, before) + q0)
    f1 = e1 + LIFT_D * (q0 + q1)
    return f0 * (1 / LIFT_K), q0 * LIFT_K, f1 * (1 / LIFT_K), q1 * LIFT_K


def exchange(nx, ny, nz, weights, v_hbm, fy_hbm, z1_hbm, ty_hbm, te_hbm, tl_hbm, zu_hbm, ys_ref, tl_out, e2_ref, e34_ref, tl_ref, zu_ref,
             v_ref, vo_ref, vi_ref, fy_ref, z1_ref, ty_ref, te_ref, te_in, zt, xh, send, recv, hello, sems):
    x, y = lax.axis_index("gx"), lax.axis_index("gy")
    z = lax.rem(x, nz)

    def device(dx, dy):
        return lax.rem(x + dx + nx, nx), lax.rem(y + dy + ny, ny)

    copies = {dx: [] for dx in OFFSETS}
    for i, ((dx, dy), ((e, ne), (r, nr))) in enumerate(MOVES):
        at = (pl.ds(e, ne), pl.ds(r, nr))
        copies[dx].append(pltpu.make_async_remote_copy(
            src_ref=vo_ref.at[at], dst_ref=vi_ref.at[at], send_sem=send.at[i], recv_sem=recv.at[i],
            device_id=device(-dx, -dy), device_id_type=MESH))

    def start(dx):
        for copy in copies[dx]:
            copy.start()

    def arrive(dx):
        for copy in copies[dx]:
            copy.wait_recv()

    barrier = pltpu.get_barrier_semaphore()

    def greet(dx):
        for o in GROUP[dx]:
            pl.semaphore_signal(barrier, inc=1, device_id=device(*o), device_id_type=MESH)

    greet(-2)
    pl.when(z != nz - 1)(lambda: greet(-1))
    loads = [pltpu.make_async_copy(v_hbm.at[:, pl.ds(8 * t, 8)], v_ref.at[:, pl.ds(8 * t, 8)], sems.at[t]) for t in range(4)]
    loads += [pltpu.make_async_copy(a, b, sems.at[4 + i]) for i, (a, b) in enumerate(
        ((z1_hbm, z1_ref), (fy_hbm, fy_ref), (ty_hbm, ty_ref), (te_hbm, te_ref), (tl_hbm, tl_ref), (zu_hbm, zu_ref)))]
    for i in (0, 4, 1, 2, 3, 5, 6, 7, 8, 9):
        loads[i].start()
    pl.when(z < nz - 2)(lambda: greet(0))
    pl.when(z < nz - 3)(lambda: greet(1))
    pl.when(z < nz - 4)(lambda: greet(2))
    for e in PAIRS:
        if e in (X_AT[2], X_AT[-2]):
            vi_ref[e, 8:24, :] = jnp.zeros((16, 128), F32)
        elif e >= X_AT[1] and e not in (X_AT[1], X_AT[1] + 1, X_AT[-1], X_AT[-1] + 1):
            vi_ref[e, 48:64, :] = jnp.zeros((16, 128), F32)
    prepare(weights, z1_ref, fy_ref, v_ref, vo_ref, zt, xh, {**dict(enumerate(loads[:4])), "z1": loads[4], "fy": loads[5]})
    greeted = jnp.where(z == 0, 14, jnp.where(z == 1, 19, jnp.where(z < nz - 2, 24, jnp.where(z == nz - 2, 5, 10))))
    pl.semaphore_wait(barrier, greeted)

    def say_hello(dx, dys):
        for dy in dys:
            pl.semaphore_signal(hello.at[dx - 1], inc=1, device_id=device(dx, dy), device_id_type=MESH)

    @pl.when(z == nz - 3)
    def _():
        say_hello(1, (0,))
        say_hello(2, (0,))

    pl.when(z != nz - 2)(lambda: start(-1))
    start(-2)
    pl.when(z == nz - 1)(lambda: say_hello(1, range(-2, 3)))
    pl.when(z >= nz - 2)(lambda: say_hello(2, range(-2, 3)))

    @pl.when(z < nz - 2)
    def _():
        start(0)
        pl.when(z > 0)(lambda: start(1))
        pl.when(z > 1)(lambda: start(2))

    @pl.when(z == nz - 2)
    def _():
        pl.semaphore_wait(hello.at[0], 1)
        start(-1)

    @pl.when(z == nz - 1)
    def _():
        pl.semaphore_wait(hello.at[1], 1)

    @pl.when(z >= nz - 2)
    def _():
        start(1)
        start(0)
        start(2)

    sub = lax.broadcasted_iota(jnp.int32, (8, 128), 0)
    first, last = sub == 0, sub == 7

    def plane(x):
        if 2 <= x < 34:
            x = x - 2
            p = [zt[x, pl.ds(r, 8, 4), :] for r in range(4)]
            at = [(Y_STATES + 4 * (k % 2) + x // 8, Y_AT[-1 if k < 2 else 1] + x % 8) for k in range(4)]
            x = x + 2
        else:
            dx, q = (-1, x) if x < 2 else (1, x - 34)
            p = [vi_ref[X_STATES[dx] + q, pl.ds(r, 8, 4), :] for r in range(4)]
            at = [(X_STATES[dx], Y_AT[-1 if k < 2 else 1] + 2 * q + k % 2) for k in range(4)]
        halo = [jnp.broadcast_to(vi_ref[e, pl.ds(r, 1), :], (8, 128)) for e, r in at]
        for r, v in enumerate(split_y(p, halo, first, last)):
            ys_ref[x, r] = v

    def upper(first_pair, count, out_ref):
        done = []
        for i in range(first_pair, first_pair + count):
            e = PAIRS[i]
            v = vi_ref[e]
            own = vo_ref[e, 0:32, :] if i < COUNT[0] // 2 else jnp.concatenate([v[0:24], jnp.zeros((8, 128), F32)], 0)
            done.append(jnp.concatenate([own, v[32:]], 0))
        for i in range(0, count, 2):
            high, mid, low = split(jnp.concatenate(done[i:i + 2], 1))
            r = (dot(whole(ty_ref, 1, columns=192), jnp.concatenate([high, mid, high], 0))
                 + dot(whole(ty_ref, 0, columns=192), jnp.concatenate([high, mid, low], 0)))
            for j in range(min(2, count - i)):
                for t in range(4):
                    out_ref[t // 2, first_pair % EARLY + i + j, :, 128 * (t % 2):128 * (t % 2) + 128] = r[8 * t:8 * t + 8, 128 * j:128 * j + 128]

    loads[6].wait()
    arrive(0)
    for x in range(2, 34):
        plane(x)
    upper(0, 10, te_in)
    arrive(1)
    plane(34)
    plane(35)
    arrive(2)
    upper(10, 5, te_in)
    loads[7].wait()
    for u, (ref, at, rows) in enumerate(((e2_ref, 0, 128), (e34_ref, 128, 96))):
        high, mid, low = split(te_in[u].reshape(8 * EARLY, 256))
        high_mid, high_low = [jnp.concatenate([high, w], 0) for w in (mid, low)]
        m = [[whole(te_ref, k, h, rows=slice(at, at + rows), columns=240) for k in range(3)] for h in (0, 1)]
        v = [dot(m[h][2], high_low) + dot(m[h][1], high_mid) + dot(m[h][0], high_mid) for h in (0, 1)]
        ref[...] = jnp.where(lax.broadcasted_iota(jnp.int32, (rows, 256), 1) % 128 < 64, v[0], v[1])

    @pl.when(z == 0)
    def _():
        pl.semaphore_wait(hello.at[0], 5)
        start(1)

    @pl.when(z < 2)
    def _():
        pl.semaphore_wait(hello.at[1], 5)
        start(2)

    arrive(-1)
    arrive(-2)
    plane(0)
    plane(1)
    upper(15, 5, tl_out)
    loads[8].wait()
    loads[9].wait()
    for dx in OFFSETS:
        for copy in copies[dx]:
            copy.wait_send()


def finish(ys, tl, e2_ref, e34_ref, tl_ref, zu_ref, out_ref, up, done, sems):
    sub = lax.broadcasted_iota(jnp.int32, (8, 128), 0)
    lane = lax.broadcasted_iota(jnp.int32, (8, 128), 1)

    def upper(u, at, rows, early):
        v = stacked(tl[u].reshape(8 * (len(PAIRS) - EARLY), 256))
        v = [dot(whole(tl_ref, h, rows=slice(at, at + rows), columns=240), v) for h in (0, 1)]
        return early + jnp.where(lax.broadcasted_iota(jnp.int32, (rows, 256), 1) % 128 < 64, v[0], v[1])

    v = upper(0, 0, 128, e2_ref[...])
    l2 = wide_dot(jnp.concatenate([v[:, :128], v[:, 128:]], 0), zu_ref, 0).reshape(2, 16, 8, 128)
    v = upper(1, 128, 96, e34_ref[...])
    l3 = wide_dot(v[:64, :128], zu_ref, 1).reshape(8, 8, 128)
    l4 = wide_dot(v[64:, 128:], zu_ref, 2).reshape(4, 8, 128)
    for i in range(16):
        for t in (0, 1):
            v = l2[t][i]
            if i % 2 == 0 and t == 0:
                w = l3[i // 2]
                if i % 4 == 0:
                    w = jnp.where((lane % 8 == 0) & (sub % 2 == 0), l4[i // 4], w)
                v = jnp.where(lane % 4 == 0, w, v)
            up[i, t] = v

    odd_lane = lane % 2 == 1
    state = {}
    copies = []
    for r in range(4):
        before = ys[0, r] + LIFT_A * ys[2, r]
        state[r] = (before, ys[1, r] + LIFT_B * before, None)
    for i in range(17):
        for r in range(4):
            o, e, q = state[r]
            if i < 16:
                p = ys[2 + 2 * i, r]
                o_now = ys[3 + 2 * i, r] + LIFT_A * (p + ys[4 + 2 * i, r])
                e_now = p + LIFT_B * (o + o_now)
            else:
                o_now, e_now = None, ys[35, r] + LIFT_B * o
            q_now = o + LIFT_C * (e + e_now)
            if i > 0:
                low = (e + LIFT_D * (q + q_now)) * (1 / LIFT_K)
                if r % 2 == 0:
                    low = jnp.where(odd_lane, low, up[i - 1, r // 2])
                done[2 * i - 2, pl.ds(r, 8, 4), :] = low
                done[2 * i - 1, pl.ds(r, 8, 4), :] = q_now * LIFT_K
            state[r] = (o_now, e_now, q_now)
        if i in (4, 8, 12, 16):
            piece = pl.ds(2 * i - 8, 8)
            copy = pltpu.make_async_copy(done.at[piece], out_ref.at[piece], sems.at[i // 4 - 1])
            copy.start()
            copies.append(copy)
    for copy in copies:
        copy.wait()


def solution(mesh):
    nx, ny = mesh.shape["gx"], mesh.shape["gy"]
    weights, (fy, z1, ty, te, tl, zu) = operators()
    vmem, hbm = pl.BlockSpec(memory_space=pltpu.VMEM), pl.BlockSpec(memory_space=pltpu.HBM)
    limit = 24 * 1024 * 1024
    block = (32, 32, 128)
    moves = pltpu.SemaphoreType.DMA((len(MOVES),))

    def kept(*ms):
        return [pltpu.with_memory_space_constraint(jnp.asarray(m), pltpu.HBM) for m in ms]

    def local(v):
        parts = pl.pallas_call(
            functools.partial(exchange, nx, ny, 8, weights.tolist()),
            out_shape=[*(pltpu.VMEM(s, F32) for s in ((36, 4, 8, 128), (2, len(PAIRS) - EARLY, 8, 256), (128, 256), (96, 256))),
                       *(pltpu.VMEM(m.shape, BF16) for m in (tl, zu))],
            in_specs=[hbm] * 7, out_specs=[vmem] * 6,
            scratch_shapes=[pltpu.VMEM(block, F32), *([pltpu.VMEM((ENTRIES, ROWS, 128), F32)] * 2), *(pltpu.VMEM(m.shape, BF16) for m in (fy, z1, ty, te)),
                            pltpu.VMEM((2, EARLY, 8, 256), F32), pltpu.VMEM(block, F32), pltpu.VMEM((4, 32, 128), F32),
                            moves, moves, pltpu.SemaphoreType.REGULAR((2,)), pltpu.SemaphoreType.DMA((10,))],
            compiler_params=pltpu.CompilerParams(collective_id=0, has_side_effects=True, vmem_limit_bytes=limit),
        )(*kept(v, fy, z1, ty, te, tl, zu))
        return pl.pallas_call(
            finish,
            out_shape=jax.ShapeDtypeStruct(block, F32),
            in_specs=[vmem] * 6, out_specs=pl.BlockSpec(memory_space=pl.ANY),
            scratch_shapes=[pltpu.VMEM((16, 2, 8, 128), F32), pltpu.VMEM(block, F32), pltpu.SemaphoreType.DMA((4,))],
            compiler_params=pltpu.CompilerParams(vmem_limit_bytes=limit),
        )(*parts)

    spec = P("gx", "gy", None)
    return jax.shard_map(local, mesh=mesh, in_specs=(spec,), out_specs=spec, check_vma=False)
```

```python
import functools

import jax
import jax.numpy as jnp
import ml_dtypes
import numpy as np
from jax import lax
from jax.experimental import pallas as pl
from jax.experimental.pallas import tpu as pltpu
from jax.sharding import PartitionSpec as P

LIFT_A, LIFT_B, LIFT_C, LIFT_D = -1.586134342, -0.05298011854, 0.8829110762, 0.4435068522
LIFT_K = 1.149604398
MESH = pl.DeviceIdType.MESH
F32, BF16 = jnp.float32, jnp.bfloat16

COUNT = {0: 20, 1: 8, 2: 2, -1: 8, -2: 2}
X_AT = {0: 0, 1: 18, 2: 24, -1: 25, -2: 31}
Y_AT = {0: 0, -1: 32, 1: 40, -2: 48, 2: 56}
ENTRIES, ROWS = 32, 64
PAIRS = [X_AT[o] + p for o, c in COUNT.items() for p in range(c // 2)]
EARLY = 15
Y_STATES = 10
X_STATES = {1: 22, -1: 29}
OFFSETS = (0, -1, 1, -2, 2)
GROUP = {dx: [(dx, dy) for dy in OFFSETS if (dx, dy) != (0, 0)] for dx in OFFSETS}


def pieces(dx, dy):
    rows = (Y_AT[dy], 8)
    if dx == 0:
        return [((0, 18 if abs(dy) == 1 else 10), rows)]
    if abs(dx) == 2:
        return [((X_AT[dx], 1), rows)]
    if dy == 0:
        return [((X_STATES[dx], 2), (0, 32)), ((X_AT[dx], 4), (0, 24))]
    return [((X_AT[dx], 5 if abs(dy) == 1 else 2), rows)]


MOVES = [(o, piece) for dx in OFFSETS for o in GROUP[dx] for piece in pieces(*o)]


def lift_1d(v):
    even, odd = v[0::2], v[1::2]
    odd = odd + LIFT_A * (even + np.roll(even, -1, 0))
    even = even + LIFT_B * (np.roll(odd, 1, 0) + odd)
    odd = odd + LIFT_C * (even + np.roll(even, -1, 0))
    even = even + LIFT_D * (np.roll(odd, 1, 0) + odd)
    return even / LIFT_K, odd * LIFT_K


def interleave(low, high):
    out = np.empty((2 * low.shape[0], low.shape[1]))
    out[0::2], out[1::2] = low, high
    return out


def row_space(parts, count):
    basis = np.zeros((0, parts[0].shape[1]))
    for part in parts:
        rest = part - part @ basis.T @ basis
        size, rows = np.linalg.svd(rest)[1:]
        basis = np.concatenate([basis, rows[:int((size > 1e-9).sum())]])
    return np.concatenate([basis, np.zeros((count - len(basis), basis.shape[1]))])


def thirds(matrix):
    out, rest = [], np.asarray(matrix, np.float64)
    for _ in range(3):
        out.append(rest.astype(ml_dtypes.bfloat16))
        rest = rest - out[-1].astype(np.float64)
    return out


def operators():
    n, blocks, mid = 32, 16, 8
    low, levels = np.eye(n * blocks), {}
    for level in range(1, 5):
        low, high = lift_1d(low)
        m = n >> level
        levels[level] = interleave(low[mid * m:(mid + 1) * m], high[mid * m:(mid + 1) * m])
    functional, combine = {}, {}
    for offset, count in COUNT.items():
        parts = [levels[level][:, (mid + offset) * n:(mid + offset + 1) * n] for level in (4, 3, 2)]
        functional[offset] = row_space(parts, count)
        combine[offset] = np.concatenate(parts[::-1])
    basis = np.stack(own_basis(np.eye(n)))
    inverse = np.linalg.pinv(basis)
    weights = np.concatenate([functional[o] @ inverse for o in COUNT if o])
    cx = [np.concatenate([(combine[o] @ (functional[o].T if o else inverse))[:, h::2] for o in COUNT], 1) for h in (0, 1)]
    early, late = [np.stack([np.kron(c[:, part], np.eye(8)) for c in cx]) for part in (slice(0, EARLY), slice(EARLY, None))]
    high, mid_, low = thirds(early)
    early = np.stack([np.concatenate(m, 2) for m in ((high, high), (mid_, mid_), (low, high))])
    high, mid_, low = thirds(late)
    late = np.concatenate([high, high, high, mid_, mid_, low], 2)
    fy, cy = np.zeros((ROWS, 32)), np.zeros((28, ROWS))
    for offset, count in COUNT.items():
        at = Y_AT[offset]
        fy[at:at + count], cy[:, at:at + count] = functional[offset], combine[offset] @ functional[offset].T
    ty = np.zeros((32, ROWS))
    ty[0:8], ty[8:16], ty[16:24], ty[24:32:2] = cy[0:16:2], cy[1:16:2], cy[16:24], cy[24:28]
    high, mid_, low = thirds(fy)
    fy = np.concatenate([high, high, high, mid_, mid_, low], 1)
    high, mid_, low = thirds(ty)
    ty = np.stack([np.concatenate(m, 1) for m in ((high, high, high), (mid_, mid_, low))])
    low, high = lift_1d(np.eye(128))
    z1 = wide(interleave(low, high).T)
    zp = np.concatenate(thirds(np.kron(np.eye(2), low.T)), 1)
    low, zu = np.eye(64), np.zeros((3, 64, 128))
    for level in range(3):
        low, high = lift_1d(low)
        zu[level, :, ::2 << level] = interleave(low, high).T
    zu = np.stack([wide(np.concatenate([m, m])) for m in zu])
    return weights, [tiles(m) for m in (zp, fy, z1, ty, early, late, zu)]


def wide(matrix):
    high, mid, low = thirds(matrix)
    return np.concatenate([np.concatenate(m) for m in ((high, high), (mid, mid), (low, high))], 1)


def tiles(matrix):
    columns = -(-matrix.shape[-1] // 128) * 128
    padded = np.zeros((*matrix.shape[:-1], columns), matrix.dtype)
    padded[..., :matrix.shape[-1]] = matrix
    return np.moveaxis(padded.reshape(*matrix.shape[:-1], columns // 128, 128), -2, -3)


def whole(ref, *at, rows=slice(None), columns=None):
    count = ref.shape[len(at)]
    out = ref[(*at, 0, rows)] if count == 1 else jnp.concatenate([ref[(*at, i, rows)] for i in range(count)], 1)
    return out if columns is None else out[:, :columns]


def dot(a, b):
    return lax.dot_general(a, b, (((1,), (0,)), ((), ())), preferred_element_type=F32)


def split(v):
    high = v.astype(BF16)
    rest = v - high.astype(F32)
    mid = rest.astype(BF16)
    return high, mid, (rest - mid.astype(F32)).astype(BF16)


def stacked(v):
    high, mid, low = split(v)
    return jnp.concatenate([high, mid, low, high, mid, high], 0)


def wide_dot(v, ref, *at):
    high, mid, low = split(v)
    m = whole(ref, *at)
    n = m.shape[1] // 3
    v = dot(jnp.concatenate([high, mid], 1), m[:, :2 * n])
    return dot(jnp.concatenate([high, low], 1), m[:, 2 * n:]) + v[:, n:] + v[:, :n]


def states(s):
    a = s(31) + LIFT_A * s(30)
    b = s(30) + LIFT_B * (s(29) + LIFT_A * (s(28) + s(30)))
    c = s(0)
    d = s(0) + LIFT_B * (s(1) + LIFT_A * (s(0) + s(2)))
    return a, b, c, d


def own_basis(v):
    out, odd, even, odd3 = [], 0.0, 0.0, 0.0
    for i in range(17):
        if i < 16:
            after = v[2 * i + 2] if i < 15 else 0.0
            odd_now = v[2 * i + 1] + LIFT_A * (v[2 * i] + after)
            even_now = v[2 * i] + LIFT_B * (odd + odd_now)
        else:
            odd_now, even_now = None, LIFT_B * odd
        if i > 0:
            odd3_now = odd + LIFT_C * (even + even_now)
            out.append(even + LIFT_D * (odd3 + odd3_now))
            odd3 = odd3_now
        odd, even = odd_now, even_now
    return [*out, *states(lambda i: v[i])]


def prepare_states(v_ref, vo_ref, xh):
    for q, plane in enumerate(states(lambda x: v_ref[x])):
        xh[q] = plane
        vo_ref[X_STATES[-1 if q < 2 else 1] + q % 2, 0:32, :] = plane
    for p, rows in enumerate(states(lambda y: xh[:, y, :])):
        at = Y_AT[-1 if p < 2 else 1] + 2 * (p % 2)
        vo_ref[X_STATES[-1], at:at + 2, :] = rows[0:2]
        vo_ref[X_STATES[1], at:at + 2, :] = rows[2:4]
    for e in X_STATES.values():
        for dy in (-1, 1):
            vo_ref[e, Y_AT[dy] + 4:Y_AT[dy] + 8, :] = jnp.zeros((4, 128), F32)


def prepare_pairs(first, count, weights, zp_ref, fy_ref, vo_ref, basis):
    sides = []
    for h in (0, 1):
        rows = []
        for i in range(first, first + count):
            f = 2 * i + h
            for t in range(4):
                if f < 20:
                    rows.append(basis[f, t])
                    continue
                terms = [w * basis[k, t] for k, w in enumerate(weights[f - 20]) if abs(w) > 1e-14]
                while len(terms) > 1:
                    terms = [sum(terms[k:k + 2][1:], terms[k]) for k in range(0, len(terms), 2)]
                rows.append(terms[0] if terms else jnp.zeros((8, 128), F32))
        sides.append(jnp.concatenate(rows, 0))
    high, mid, low = split(jnp.concatenate(sides, 1))
    m = whole(zp_ref)
    packed = dot(high, m[:, :256]) + dot(mid, m[:, :256])
    packed = dot(low, m[:, :128]) + dot(high, m[:, 256:]) + packed[:, 128:] + packed[:, :128]
    columns = [stacked(packed[32 * i:32 * i + 32]) for i in range(count)]
    for i in range(0, count, 2):
        rows = dot(whole(fy_ref, columns=192), jnp.concatenate(columns[i:i + 2], 1))
        for j in range(min(2, count - i)):
            vo_ref[PAIRS[first + i + j]] = rows[:, 128 * j:128 * j + 128]


def prepare_rows(vo_ref, zt):
    for q, rows in enumerate(states(lambda y: zt[:, y, :])):
        at = Y_AT[-1 if q < 2 else 1]
        for t in range(4):
            vo_ref[Y_STATES + 4 * (q % 2) + t, at:at + 8, :] = rows[8 * t:8 * t + 8]


def split_y(p, halo, first, last):
    a, b, c, d = halo
    p0, p1, p2, p3 = p

    def following(v, edge):
        return jnp.where(last, edge, pltpu.roll(v, 7, 0))

    def preceding(v, edge):
        return jnp.where(first, edge, pltpu.roll(v, 1, 0))

    o0 = p1 + LIFT_A * (p0 + p2)
    o1 = p3 + LIFT_A * (p2 + following(p0, c))
    before = a + LIFT_A * p0
    e0 = p0 + LIFT_B * (preceding(o1, before) + o0)
    e1 = p2 + LIFT_B * (o0 + o1)
    q0 = o0 + LIFT_C * (e0 + e1)
    q1 = o1 + LIFT_C * (e1 + following(e0, d + LIFT_B * o1))
    before = before + LIFT_C * (b + LIFT_B * before + e0)
    f0 = e0 + LIFT_D * (preceding(q1, before) + q0)
    f1 = e1 + LIFT_D * (q0 + q1)
    return f0 * (1 / LIFT_K), q0 * LIFT_K, f1 * (1 / LIFT_K), q1 * LIFT_K


def exchange(nx, ny, nz, weights, v_hbm, zp_hbm, fy_hbm, z1_hbm, ty_hbm, te_hbm, tl_hbm, zu_hbm,
             ys_ref, done, tl_out, e2_ref, e34_ref, tl_ref, zu_ref,
             v_ref, vo_ref, vi_ref, zp_ref, fy_ref, z1_ref, ty_ref, te_ref, te_in, zt, basis, xh, xz, send, recv, hello, sems):
    x, y = lax.axis_index("gx"), lax.axis_index("gy")
    z = lax.rem(x, nz)

    def device(dx, dy):
        return lax.rem(x + dx + nx, nx), lax.rem(y + dy + ny, ny)

    copies = {dx: [] for dx in OFFSETS}
    for i, ((dx, dy), ((e, ne), (r, nr))) in enumerate(MOVES):
        at = (pl.ds(e, ne), pl.ds(r, nr))
        copies[dx].append(pltpu.make_async_remote_copy(
            src_ref=vo_ref.at[at], dst_ref=vi_ref.at[at], send_sem=send.at[i], recv_sem=recv.at[i],
            device_id=device(-dx, -dy), device_id_type=MESH))

    def start(dx, part=slice(None)):
        for copy in copies[dx][part]:
            copy.start()

    def arrive(dx):
        for copy in copies[dx]:
            copy.wait_recv()

    barrier = pltpu.get_barrier_semaphore()

    def greet(dx):
        for o in GROUP[dx]:
            pl.semaphore_signal(barrier, inc=1, device_id=device(*o), device_id_type=MESH)

    def say_hello(dx, dys):
        for dy in dys:
            pl.semaphore_signal(hello.at[dx - 1], inc=1, device_id=device(dx, dy), device_id_type=MESH)

    greet(-2)
    pl.when(z != nz - 1)(lambda: greet(-1))
    loads = [pltpu.make_async_copy(v_hbm.at[pl.ds(8 * t, 8)], v_ref.at[pl.ds(8 * t, 8)], sems.at[t]) for t in range(4)]
    loads += [pltpu.make_async_copy(a, b, sems.at[4 + i]) for i, (a, b) in enumerate(
        ((zp_hbm, zp_ref), (fy_hbm, fy_ref), (z1_hbm, z1_ref), (ty_hbm, ty_ref), (te_hbm, te_ref), (tl_hbm, tl_ref), (zu_hbm, zu_ref)))]
    for i in (3, 0, 1, 2, 4, 5):
        loads[i].start()
    pl.when(z < nz - 2)(lambda: greet(0))
    pl.when(z < nz - 3)(lambda: greet(1))
    pl.when(z < nz - 4)(lambda: greet(2))
    for e in PAIRS:
        if e in (X_AT[2], X_AT[-2]):
            vi_ref[e, 8:24, :] = jnp.zeros((16, 128), F32)
        elif e >= X_AT[1] and e not in (X_AT[1], X_AT[1] + 1, X_AT[-1], X_AT[-1] + 1):
            vi_ref[e, 48:64, :] = jnp.zeros((16, 128), F32)

    @pl.when(z >= nz - 2)
    def _():
        pl.semaphore_wait(barrier, jnp.where(z == nz - 2, 5, 10))
        say_hello(2, range(-2, 3))
        pl.when(z == nz - 1)(lambda: say_hello(1, range(-2, 3)))

    for load in loads[:4]:
        load.wait()
    prepare_states(v_ref, vo_ref, xh)
    pl.when(z == nz - 1)(lambda: start(-1, slice(0, 1)))
    for t in range(4):
        for i, value in enumerate(own_basis([v_ref[x, 8 * t:8 * t + 8, :] for x in range(32)])):
            basis[i, t] = value
    loads[4].wait()
    loads[5].wait()
    prepare_pairs(EARLY, len(PAIRS) - EARLY, weights, zp_ref, fy_ref, vo_ref, basis)

    @pl.when(z >= nz - 2)
    def _():
        start(-2)
        pl.when(z == nz - 1)(lambda: start(-1, slice(1, None)))

    for load in loads[6:]:
        load.start()
    prepare_pairs(0, EARLY, weights, zp_ref, fy_ref, vo_ref, basis)
    loads[6].wait()
    for t in range(4):
        zt[:, 8 * t:8 * t + 8, :] = wide_dot(v_ref[:, 8 * t:8 * t + 8, :].reshape(256, 128), z1_ref).reshape(32, 8, 128)
    prepare_rows(vo_ref, zt)

    @pl.when(z < nz - 2)
    def _():
        pl.semaphore_wait(barrier, jnp.where(z == 0, 14, jnp.where(z == 1, 19, 24)))

        @pl.when(z == nz - 3)
        def _():
            say_hello(1, (0,))
            say_hello(2, (0,))

        start(-2)
        pl.when(z > 1)(lambda: start(2))
        start(-1)
        pl.when(z > 0)(lambda: start(1))
        start(0)

    @pl.when(z == nz - 2)
    def _():
        pl.semaphore_wait(hello.at[0], 1)
        start(-1)

    @pl.when(z == nz - 1)
    def _():
        pl.semaphore_wait(hello.at[1], 1)

    @pl.when(z >= nz - 2)
    def _():
        start(2)
        start(1)
        start(0)

    sub = lax.broadcasted_iota(jnp.int32, (8, 128), 0)
    first, last = sub == 0, sub == 7

    def row(ref, e, r):
        return jnp.broadcast_to(ref[e, pl.ds(r, 1), :], (8, 128))

    def plane(x):
        p = [zt[x, pl.ds(r, 8, 4), :] for r in range(4)]
        halo = [row(vi_ref, Y_STATES + 4 * (k % 2) + x // 8, Y_AT[-1 if k < 2 else 1] + x % 8) for k in range(4)]
        for r, v in enumerate(split_y(p, halo, first, last)):
            ys_ref[x + 2, r] = v

    def state_planes(dx):
        e, side = X_STATES[dx], (dx + 1) // 2
        xz[side] = wide_dot(jnp.concatenate([vi_ref[e, 0:32, :], vi_ref[e + 1, 0:32, :], vi_ref[e, 32:48, :]], 0), z1_ref)
        for q in (0, 1):
            p = [xz[side, pl.ds(32 * q + r, 8, 4), :] for r in range(4)]
            halo = [row(xz, side, 64 + 8 * (k // 2) + 2 * (k % 2) + q) for k in range(4)]
            for r, v in enumerate(split_y(p, halo, first, last)):
                ys_ref[34 * side + q, r] = v

    def upper(first_pair, count, out_ref):
        done = []
        for i in range(first_pair, first_pair + count):
            e = PAIRS[i]
            v = vi_ref[e]
            own = vo_ref[e, 0:32, :] if i < COUNT[0] // 2 else jnp.concatenate([v[0:24], jnp.zeros((8, 128), F32)], 0)
            done.append(jnp.concatenate([own, v[32:]], 0))
        for i in range(0, count, 2):
            high, mid, low = split(jnp.concatenate(done[i:i + 2], 1))
            r = (dot(whole(ty_ref, 1, columns=192), jnp.concatenate([high, mid, high], 0))
                 + dot(whole(ty_ref, 0, columns=192), jnp.concatenate([high, mid, low], 0)))
            for j in range(min(2, count - i)):
                for t in range(4):
                    out_ref[t // 2, first_pair % EARLY + i + j, :, 128 * (t % 2):128 * (t % 2) + 128] = r[8 * t:8 * t + 8, 128 * j:128 * j + 128]

    loads[7].wait()
    arrive(0)
    for x in range(32):
        plane(x)
    upper(0, 10, te_in)

    @pl.when(z < 2)
    def _():
        pl.semaphore_wait(hello.at[1], 5)
        start(2)

    @pl.when(z == 0)
    def _():
        pl.semaphore_wait(hello.at[0], 5)
        start(1)

    arrive(1)
    state_planes(1)
    arrive(2)
    upper(10, 5, te_in)
    loads[8].wait()
    for u, (ref, at, rows) in enumerate(((e2_ref, 0, 128), (e34_ref, 128, 96))):
        high, mid, low = split(te_in[u].reshape(8 * EARLY, 256))
        high_mid, high_low = [jnp.concatenate([high, w], 0) for w in (mid, low)]
        m = [[whole(te_ref, k, h, rows=slice(at, at + rows), columns=240) for k in range(3)] for h in (0, 1)]
        v = [dot(m[h][2], high_low) + dot(m[h][1], high_mid) + dot(m[h][0], high_mid) for h in (0, 1)]
        ref[...] = jnp.where(lax.broadcasted_iota(jnp.int32, (rows, 256), 1) % 128 < 64, v[0], v[1])

    lift_x(ys_ref, done)
    loads[9].wait()
    loads[10].wait()
    arrive(-1)
    arrive(-2)
    state_planes(-1)
    upper(15, 5, tl_out)
    for dx in OFFSETS:
        for copy in copies[dx]:
            copy.wait_send()


def lift_x(ys, done):
    state = {}
    for r in range(4):
        state[r] = (ys[3, r] + LIFT_A * (ys[2, r] + ys[4, r]), None, None)
    for i in range(1, 17):
        for r in range(4):
            o, e, q = state[r]
            if i < 16:
                p = ys[2 + 2 * i, r]
                o_now = ys[3 + 2 * i, r] + LIFT_A * (p + ys[4 + 2 * i, r])
                e_now = p + LIFT_B * (o + o_now)
            else:
                o_now, e_now = None, ys[35, r] + LIFT_B * o
            q_now = None
            if i > 1:
                q_now = o + LIFT_C * (e + e_now)
                done[i - 1, 1, pl.ds(r, 8, 4), :] = q_now * LIFT_K
            if i > 2:
                done[i - 1, 0, pl.ds(r, 8, 4), :] = (e + LIFT_D * (q + q_now)) * (1 / LIFT_K)
            state[r] = (o_now, e_now, q_now)


def first_x(ys, r):
    o = [ys[0, r] + LIFT_A * ys[2, r], *(ys[3 + 2 * i, r] + LIFT_A * (ys[2 + 2 * i, r] + ys[4 + 2 * i, r]) for i in range(3))]
    e = [ys[1, r] + LIFT_B * o[0], *(ys[2 + 2 * i, r] + LIFT_B * (o[i] + o[i + 1]) for i in range(3))]
    q = [o[i] + LIFT_C * (e[i] + e[i + 1]) for i in range(3)]
    low = [(e[i + 1] + LIFT_D * (q[i] + q[i + 1])) * (1 / LIFT_K) for i in range(2)]
    return low[0], q[1] * LIFT_K, low[1]


def finish(ys, done, tl, e2_ref, e34_ref, tl_ref, zu_ref, out_ref, even, odd, sems):
    sub = lax.broadcasted_iota(jnp.int32, (8, 128), 0)
    lane = lax.broadcasted_iota(jnp.int32, (8, 128), 1)
    copies = [pltpu.make_async_copy(done.at[pl.ds(1, 15), 1], out_ref.at[pl.ds(1, 15), 1], sems.at[0])]
    copies[0].start()

    def upper(u, at, rows, early):
        v = stacked(tl[u].reshape(8 * (len(PAIRS) - EARLY), 256))
        v = [dot(whole(tl_ref, h, rows=slice(at, at + rows), columns=240), v) for h in (0, 1)]
        return early + jnp.where(lax.broadcasted_iota(jnp.int32, (rows, 256), 1) % 128 < 64, v[0], v[1])

    v = upper(0, 0, 128, e2_ref[...])
    l2 = wide_dot(jnp.concatenate([v[:, :128], v[:, 128:]], 0), zu_ref, 0).reshape(2, 16, 8, 128)
    v = upper(1, 128, 96, e34_ref[...])
    l3 = wide_dot(v[:64, :128], zu_ref, 1).reshape(8, 8, 128)
    l4 = wide_dot(v[64:, 128:], zu_ref, 2).reshape(4, 8, 128)
    low = {}
    for r in range(4):
        low[0, r], v, low[1, r] = first_x(ys, r)
        odd[pl.ds(r, 8, 4), :] = v
    copies.append(pltpu.make_async_copy(odd, out_ref.at[0, 1], sems.at[1]))
    copies[-1].start()
    odd_lane = lane % 2 == 1
    for i in range(16):
        for r in range(4):
            v = low[i, r] if i < 2 else done[i, 0, pl.ds(r, 8, 4), :]
            if r % 2 == 0:
                w = l2[r // 2, i]
                if i % 2 == 0 and r == 0:
                    u = l3[i // 2]
                    if i % 4 == 0:
                        u = jnp.where((lane % 8 == 0) & (sub % 2 == 0), l4[i // 4], u)
                    w = jnp.where(lane % 4 == 0, u, w)
                v = jnp.where(odd_lane, v, w)
            even[i, pl.ds(r, 8, 4), :] = v
        if i % 4 == 3:
            piece = pl.ds(i - 3, 4)
            copies.append(pltpu.make_async_copy(even.at[piece], out_ref.at[piece, 0], sems.at[2 + i // 4]))
            copies[-1].start()
    for copy in copies:
        copy.wait()


def solution(mesh):
    nx, ny = mesh.shape["gx"], mesh.shape["gy"]
    weights, (zp, fy, z1, ty, te, tl, zu) = operators()
    vmem, hbm = pl.BlockSpec(memory_space=pltpu.VMEM), pl.BlockSpec(memory_space=pltpu.HBM)
    limit = 24 * 1024 * 1024
    block, pairs = (32, 32, 128), (16, 2, 32, 128)
    moves = pltpu.SemaphoreType.DMA((len(MOVES),))

    def kept(*ms):
        return [pltpu.with_memory_space_constraint(jnp.asarray(m), pltpu.HBM) for m in ms]

    def local(v):
        parts = pl.pallas_call(
            functools.partial(exchange, nx, ny, 8, weights.tolist()),
            out_shape=[*(pltpu.VMEM(s, F32) for s in ((36, 4, 8, 128), pairs, (2, len(PAIRS) - EARLY, 8, 256), (128, 256), (96, 256))),
                       *(pltpu.VMEM(m.shape, BF16) for m in (tl, zu))],
            in_specs=[hbm] * 8, out_specs=[vmem] * 7,
            scratch_shapes=[pltpu.VMEM(block, F32), *([pltpu.VMEM((ENTRIES, ROWS, 128), F32)] * 2), *(pltpu.VMEM(m.shape, BF16) for m in (zp, fy, z1, ty, te)),
                            pltpu.VMEM((2, EARLY, 8, 256), F32), pltpu.VMEM(block, F32), pltpu.VMEM((20, 4, 8, 128), F32), pltpu.VMEM((4, 32, 128), F32),
                            pltpu.VMEM((2, 80, 128), F32), moves, moves, pltpu.SemaphoreType.REGULAR((2,)), pltpu.SemaphoreType.DMA((11,))],
            compiler_params=pltpu.CompilerParams(collective_id=0, has_side_effects=True, vmem_limit_bytes=limit),
        )(*kept(v, zp, fy, z1, ty, te, tl, zu))
        return pl.pallas_call(
            finish,
            out_shape=jax.ShapeDtypeStruct(pairs, F32),
            in_specs=[vmem] * 7, out_specs=pl.BlockSpec(memory_space=pl.ANY),
            scratch_shapes=[pltpu.VMEM((16, 32, 128), F32), pltpu.VMEM((32, 128), F32), pltpu.SemaphoreType.DMA((6,))],
            compiler_params=pltpu.CompilerParams(vmem_limit_bytes=limit),
        )(*parts).reshape(block)

    spec = P("gx", "gy", None)
    return jax.shard_map(local, mesh=mesh, in_specs=(spec,), out_specs=spec, check_vma=False)
```

```python
import functools

import jax
import jax.numpy as jnp
import ml_dtypes
import numpy as np
from jax import lax
from jax.experimental import pallas as pl
from jax.experimental.pallas import tpu as pltpu
from jax.sharding import PartitionSpec as P

LIFT_A, LIFT_B, LIFT_C, LIFT_D = -1.586134342, -0.05298011854, 0.8829110762, 0.4435068522
LIFT_K = 1.149604398
MESH = pl.DeviceIdType.MESH
F32, BF16 = jnp.float32, jnp.bfloat16

COUNT = {0: 20, 1: 8, 2: 2, -1: 8, -2: 2}
X_AT = {0: 0, 1: 18, 2: 24, -1: 25, -2: 31}
Y_AT = {0: 0, -1: 32, 1: 40, -2: 48, 2: 56}
ENTRIES, ROWS = 32, 64
PAIRS = [X_AT[o] + p for o, c in COUNT.items() for p in range(c // 2)]
LATE = (6, 8, 4)
EARLY = 15
Y_STATES = 10
X_STATES = {1: 22, -1: 29}
OFFSETS = (0, -1, 1, -2, 2)
GROUP = {dx: [(dx, dy) for dy in (-2, 2, -1, 1, 0) if (dx, dy) != (0, 0)] for dx in OFFSETS}


def pieces(dx, dy):
    if dx == 0:
        return [(False, (0, 18), (Y_AT[dy], 8))] if abs(dy) == 1 else [(False, (0, 10), (Y_AT[dy], 2))]
    if abs(dx) == 2:
        return [(False, (X_AT[dx], 1), (Y_AT[dy], 2 if abs(dy) == 2 else 4))]
    if dy == 0:
        return [(True, (X_STATES[dx], 2), (0, 32)), (False, (X_AT[dx], 4), (0, 20))]
    if abs(dy) == 1:
        return [(True, (X_STATES[dx], 1), (Y_AT[dy], 4)), (False, (X_AT[dx], 4), (Y_AT[dy], 8))]
    return [(False, (X_AT[dx], 2), (Y_AT[dy], 2))]


MOVES = [(dx, dy, *piece) for dx in OFFSETS for dx, dy in GROUP[dx] for piece in pieces(dx, dy)]


def unsent():
    sent = {(e, r) for _, _, _, (e0, ne), (r0, nr) in MOVES for e in range(e0, e0 + ne) for r in range(r0, r0 + nr)}
    out = [(e, Y_AT[dy] + 4, 4) for e in X_STATES.values() for dy in (-1, 1)]
    for e in PAIRS:
        for tile in range(32 if e < X_AT[1] else 0, ROWS, 8):
            count = sum((e, r) in sent for r in range(tile, tile + 8))
            if count < 8 and tile != 24:
                out.append((e, tile + count, 8 - count))
    return out


def lift_1d(v):
    even, odd = v[0::2], v[1::2]
    odd = odd + LIFT_A * (even + np.roll(even, -1, 0))
    even = even + LIFT_B * (np.roll(odd, 1, 0) + odd)
    odd = odd + LIFT_C * (even + np.roll(even, -1, 0))
    even = even + LIFT_D * (np.roll(odd, 1, 0) + odd)
    return even / LIFT_K, odd * LIFT_K


def interleave(low, high):
    out = np.empty((2 * low.shape[0], low.shape[1]))
    out[0::2], out[1::2] = low, high
    return out


def row_space(parts, count):
    basis = np.zeros((0, parts[0].shape[1]))
    for part in parts:
        rest = part - part @ basis.T @ basis
        size, rows = np.linalg.svd(rest)[1:]
        basis = np.concatenate([basis, rows[:int((size > 1e-9).sum())]])
    return np.concatenate([basis, np.zeros((count - len(basis), basis.shape[1]))])


def thirds(matrix):
    out, rest = [], np.asarray(matrix, np.float64)
    for _ in range(3):
        out.append(rest.astype(ml_dtypes.bfloat16))
        rest = rest - out[-1].astype(np.float64)
    return out


def operators():
    n, blocks, mid = 32, 16, 8
    low, levels = np.eye(n * blocks), {}
    for level in range(1, 5):
        low, high = lift_1d(low)
        m = n >> level
        levels[level] = interleave(low[mid * m:(mid + 1) * m], high[mid * m:(mid + 1) * m])
    functional, combine = {}, {}
    for offset, count in COUNT.items():
        parts = [levels[level][:, (mid + offset) * n:(mid + offset + 1) * n] for level in (4, 3, 2)]
        functional[offset] = row_space(parts, count)
        combine[offset] = np.concatenate(parts[::-1])
    basis = np.stack(own_basis(np.eye(n)))
    inverse = np.linalg.pinv(basis)
    weights = np.concatenate([functional[o] @ inverse for o in COUNT if o])
    cx = [np.concatenate([(combine[o] @ (functional[o].T if o else inverse))[:, h::2] for o in COUNT], 1) for h in (0, 1)]
    first = [at + i for at, count in zip((0, 16, 24), LATE) for i in range(count)]
    assert all(np.abs(np.delete(c[:, EARLY:], first, 0)).max() < 1e-12 for c in cx)
    early = np.stack([np.kron(c[:, :EARLY], np.eye(8)) for c in cx])
    late = np.stack([np.kron(c[first, EARLY:], np.eye(8)) for c in cx])
    high, mid_, low = thirds(early)
    early = np.stack([np.concatenate(m, 2) for m in ((high, high), (mid_, mid_), (low, high))])
    high, mid_, low = thirds(late)
    late = np.concatenate([high, high, high, mid_, mid_, low], 2)
    fy, cy = np.zeros((ROWS, 32)), np.zeros((28, ROWS))
    for offset, count in COUNT.items():
        at = Y_AT[offset]
        fy[at:at + count], cy[:, at:at + count] = functional[offset], combine[offset] @ functional[offset].T
    ty = np.zeros((32, ROWS))
    ty[0:8], ty[8:16], ty[16:24], ty[24:32:2] = cy[0:16:2], cy[1:16:2], cy[16:24], cy[24:28]
    high, mid_, low = thirds(fy)
    fy = np.concatenate([high, high, high, mid_, mid_, low], 1)
    high, mid_, low = thirds(ty)
    ty = np.stack([np.concatenate(m, 1) for m in ((high, high, high), (mid_, mid_, low))])
    low, high = lift_1d(np.eye(128))
    z1 = wide(interleave(low, high).T)
    zp = np.concatenate(thirds(np.kron(np.eye(2), low.T)), 1)
    low, zu = np.eye(64), np.zeros((3, 64, 128))
    for level in range(3):
        low, high = lift_1d(low)
        zu[level, :, ::2 << level] = interleave(low, high).T
    zu = np.stack([wide(np.concatenate([m, m])) for m in zu])
    return weights, [tiles(m) for m in (zp, fy, z1, ty, early, late, zu)]


def wide(matrix):
    high, mid, low = thirds(matrix)
    return np.concatenate([np.concatenate(m) for m in ((high, high), (mid, mid), (low, high))], 1)


def tiles(matrix):
    columns = -(-matrix.shape[-1] // 128) * 128
    padded = np.zeros((*matrix.shape[:-1], columns), matrix.dtype)
    padded[..., :matrix.shape[-1]] = matrix
    return np.moveaxis(padded.reshape(*matrix.shape[:-1], columns // 128, 128), -2, -3)


def whole(ref, *at, rows=slice(None), columns=None):
    count = ref.shape[len(at)]
    out = ref[(*at, 0, rows)] if count == 1 else jnp.concatenate([ref[(*at, i, rows)] for i in range(count)], 1)
    return out if columns is None else out[:, :columns]


def dot(a, b):
    return lax.dot_general(a, b, (((1,), (0,)), ((), ())), preferred_element_type=F32)


def split(v):
    high = v.astype(BF16)
    rest = v - high.astype(F32)
    mid = rest.astype(BF16)
    return high, mid, (rest - mid.astype(F32)).astype(BF16)


def stacked(v):
    high, mid, low = split(v)
    return jnp.concatenate([high, mid, low, high, mid, high], 0)


def wide_dot(v, ref, *at):
    high, mid, low = split(v)
    m = whole(ref, *at)
    n = m.shape[1] // 3
    v = dot(jnp.concatenate([high, mid], 1), m[:, :2 * n])
    return dot(jnp.concatenate([high, low], 1), m[:, 2 * n:]) + v[:, n:] + v[:, :n]


def states(s, side):
    if side < 0:
        return s(31) + LIFT_A * s(30), s(30) + LIFT_B * (s(29) + LIFT_A * (s(28) + s(30)))
    return s(0), s(0) + LIFT_B * (s(1) + LIFT_A * (s(0) + s(2)))


def own_basis(v):
    out, odd, even, odd3 = [], 0.0, 0.0, 0.0
    for i in range(17):
        if i < 16:
            after = v[2 * i + 2] if i < 15 else 0.0
            odd_now = v[2 * i + 1] + LIFT_A * (v[2 * i] + after)
            even_now = v[2 * i] + LIFT_B * (odd + odd_now)
        else:
            odd_now, even_now = None, LIFT_B * odd
        if i > 0:
            odd3_now = odd + LIFT_C * (even + even_now)
            out.append(even + LIFT_D * (odd3 + odd3_now))
            odd3 = odd3_now
        odd, even = odd_now, even_now
    return [*out, *states(lambda i: v[i], -1), *states(lambda i: v[i], 1)]


def prepare_states(dx, v_ref, vo_ref, xh):
    e = X_STATES[dx]
    for q, plane in enumerate(states(lambda x: v_ref[x], dx)):
        xh[q] = plane
        vo_ref[e + q, 0:32, :] = plane
    for dy in (-1, 1):
        at = Y_AT[dy]
        for p, rows in enumerate(states(lambda y: xh[:, y, :], dy)):
            vo_ref[e, at + 2 * p:at + 2 * p + 2, :] = rows
        vo_ref[e, at + 4:at + 8, :] = jnp.zeros((4, 128), F32)


def prepare_pairs(first, count, weights, zp_ref, fy_ref, vo_ref, basis):
    sides = []
    for h in (0, 1):
        rows = []
        for i in range(first, first + count):
            f = 2 * i + h
            for t in range(4):
                if f < 20:
                    rows.append(basis[f, t])
                    continue
                terms = [w * basis[k, t] for k, w in enumerate(weights[f - 20]) if abs(w) > 1e-14]
                while len(terms) > 1:
                    terms = [sum(terms[k:k + 2][1:], terms[k]) for k in range(0, len(terms), 2)]
                rows.append(terms[0] if terms else jnp.zeros((8, 128), F32))
        sides.append(jnp.concatenate(rows, 0))
    high, mid, low = split(jnp.concatenate(sides, 1))
    m = whole(zp_ref)
    packed = dot(high, m[:, :256]) + dot(mid, m[:, :256])
    packed = dot(low, m[:, :128]) + dot(high, m[:, 256:]) + packed[:, 128:] + packed[:, :128]
    columns = [stacked(packed[32 * i:32 * i + 32]) for i in range(count)]
    for i in range(0, count, 2):
        rows = dot(whole(fy_ref, columns=192), jnp.concatenate(columns[i:i + 2], 1))
        for j in range(min(2, count - i)):
            vo_ref[PAIRS[first + i + j]] = rows[:, 128 * j:128 * j + 128]


def prepare_rows(vo_ref, zt):
    for dy in (-1, 1):
        for q, rows in enumerate(states(lambda y: zt[:, y, :], dy)):
            for t in range(4):
                vo_ref[Y_STATES + 4 * q + t, Y_AT[dy]:Y_AT[dy] + 8, :] = rows[8 * t:8 * t + 8]


def split_y(p, halo, first, last):
    a, b, c, d = halo
    p0, p1, p2, p3 = p

    def following(v, edge):
        return jnp.where(last, edge, pltpu.roll(v, 7, 0))

    def preceding(v, edge):
        return jnp.where(first, edge, pltpu.roll(v, 1, 0))

    o0 = p1 + LIFT_A * (p0 + p2)
    o1 = p3 + LIFT_A * (p2 + following(p0, c))
    before = a + LIFT_A * p0
    e0 = p0 + LIFT_B * (preceding(o1, before) + o0)
    e1 = p2 + LIFT_B * (o0 + o1)
    q0 = o0 + LIFT_C * (e0 + e1)
    q1 = o1 + LIFT_C * (e1 + following(e0, d + LIFT_B * o1))
    before = before + LIFT_C * (b + LIFT_B * before + e0)
    f0 = e0 + LIFT_D * (preceding(q1, before) + q0)
    f1 = e1 + LIFT_D * (q0 + q1)
    return f0 * (1 / LIFT_K), q0 * LIFT_K, f1 * (1 / LIFT_K), q1 * LIFT_K


def exchange(nx, ny, nz, weights, v_hbm, zp_hbm, fy_hbm, z1_hbm, ty_hbm, te_hbm, tl_hbm, zu_hbm,
             done, tl_out, e2_ref, e34_ref, tl_ref, zu_ref,
             v_ref, vo_ref, vi_ref, ys_ref, zp_ref, fy_ref, z1_ref, ty_ref, te_ref, te_in, zt, basis, xh, up, xz, send, recv, hello, sems):
    x, y = lax.axis_index("gx"), lax.axis_index("gy")
    z = lax.rem(x, nz)

    def device(dx, dy):
        return lax.rem(x + dx + nx, nx), lax.rem(y + dy + ny, ny)

    copies = []
    for i, (dx, dy, is_states, (e, ne), (r, nr)) in enumerate(MOVES):
        at = (pl.ds(e, ne), pl.ds(r, nr))
        copies.append((dx, dy, is_states, pltpu.make_async_remote_copy(
            src_ref=vo_ref.at[at], dst_ref=vi_ref.at[at], send_sem=send.at[i], recv_sem=recv.at[i],
            device_id=device(-dx, -dy), device_id_type=MESH)))

    def start(which, kinds=(True, False)):
        for dx, _, is_states, copy in copies:
            if dx == which and is_states in kinds:
                copy.start()

    def start_ahead(kinds, waits):
        for dx, dy, is_states, copy in copies:
            if dx == -1 and is_states in kinds:
                if dy in (0, 1):
                    pl.when(((x == nx - 1) & (y == dy)) == waits)(copy.start)
                elif not waits:
                    copy.start()

    def arrive(which, kinds=(True, False)):
        for dx, _, is_states, copy in copies:
            if dx == which and is_states in kinds:
                copy.wait_recv()

    barrier = pltpu.get_barrier_semaphore()

    def greet(dx):
        for o in GROUP[dx]:
            pl.semaphore_signal(barrier, inc=1, device_id=device(*o), device_id_type=MESH)

    def say_hello(dx, dys):
        for dy in dys:
            pl.semaphore_signal(hello.at[dx - 1], inc=1, device_id=device(dx, dy), device_id_type=MESH)

    greet(-2)
    pl.when(z != nz - 1)(lambda: greet(-1))
    loads = [pltpu.make_async_copy(v_hbm.at[pl.ds(8 * t, 8)], v_ref.at[pl.ds(8 * t, 8)], sems.at[t]) for t in range(4)]
    loads += [pltpu.make_async_copy(a, b, sems.at[4 + i]) for i, (a, b) in enumerate(
        ((zp_hbm, zp_ref), (fy_hbm, fy_ref), (z1_hbm, z1_ref), (ty_hbm, ty_ref), (te_hbm, te_ref), (tl_hbm, tl_ref), (zu_hbm, zu_ref)))]
    for i in (3, 0, 1, 2, 4, 5):
        loads[i].start()
    pl.when(z < nz - 2)(lambda: greet(0))
    pl.when(z < nz - 3)(lambda: greet(1))
    pl.when(z < nz - 4)(lambda: greet(2))
    for e, r, count in unsent():
        vi_ref[e, r:r + count, :] = jnp.zeros((count, 128), F32)

    @pl.when(z >= nz - 2)
    def _():
        pl.semaphore_wait(barrier, jnp.where(z == nz - 2, 5, 10))
        say_hello(2, range(-2, 3))
        pl.when(z == nz - 1)(lambda: say_hello(1, range(-2, 3)))

    loads[3].wait()
    prepare_states(-1, v_ref, vo_ref, xh)
    pl.when(z == nz - 1)(lambda: start_ahead((True,), False))
    for load in loads[:3]:
        load.wait()
    for t in range(4):
        for i, value in enumerate(own_basis([v_ref[x, 8 * t:8 * t + 8, :] for x in range(32)])):
            basis[i, t] = value
    loads[4].wait()
    loads[5].wait()
    prepare_pairs(EARLY, len(PAIRS) - EARLY, weights, zp_ref, fy_ref, vo_ref, basis)

    @pl.when(z >= nz - 2)
    def _():
        start(-2)
        pl.when(z == nz - 1)(lambda: start_ahead((False,), False))

    for load in loads[6:]:
        load.start()
    prepare_states(1, v_ref, vo_ref, xh)
    prepare_pairs(0, EARLY, weights, zp_ref, fy_ref, vo_ref, basis)
    loads[6].wait()
    for t in range(4):
        zt[:, 8 * t:8 * t + 8, :] = wide_dot(v_ref[:, 8 * t:8 * t + 8, :].reshape(256, 128), z1_ref).reshape(32, 8, 128)
    prepare_rows(vo_ref, zt)

    @pl.when(z < nz - 2)
    def _():
        pl.semaphore_wait(barrier, jnp.where(z == 0, 14, jnp.where(z == 1, 19, 24)))

        @pl.when(z == nz - 3)
        def _():
            say_hello(1, (0,))
            say_hello(2, (0,))

        start(-2)
        pl.when(z > 1)(lambda: start(2))
        start(-1)
        pl.when(z > 0)(lambda: start(1))
        start(0)

    @pl.when(z == nz - 2)
    def _():
        pl.semaphore_wait(hello.at[0], 1)
        start(-1)

    @pl.when(z == nz - 1)
    def _():
        pl.semaphore_wait(hello.at[1], 1)
        start_ahead((True, False), True)

    @pl.when(z >= nz - 2)
    def _():
        start(2)
        start(1)
        start(0)

    sub = lax.broadcasted_iota(jnp.int32, (8, 128), 0)
    first, last = sub == 0, sub == 7

    def row(ref, e, r):
        return jnp.broadcast_to(ref[e, pl.ds(r, 1), :], (8, 128))

    def plane(x):
        p = [zt[x, pl.ds(r, 8, 4), :] for r in range(4)]
        halo = [row(vi_ref, Y_STATES + 4 * (k % 2) + x // 8, Y_AT[-1 if k < 2 else 1] + x % 8) for k in range(4)]
        for r, v in enumerate(split_y(p, halo, first, last)):
            ys_ref[x + 2, r] = v

    def state_planes(dx):
        e, side = X_STATES[dx], (dx + 1) // 2
        xz[side] = wide_dot(jnp.concatenate([vi_ref[e, 0:32, :], vi_ref[e + 1, 0:32, :], vi_ref[e, 32:48, :]], 0), z1_ref)
        for q in (0, 1):
            p = [xz[side, pl.ds(32 * q + r, 8, 4), :] for r in range(4)]
            halo = [row(xz, side, 64 + 8 * (k // 2) + 2 * (k % 2) + q) for k in range(4)]
            for r, v in enumerate(split_y(p, halo, first, last)):
                ys_ref[34 * side + q, r] = v

    def upper(first_pair, count, out_ref):
        done = []
        for i in range(first_pair, first_pair + count):
            e = PAIRS[i]
            v = vi_ref[e]
            own = vo_ref[e, 0:32, :] if i < COUNT[0] // 2 else jnp.concatenate([v[0:24], jnp.zeros((8, 128), F32)], 0)
            done.append(jnp.concatenate([own, v[32:]], 0))
        for i in range(0, count, 2):
            high, mid, low = split(jnp.concatenate(done[i:i + 2], 1))
            r = (dot(whole(ty_ref, 1, columns=192), jnp.concatenate([high, mid, high], 0))
                 + dot(whole(ty_ref, 0, columns=192), jnp.concatenate([high, mid, low], 0)))
            for j in range(min(2, count - i)):
                for t in range(4):
                    out_ref[t // 2, first_pair % EARLY + i + j, :, 128 * (t % 2):128 * (t % 2) + 128] = r[8 * t:8 * t + 8, 128 * j:128 * j + 128]

    loads[7].wait()
    arrive(0)
    for x in range(32):
        plane(x)
    upper(0, 10, te_in)

    arrive(1)
    state_planes(1)
    arrive(2)
    upper(10, 5, te_in)
    loads[8].wait()
    for u, (ref, at, rows) in enumerate(((e2_ref, 0, 128), (e34_ref, 128, 96))):
        high, mid, low = split(te_in[u].reshape(8 * EARLY, 256))
        high_mid, high_low = [jnp.concatenate([high, w], 0) for w in (mid, low)]
        m = [[whole(te_ref, k, h, rows=slice(at, at + rows), columns=240) for k in range(3)] for h in (0, 1)]
        v = [dot(m[h][2], high_low) + dot(m[h][1], high_mid) + dot(m[h][0], high_mid) for h in (0, 1)]
        ref[...] = jnp.where(lax.broadcasted_iota(jnp.int32, (rows, 256), 1) % 128 < 64, v[0], v[1])

    loads[10].wait()
    l2 = wide_dot(jnp.concatenate([e2_ref[:, :128], e2_ref[:, 128:]], 0), zu_ref, 0).reshape(2, 16, 8, 128)
    l3 = wide_dot(e34_ref[:64, :128], zu_ref, 1).reshape(8, 8, 128)
    l4 = wide_dot(e34_ref[64:, 128:], zu_ref, 2).reshape(4, 8, 128)
    for i in range(2, 16):
        for t in (0, 1):
            up[i, t] = merge(i, t, l2[t, i], l3, l4)
    lift_x(ys_ref, up, done)
    loads[9].wait()

    @pl.when(z < 2)
    def _():
        pl.semaphore_wait(hello.at[1], 5)
        start(2)

    @pl.when(z == 0)
    def _():
        pl.semaphore_wait(hello.at[0], 5)
        start(1)

    arrive(-1, (True,))
    state_planes(-1)
    first_x(ys_ref, done)
    arrive(-2)
    arrive(-1, (False,))
    upper(15, 5, tl_out)
    for *_, copy in copies:
        copy.wait_send()


def merge(i, t, v, l3, l4):
    sub = lax.broadcasted_iota(jnp.int32, (8, 128), 0)
    lane = lax.broadcasted_iota(jnp.int32, (8, 128), 1)
    if i % 2 or t:
        return v
    w = l3[i // 2]
    if i % 4 == 0:
        w = jnp.where((lane % 8 == 0) & (sub % 2 == 0), l4[i // 4], w)
    return jnp.where(lane % 4 == 0, w, v)


def lift_x(ys, up, done):
    odd_lane = lax.broadcasted_iota(jnp.int32, (8, 128), 1) % 2 == 1
    state = {}
    for r in range(4):
        state[r] = (ys[3, r] + LIFT_A * (ys[2, r] + ys[4, r]), None, None)
    for i in range(1, 17):
        for r in range(4):
            o, e, q = state[r]
            if i < 16:
                p = ys[2 + 2 * i, r]
                o_now = ys[3 + 2 * i, r] + LIFT_A * (p + ys[4 + 2 * i, r])
                e_now = p + LIFT_B * (o + o_now)
            else:
                o_now, e_now = None, ys[35, r] + LIFT_B * o
            q_now = None
            if i > 1:
                q_now = o + LIFT_C * (e + e_now)
                done[i - 1, 1, pl.ds(r, 8, 4), :] = q_now * LIFT_K
            if i > 2:
                low = (e + LIFT_D * (q + q_now)) * (1 / LIFT_K)
                done[i - 1, 0, pl.ds(r, 8, 4), :] = low if r % 2 else jnp.where(odd_lane, low, up[i - 1, r // 2])
            state[r] = (o_now, e_now, q_now)


def first_x(ys, done):
    for r in range(4):
        o = [ys[0, r] + LIFT_A * ys[2, r], *(ys[3 + 2 * i, r] + LIFT_A * (ys[2 + 2 * i, r] + ys[4 + 2 * i, r]) for i in range(3))]
        e = [ys[1, r] + LIFT_B * o[0], *(ys[2 + 2 * i, r] + LIFT_B * (o[i] + o[i + 1]) for i in range(3))]
        q = [o[i] + LIFT_C * (e[i] + e[i + 1]) for i in range(3)]
        for i in range(2):
            done[i, 0, pl.ds(r, 8, 4), :] = (e[i + 1] + LIFT_D * (q[i] + q[i + 1])) * (1 / LIFT_K)
        done[0, 1, pl.ds(r, 8, 4), :] = q[1] * LIFT_K


def finish(done, tl, e2_ref, e34_ref, tl_ref, zu_ref, out_ref, even, sems):
    lane = lax.broadcasted_iota(jnp.int32, (8, 128), 1)
    copies = []

    def store(source, at, side):
        copies.append(pltpu.make_async_copy(source, out_ref.at[at, side], sems.at[len(copies)]))
        copies[-1].start()

    for at in ((0, 16, 1), (5, 6, 0), (7, 8, 0), (9, 10, 0), (11, 12, 0), (13, 16, 0)):
        piece = pl.ds(at[0], at[1] - at[0])
        store(done.at[piece, at[2]], piece, at[2])

    def late(u, at, rows):
        v = stacked(tl[u].reshape(8 * (len(PAIRS) - EARLY), 256))
        v = [dot(whole(tl_ref, h, rows=slice(at, at + rows), columns=240), v) for h in (0, 1)]
        return jnp.where(lax.broadcasted_iota(jnp.int32, (rows, 256), 1) % 128 < 64, v[0], v[1])

    v = e2_ref[0:48, :] + late(0, 0, 48)
    l2 = wide_dot(jnp.concatenate([v[:, :128], v[:, 128:]], 0), zu_ref, 0).reshape(2, 6, 8, 128)
    v = e34_ref[...] + late(1, 48, 96)
    l3 = wide_dot(v[:64, :128], zu_ref, 1).reshape(8, 8, 128)
    l4 = wide_dot(v[64:, 128:], zu_ref, 2).reshape(4, 8, 128)
    for k, i in enumerate((0, 1, 2, 3, 4, 6, 8, 10, 12)):
        for r in range(4):
            v = done[i, 0, pl.ds(r, 8, 4), :]
            if i < 5 and r % 2 == 0:
                v = jnp.where(lane % 2 == 1, v, merge(i, r // 2, l2[r // 2, i], l3, l4))
            elif r == 0:
                v = merge(i, 0, v, l3, l4)
            even[k, pl.ds(r, 8, 4), :] = v
        if i == 4:
            store(even.at[pl.ds(0, 5)], pl.ds(0, 5), 0)
        elif i > 4:
            store(even.at[k], i, 0)
    for copy in copies:
        copy.wait()


def solution(mesh):
    nx, ny = mesh.shape["gx"], mesh.shape["gy"]
    weights, (zp, fy, z1, ty, te, tl, zu) = operators()
    vmem, hbm = pl.BlockSpec(memory_space=pltpu.VMEM), pl.BlockSpec(memory_space=pltpu.HBM)
    limit = 24 * 1024 * 1024
    block, pairs = (32, 32, 128), (16, 2, 32, 128)
    moves = pltpu.SemaphoreType.DMA((len(MOVES),))

    def kept(*ms):
        return [pltpu.with_memory_space_constraint(jnp.asarray(m), pltpu.HBM) for m in ms]

    def local(v):
        parts = pl.pallas_call(
            functools.partial(exchange, nx, ny, 8, weights.tolist()),
            out_shape=[*(pltpu.VMEM(s, F32) for s in (pairs, (2, len(PAIRS) - EARLY, 8, 256), (128, 256), (96, 256))),
                       *(pltpu.VMEM(m.shape, BF16) for m in (tl, zu))],
            in_specs=[hbm] * 8, out_specs=[vmem] * 6,
            scratch_shapes=[pltpu.VMEM(block, F32), *([pltpu.VMEM((ENTRIES, ROWS, 128), F32)] * 2), pltpu.VMEM((36, 4, 8, 128), F32), *(pltpu.VMEM(m.shape, BF16) for m in (zp, fy, z1, ty, te)),
                            pltpu.VMEM((2, EARLY, 8, 256), F32), pltpu.VMEM(block, F32), pltpu.VMEM((20, 4, 8, 128), F32), pltpu.VMEM((2, 32, 128), F32), pltpu.VMEM((16, 2, 8, 128), F32),
                            pltpu.VMEM((2, 80, 128), F32), moves, moves, pltpu.SemaphoreType.REGULAR((2,)), pltpu.SemaphoreType.DMA((11,))],
            compiler_params=pltpu.CompilerParams(collective_id=0, has_side_effects=True, vmem_limit_bytes=limit),
        )(*kept(v, zp, fy, z1, ty, te, tl, zu))
        return pl.pallas_call(
            finish,
            out_shape=jax.ShapeDtypeStruct(pairs, F32),
            in_specs=[vmem] * 6, out_specs=pl.BlockSpec(memory_space=pl.ANY),
            scratch_shapes=[pltpu.VMEM((9, 32, 128), F32), pltpu.SemaphoreType.DMA((11,))],
            compiler_params=pltpu.CompilerParams(vmem_limit_bytes=limit),
        )(*parts).reshape(block)

    spec = P("gx", "gy", None)
    return jax.shard_map(local, mesh=mesh, in_specs=(spec,), out_specs=spec, check_vma=False)
```

```python
import functools

import jax
import jax.numpy as jnp
import ml_dtypes
import numpy as np
from jax import lax
from jax.experimental import pallas as pl
from jax.experimental.pallas import tpu as pltpu
from jax.sharding import PartitionSpec as P

LIFT_A, LIFT_B, LIFT_C, LIFT_D = -1.586134342, -0.05298011854, 0.8829110762, 0.4435068522
LIFT_K = 1.149604398
MESH = pl.DeviceIdType.MESH
F32, BF16 = jnp.float32, jnp.bfloat16

COUNT = {0: 20, 1: 8, 2: 2, -1: 8, -2: 2}
X_AT = {0: 0, 1: 18, 2: 24, -1: 25, -2: 31}
Y_AT = {0: 0, -1: 32, 1: 40, -2: 48, 2: 56}
ENTRIES, ROWS = 32, 64
PAIRS = [X_AT[o] + p for o, c in COUNT.items() for p in range(c // 2)]
LATE = (6, 8, 4)
EARLY = 15
Y_STATES = 10
X_STATES = {1: 22, -1: 29}
OFFSETS = (0, -1, 1, -2, 2)
GROUP = {dx: [(dx, dy) for dy in (-2, 2, -1, 1, 0) if (dx, dy) != (0, 0)] for dx in OFFSETS}


def pieces(dx, dy):
    if dx == 0:
        return [(False, (0, 18), (Y_AT[dy], 8))] if abs(dy) == 1 else [(False, (0, 10), (Y_AT[dy], 2))]
    if abs(dx) == 2:
        return [(False, (X_AT[dx], 1), (Y_AT[dy], 2 if abs(dy) == 2 else 4))]
    if dy == 0:
        return [(True, (X_STATES[dx], 2), (0, 32)), (False, (X_AT[dx], 4), (0, 20))]
    if abs(dy) == 1:
        return [(True, (X_STATES[dx], 1), (Y_AT[dy], 4)), (False, (X_AT[dx], 4), (Y_AT[dy], 7))]
    return [(False, (X_AT[dx], 2), (Y_AT[dy], 2))]


MOVES = [(dx, dy, *piece) for dx in OFFSETS for dx, dy in GROUP[dx] for piece in pieces(dx, dy)]


def counter(dx, dy, is_states):
    return ["0 1", "0 2", "-1 s", "-1 p", "1 s", "1 p", "-2 p", "2 p"].index(f"0 {abs(dy)}" if dx == 0 else f"{dx} {'s' if is_states else 'p'}")


COUNTERS = 8


def area(rows):
    return next((rows // r, r) for r in range(ROWS, 0, -1) if rows % r == 0 and rows // r <= ENTRIES)


def unsent():
    sent = {(e, r) for _, _, _, (e0, ne), (r0, nr) in MOVES for e in range(e0, e0 + ne) for r in range(r0, r0 + nr)}
    out = [(e, Y_AT[dy] + 4, 4) for e in X_STATES.values() for dy in (-1, 1)]
    for e in PAIRS:
        for tile in range(32 if e < X_AT[1] else 0, ROWS, 8):
            count = sum((e, r) in sent for r in range(tile, tile + 8))
            if count < 8 and tile != 24:
                out.append((e, tile + count, 8 - count))
    return out


def lift_1d(v):
    even, odd = v[0::2], v[1::2]
    odd = odd + LIFT_A * (even + np.roll(even, -1, 0))
    even = even + LIFT_B * (np.roll(odd, 1, 0) + odd)
    odd = odd + LIFT_C * (even + np.roll(even, -1, 0))
    even = even + LIFT_D * (np.roll(odd, 1, 0) + odd)
    return even / LIFT_K, odd * LIFT_K


def interleave(low, high):
    out = np.empty((2 * low.shape[0], low.shape[1]))
    out[0::2], out[1::2] = low, high
    return out


def row_space(parts, count):
    basis = np.zeros((0, parts[0].shape[1]))
    for part in parts:
        rest = part - part @ basis.T @ basis
        size, rows = np.linalg.svd(rest)[1:]
        basis = np.concatenate([basis, rows[:int((size > 1e-9).sum())]])
    return np.concatenate([basis, np.zeros((count - len(basis), basis.shape[1]))])


def thirds(matrix):
    out, rest = [], np.asarray(matrix, np.float64)
    for _ in range(3):
        out.append(rest.astype(ml_dtypes.bfloat16))
        rest = rest - out[-1].astype(np.float64)
    return out


def operators():
    n, blocks, mid = 32, 16, 8
    low, levels = np.eye(n * blocks), {}
    for level in range(1, 5):
        low, high = lift_1d(low)
        m = n >> level
        levels[level] = interleave(low[mid * m:(mid + 1) * m], high[mid * m:(mid + 1) * m])
    functional, combine = {}, {}
    for offset, count in COUNT.items():
        parts = [levels[level][:, (mid + offset) * n:(mid + offset + 1) * n] for level in (4, 3, 2)]
        functional[offset] = row_space(parts, count)
        combine[offset] = np.concatenate(parts[::-1])
    basis = np.stack(own_basis(np.eye(n)))
    inverse = np.linalg.pinv(basis)
    weights = np.concatenate([functional[o] @ inverse for o in COUNT if o])
    cx = [np.concatenate([(combine[o] @ (functional[o].T if o else inverse))[:, h::2] for o in COUNT], 1) for h in (0, 1)]
    first = [at + i for at, count in zip((0, 16, 24), LATE) for i in range(count)]
    assert all(np.abs(np.delete(c[:, EARLY:], first, 0)).max() < 1e-12 for c in cx)
    early = np.stack([np.kron(c[:, :EARLY], np.eye(8)) for c in cx])
    late = np.stack([np.kron(c[first, EARLY:], np.eye(8)) for c in cx])
    high, mid_, low = thirds(early)
    early = np.stack([np.concatenate(m, 2) for m in ((high, high), (mid_, mid_), (low, high))])
    high, mid_, low = thirds(late)
    late = np.concatenate([high, high, high, mid_, mid_, low], 2)
    fy, cy = np.zeros((ROWS, 32)), np.zeros((28, ROWS))
    for offset, count in COUNT.items():
        at = Y_AT[offset]
        fy[at:at + count], cy[:, at:at + count] = functional[offset], combine[offset] @ functional[offset].T
    ty = np.zeros((32, ROWS))
    ty[0:8], ty[8:16], ty[16:24], ty[24:32:2] = cy[0:16:2], cy[1:16:2], cy[16:24], cy[24:28]
    high, mid_, low = thirds(fy)
    fy = np.concatenate([high, high, high, mid_, mid_, low], 1)
    high, mid_, low = thirds(ty)
    ty = np.stack([np.concatenate(m, 1) for m in ((high, high, high), (mid_, mid_, low))])
    low, high = lift_1d(np.eye(128))
    z1 = wide(interleave(low, high).T)
    zp = np.concatenate(thirds(np.kron(np.eye(2), low.T)), 1)
    low, zu = np.eye(64), np.zeros((3, 64, 128))
    for level in range(3):
        low, high = lift_1d(low)
        zu[level, :, ::2 << level] = interleave(low, high).T
    zu = np.stack([wide(np.concatenate([m, m])) for m in zu])
    return weights, [tiles(m) for m in (zp, fy, z1, ty, early, late, zu)]


def wide(matrix):
    high, mid, low = thirds(matrix)
    return np.concatenate([np.concatenate(m) for m in ((high, high), (mid, mid), (low, high))], 1)


def tiles(matrix):
    columns = -(-matrix.shape[-1] // 128) * 128
    padded = np.zeros((*matrix.shape[:-1], columns), matrix.dtype)
    padded[..., :matrix.shape[-1]] = matrix
    return np.moveaxis(padded.reshape(*matrix.shape[:-1], columns // 128, 128), -2, -3)


def whole(ref, *at, rows=slice(None), columns=None):
    count = ref.shape[len(at)]
    out = ref[(*at, 0, rows)] if count == 1 else jnp.concatenate([ref[(*at, i, rows)] for i in range(count)], 1)
    return out if columns is None else out[:, :columns]


def dot(a, b):
    return lax.dot_general(a, b, (((1,), (0,)), ((), ())), preferred_element_type=F32)


def split(v):
    high = v.astype(BF16)
    rest = v - high.astype(F32)
    mid = rest.astype(BF16)
    return high, mid, (rest - mid.astype(F32)).astype(BF16)


def stacked(v):
    high, mid, low = split(v)
    return jnp.concatenate([high, mid, low, high, mid, high], 0)


def wide_dot(v, ref, *at):
    high, mid, low = split(v)
    m = whole(ref, *at)
    n = m.shape[1] // 3
    v = dot(jnp.concatenate([high, mid], 1), m[:, :2 * n])
    return dot(jnp.concatenate([high, low], 1), m[:, 2 * n:]) + v[:, n:] + v[:, :n]


def states(s, side):
    if side < 0:
        return s(31) + LIFT_A * s(30), s(30) + LIFT_B * (s(29) + LIFT_A * (s(28) + s(30)))
    return s(0), s(0) + LIFT_B * (s(1) + LIFT_A * (s(0) + s(2)))


def own_basis(v):
    out, odd, even, odd3 = [], 0.0, 0.0, 0.0
    for i in range(17):
        if i < 16:
            after = v[2 * i + 2] if i < 15 else 0.0
            odd_now = v[2 * i + 1] + LIFT_A * (v[2 * i] + after)
            even_now = v[2 * i] + LIFT_B * (odd + odd_now)
        else:
            odd_now, even_now = None, LIFT_B * odd
        if i > 0:
            odd3_now = odd + LIFT_C * (even + even_now)
            out.append(even + LIFT_D * (odd3 + odd3_now))
            odd3 = odd3_now
        odd, even = odd_now, even_now
    return [*out, *states(lambda i: v[i], -1), *states(lambda i: v[i], 1)]


def prepare_states(dx, v_ref, vo_ref, xh):
    e = X_STATES[dx]
    for q, plane in enumerate(states(lambda x: v_ref[x], dx)):
        xh[q] = plane
        vo_ref[e + q, 0:32, :] = plane
    for dy in (-1, 1):
        at = Y_AT[dy]
        for p, rows in enumerate(states(lambda y: xh[:, y, :], dy)):
            vo_ref[e, at + 2 * p:at + 2 * p + 2, :] = rows
        vo_ref[e, at + 4:at + 8, :] = jnp.zeros((4, 128), F32)


def prepare_pairs(first, count, weights, zp_ref, fy_ref, vo_ref, basis):
    sides = []
    for h in (0, 1):
        rows = []
        for i in range(first, first + count):
            f = 2 * i + h
            for t in range(4):
                if f < 20:
                    rows.append(basis[f, t])
                    continue
                terms = [w * basis[k, t] for k, w in enumerate(weights[f - 20]) if abs(w) > 1e-14]
                while len(terms) > 1:
                    terms = [sum(terms[k:k + 2][1:], terms[k]) for k in range(0, len(terms), 2)]
                rows.append(terms[0] if terms else jnp.zeros((8, 128), F32))
        sides.append(jnp.concatenate(rows, 0))
    high, mid, low = split(jnp.concatenate(sides, 1))
    m = whole(zp_ref)
    packed = dot(high, m[:, :256]) + dot(mid, m[:, :256])
    packed = dot(low, m[:, :128]) + dot(high, m[:, 256:]) + packed[:, 128:] + packed[:, :128]
    columns = [stacked(packed[32 * i:32 * i + 32]) for i in range(count)]
    for i in range(0, count, 2):
        rows = dot(whole(fy_ref, columns=192), jnp.concatenate(columns[i:i + 2], 1))
        for j in range(min(2, count - i)):
            vo_ref[PAIRS[first + i + j]] = rows[:, 128 * j:128 * j + 128]


def prepare_rows(vo_ref, zt):
    for dy in (-1, 1):
        for q, rows in enumerate(states(lambda y: zt[:, y, :], dy)):
            for t in range(4):
                vo_ref[Y_STATES + 4 * q + t, Y_AT[dy]:Y_AT[dy] + 8, :] = rows[8 * t:8 * t + 8]


def split_y(p, halo, first, last):
    a, b, c, d = halo
    p0, p1, p2, p3 = p

    def following(v, edge):
        return jnp.where(last, edge, pltpu.roll(v, 7, 0))

    def preceding(v, edge):
        return jnp.where(first, edge, pltpu.roll(v, 1, 0))

    o0 = p1 + LIFT_A * (p0 + p2)
    o1 = p3 + LIFT_A * (p2 + following(p0, c))
    before = a + LIFT_A * p0
    e0 = p0 + LIFT_B * (preceding(o1, before) + o0)
    e1 = p2 + LIFT_B * (o0 + o1)
    q0 = o0 + LIFT_C * (e0 + e1)
    q1 = o1 + LIFT_C * (e1 + following(e0, d + LIFT_B * o1))
    before = before + LIFT_C * (b + LIFT_B * before + e0)
    f0 = e0 + LIFT_D * (preceding(q1, before) + q0)
    f1 = e1 + LIFT_D * (q0 + q1)
    return f0 * (1 / LIFT_K), q0 * LIFT_K, f1 * (1 / LIFT_K), q1 * LIFT_K


def exchange(nx, ny, nz, weights, v_hbm, zp_hbm, fy_hbm, z1_hbm, ty_hbm, te_hbm, tl_hbm, zu_hbm,
             done, tl_out, e2_ref, e34_ref, tl_ref, zu_ref,
             v_ref, vo_ref, vi_ref, ys_ref, zp_ref, fy_ref, z1_ref, ty_ref, te_ref, te_in, zt, basis, xh, up, xz, send, recv, hello, sems):
    x, y = lax.axis_index("gx"), lax.axis_index("gy")
    z = lax.rem(x, nz)

    def device(dx, dy):
        return lax.rem(x + dx + nx, nx), lax.rem(y + dy + ny, ny)

    copies, arriving = [], [0] * COUNTERS
    for dx, dy, is_states, (e, ne), (r, nr) in MOVES:
        at, k = (pl.ds(e, ne), pl.ds(r, nr)), counter(dx, dy, is_states)
        arriving[k] += ne * nr
        copies.append((dx, dy, is_states, pltpu.make_async_remote_copy(
            src_ref=vo_ref.at[at], dst_ref=vi_ref.at[at], send_sem=send, recv_sem=recv.at[k],
            device_id=device(-dx, -dy), device_id_type=MESH)))

    def wait_rows(sem, rows):
        n, r = area(rows)
        some = vi_ref.at[pl.ds(0, n), pl.ds(0, r)]
        pltpu.make_async_copy(some, some, sem).wait()

    def start(which, kinds=(True, False)):
        for dx, _, is_states, copy in copies:
            if dx == which and is_states in kinds:
                copy.start()

    def start_ahead(kinds, waits):
        for dx, dy, is_states, copy in copies:
            if dx == -1 and is_states in kinds:
                if dy in (0, 1):
                    pl.when(((x == nx - 1) & (y == dy)) == waits)(copy.start)
                elif not waits:
                    copy.start()

    def arrive(which, kinds=(True, False)):
        for k in sorted({counter(dx, dy, is_states) for dx, dy, is_states, _ in copies if dx == which and is_states in kinds}):
            wait_rows(recv.at[k], arriving[k])

    barrier = pltpu.get_barrier_semaphore()

    def greet(dx):
        for o in GROUP[dx]:
            pl.semaphore_signal(barrier, inc=1, device_id=device(*o), device_id_type=MESH)

    def say_hello(dx, dys):
        for dy in dys:
            pl.semaphore_signal(hello.at[dx - 1], inc=1, device_id=device(dx, dy), device_id_type=MESH)

    loads = [pltpu.make_async_copy(a, b, sems.at[i]) for i, (a, b) in enumerate(
        ((v_hbm, v_ref), (zp_hbm, zp_ref), (fy_hbm, fy_ref), (z1_hbm, z1_ref), (ty_hbm, ty_ref), (te_hbm, te_ref), (tl_hbm, tl_ref), (zu_hbm, zu_ref)))]
    loads[0].start()
    pl.when(z != nz - 1)(lambda: greet(-1))
    greet(-2)
    loads[1].start()
    loads[2].start()

    @pl.when(z >= nz - 2)
    def _():
        pl.semaphore_wait(barrier, jnp.where(z == nz - 2, 5, 10))
        pl.when(z == nz - 1)(lambda: say_hello(1, range(-2, 3)))
        say_hello(2, range(-2, 3))

    @pl.when(z < nz - 2)
    def _():
        greet(0)
        pl.when(z < nz - 3)(lambda: greet(1))
        pl.when(z < nz - 4)(lambda: greet(2))

    for e, r, count in unsent():
        vi_ref[e, r:r + count, :] = jnp.zeros((count, 128), F32)
    loads[0].wait()
    prepare_states(-1, v_ref, vo_ref, xh)
    pl.when(z == nz - 1)(lambda: start_ahead((True,), False))
    for t in range(4):
        for i, value in enumerate(own_basis([v_ref[x, 8 * t:8 * t + 8, :] for x in range(32)])):
            basis[i, t] = value
    loads[1].wait()
    loads[2].wait()
    prepare_pairs(EARLY, len(PAIRS) - EARLY, weights, zp_ref, fy_ref, vo_ref, basis)

    @pl.when(z >= nz - 2)
    def _():
        start(-2)
        pl.when(z == nz - 1)(lambda: start_ahead((False,), False))

    for load in loads[3:]:
        load.start()
    prepare_states(1, v_ref, vo_ref, xh)
    prepare_pairs(0, EARLY, weights, zp_ref, fy_ref, vo_ref, basis)
    loads[3].wait()
    for t in range(4):
        zt[:, 8 * t:8 * t + 8, :] = wide_dot(v_ref[:, 8 * t:8 * t + 8, :].reshape(256, 128), z1_ref).reshape(32, 8, 128)
    prepare_rows(vo_ref, zt)

    @pl.when(z < nz - 2)
    def _():
        pl.semaphore_wait(barrier, jnp.where(z == 0, 14, jnp.where(z == 1, 19, 24)))

        @pl.when(z == nz - 3)
        def _():
            say_hello(1, (0,))
            say_hello(2, (0,))

        start(-2)
        pl.when(z > 1)(lambda: start(2))
        start(-1)
        pl.when(z > 0)(lambda: start(1))
        start(0)

    @pl.when(z == nz - 2)
    def _():
        pl.semaphore_wait(hello.at[0], 1)
        start(-1)

    @pl.when(z == nz - 1)
    def _():
        pl.semaphore_wait(hello.at[1], 1)
        start_ahead((True, False), True)

    @pl.when(z >= nz - 2)
    def _():
        start(2)
        start(1)
        start(0)

    sub = lax.broadcasted_iota(jnp.int32, (8, 128), 0)
    first, last = sub == 0, sub == 7

    def row(ref, e, r):
        return jnp.broadcast_to(ref[e, pl.ds(r, 1), :], (8, 128))

    def plane(x):
        p = [zt[x, pl.ds(r, 8, 4), :] for r in range(4)]
        halo = [row(vi_ref, Y_STATES + 4 * (k % 2) + x // 8, Y_AT[-1 if k < 2 else 1] + x % 8) for k in range(4)]
        for r, v in enumerate(split_y(p, halo, first, last)):
            ys_ref[x + 2, r] = v

    def state_planes(dx):
        e, side = X_STATES[dx], (dx + 1) // 2
        xz[side] = wide_dot(jnp.concatenate([vi_ref[e, 0:32, :], vi_ref[e + 1, 0:32, :], vi_ref[e, 32:48, :]], 0), z1_ref)
        for q in (0, 1):
            p = [xz[side, pl.ds(32 * q + r, 8, 4), :] for r in range(4)]
            halo = [row(xz, side, 64 + 8 * (k // 2) + 2 * (k % 2) + q) for k in range(4)]
            for r, v in enumerate(split_y(p, halo, first, last)):
                ys_ref[34 * side + q, r] = v

    def upper(first_pair, count, out_ref):
        done = []
        for i in range(first_pair, first_pair + count):
            e = PAIRS[i]
            v = vi_ref[e]
            own = vo_ref[e, 0:32, :] if i < COUNT[0] // 2 else jnp.concatenate([v[0:24], jnp.zeros((8, 128), F32)], 0)
            done.append(jnp.concatenate([own, v[32:]], 0))
        for i in range(0, count, 2):
            high, mid, low = split(jnp.concatenate(done[i:i + 2], 1))
            r = (dot(whole(ty_ref, 1, columns=192), jnp.concatenate([high, mid, high], 0))
                 + dot(whole(ty_ref, 0, columns=192), jnp.concatenate([high, mid, low], 0)))
            for j in range(min(2, count - i)):
                for t in range(4):
                    out_ref[t // 2, first_pair % EARLY + i + j, :, 128 * (t % 2):128 * (t % 2) + 128] = r[8 * t:8 * t + 8, 128 * j:128 * j + 128]

    loads[4].wait()
    arrive(0)
    for x in range(32):
        plane(x)
    upper(0, 10, te_in)

    arrive(1)
    state_planes(1)
    arrive(2)
    upper(10, 5, te_in)
    loads[5].wait()
    for u, (ref, at, rows) in enumerate(((e2_ref, 0, 128), (e34_ref, 128, 96))):
        high, mid, low = split(te_in[u].reshape(8 * EARLY, 256))
        high_mid, high_low = [jnp.concatenate([high, w], 0) for w in (mid, low)]
        m = [[whole(te_ref, k, h, rows=slice(at, at + rows), columns=240) for k in range(3)] for h in (0, 1)]
        v = [dot(m[h][2], high_low) + dot(m[h][1], high_mid) + dot(m[h][0], high_mid) for h in (0, 1)]
        ref[...] = jnp.where(lax.broadcasted_iota(jnp.int32, (rows, 256), 1) % 128 < 64, v[0], v[1])

    loads[7].wait()
    l2 = wide_dot(jnp.concatenate([e2_ref[:, :128], e2_ref[:, 128:]], 0), zu_ref, 0).reshape(2, 16, 8, 128)
    l3 = wide_dot(e34_ref[:64, :128], zu_ref, 1).reshape(8, 8, 128)
    l4 = wide_dot(e34_ref[64:, 128:], zu_ref, 2).reshape(4, 8, 128)
    for i in range(2, 16):
        for t in (0, 1):
            up[i, t] = merge(i, t, l2[t, i], l3, l4)
    lift_x(ys_ref, up, done)
    loads[6].wait()

    @pl.when(z < 2)
    def _():
        pl.semaphore_wait(hello.at[1], 5)
        start(2)

    @pl.when(z == 0)
    def _():
        pl.semaphore_wait(hello.at[0], 5)
        start(1)

    arrive(-1, (True,))
    state_planes(-1)
    first_x(ys_ref, done)
    arrive(-2)
    arrive(-1, (False,))
    upper(15, 5, tl_out)
    wait_rows(send, sum(arriving))


def merge(i, t, v, l3, l4):
    sub = lax.broadcasted_iota(jnp.int32, (8, 128), 0)
    lane = lax.broadcasted_iota(jnp.int32, (8, 128), 1)
    if i % 2 or t:
        return v
    w = l3[i // 2]
    if i % 4 == 0:
        w = jnp.where((lane % 8 == 0) & (sub % 2 == 0), l4[i // 4], w)
    return jnp.where(lane % 4 == 0, w, v)


def lift_x(ys, up, done):
    odd_lane = lax.broadcasted_iota(jnp.int32, (8, 128), 1) % 2 == 1
    state = {}
    for r in range(4):
        state[r] = (ys[3, r] + LIFT_A * (ys[2, r] + ys[4, r]), None, None)
    for i in range(1, 17):
        for r in range(4):
            o, e, q = state[r]
            if i < 16:
                p = ys[2 + 2 * i, r]
                o_now = ys[3 + 2 * i, r] + LIFT_A * (p + ys[4 + 2 * i, r])
                e_now = p + LIFT_B * (o + o_now)
            else:
                o_now, e_now = None, ys[35, r] + LIFT_B * o
            q_now = None
            if i > 1:
                q_now = o + LIFT_C * (e + e_now)
                done[i - 1, 1, pl.ds(r, 8, 4), :] = q_now * LIFT_K
            if i > 2:
                low = (e + LIFT_D * (q + q_now)) * (1 / LIFT_K)
                done[i - 1, 0, pl.ds(r, 8, 4), :] = low if r % 2 else jnp.where(odd_lane, low, up[i - 1, r // 2])
            state[r] = (o_now, e_now, q_now)


def first_x(ys, done):
    for r in range(4):
        o = [ys[0, r] + LIFT_A * ys[2, r], *(ys[3 + 2 * i, r] + LIFT_A * (ys[2 + 2 * i, r] + ys[4 + 2 * i, r]) for i in range(3))]
        e = [ys[1, r] + LIFT_B * o[0], *(ys[2 + 2 * i, r] + LIFT_B * (o[i] + o[i + 1]) for i in range(3))]
        q = [o[i] + LIFT_C * (e[i] + e[i + 1]) for i in range(3)]
        for i in range(2):
            done[i, 0, pl.ds(r, 8, 4), :] = (e[i + 1] + LIFT_D * (q[i] + q[i + 1])) * (1 / LIFT_K)
        done[0, 1, pl.ds(r, 8, 4), :] = q[1] * LIFT_K


def finish(done, tl, e2_ref, e34_ref, tl_ref, zu_ref, out_ref, even, sem):
    lane = lax.broadcasted_iota(jnp.int32, (8, 128), 1)

    def store(source, at, side):
        pltpu.make_async_copy(source, out_ref.at[at, side], sem).start()

    for at in ((0, 16, 1), (5, 6, 0), (7, 8, 0), (9, 10, 0), (11, 12, 0), (13, 16, 0)):
        piece = pl.ds(at[0], at[1] - at[0])
        store(done.at[piece, at[2]], piece, at[2])

    def late(u, at, rows):
        v = stacked(tl[u].reshape(8 * (len(PAIRS) - EARLY), 256))
        v = [dot(whole(tl_ref, h, rows=slice(at, at + rows), columns=240), v) for h in (0, 1)]
        return jnp.where(lax.broadcasted_iota(jnp.int32, (rows, 256), 1) % 128 < 64, v[0], v[1])

    v = e2_ref[0:48, :] + late(0, 0, 48)
    l2 = wide_dot(jnp.concatenate([v[:, :128], v[:, 128:]], 0), zu_ref, 0).reshape(2, 6, 8, 128)
    v = e34_ref[...] + late(1, 48, 96)
    l3 = wide_dot(v[:64, :128], zu_ref, 1).reshape(8, 8, 128)
    l4 = wide_dot(v[64:, 128:], zu_ref, 2).reshape(4, 8, 128)
    for k, i in enumerate((0, 1, 2, 3, 4, 6, 8, 10, 12)):
        for r in range(4):
            v = done[i, 0, pl.ds(r, 8, 4), :]
            if i < 5 and r % 2 == 0:
                v = jnp.where(lane % 2 == 1, v, merge(i, r // 2, l2[r // 2, i], l3, l4))
            elif r == 0:
                v = merge(i, 0, v, l3, l4)
            even[k, pl.ds(r, 8, 4), :] = v
        if i == 4:
            store(even.at[pl.ds(0, 5)], pl.ds(0, 5), 0)
        elif i > 4:
            store(even.at[k], i, 0)
    pltpu.make_async_copy(done, out_ref, sem).wait()


def solution(mesh):
    nx, ny = mesh.shape["gx"], mesh.shape["gy"]
    weights, (zp, fy, z1, ty, te, tl, zu) = operators()
    vmem, hbm = pl.BlockSpec(memory_space=pltpu.VMEM), pl.BlockSpec(memory_space=pltpu.HBM)
    limit = 24 * 1024 * 1024
    block, pairs = (32, 32, 128), (16, 2, 32, 128)

    def kept(*ms):
        return [pltpu.with_memory_space_constraint(jnp.asarray(m), pltpu.HBM) for m in ms]

    def local(v):
        parts = pl.pallas_call(
            functools.partial(exchange, nx, ny, 8, weights.tolist()),
            out_shape=[*(pltpu.VMEM(s, F32) for s in (pairs, (2, len(PAIRS) - EARLY, 8, 256), (128, 256), (96, 256))),
                       *(pltpu.VMEM(m.shape, BF16) for m in (tl, zu))],
            in_specs=[hbm] * 8, out_specs=[vmem] * 6,
            scratch_shapes=[pltpu.VMEM(block, F32), *([pltpu.VMEM((ENTRIES, ROWS, 128), F32)] * 2), pltpu.VMEM((36, 4, 8, 128), F32), *(pltpu.VMEM(m.shape, BF16) for m in (zp, fy, z1, ty, te)),
                            pltpu.VMEM((2, EARLY, 8, 256), F32), pltpu.VMEM(block, F32), pltpu.VMEM((20, 4, 8, 128), F32), pltpu.VMEM((2, 32, 128), F32), pltpu.VMEM((16, 2, 8, 128), F32),
                            pltpu.VMEM((2, 80, 128), F32), pltpu.SemaphoreType.DMA, pltpu.SemaphoreType.DMA((COUNTERS,)), pltpu.SemaphoreType.REGULAR((2,)), pltpu.SemaphoreType.DMA((8,))],
            compiler_params=pltpu.CompilerParams(collective_id=0, has_side_effects=True, vmem_limit_bytes=limit),
        )(*kept(v, zp, fy, z1, ty, te, tl, zu))
        return pl.pallas_call(
            finish,
            out_shape=jax.ShapeDtypeStruct(pairs, F32),
            in_specs=[vmem] * 6, out_specs=pl.BlockSpec(memory_space=pl.ANY),
            scratch_shapes=[pltpu.VMEM((9, 32, 128), F32), pltpu.SemaphoreType.DMA],
            compiler_params=pltpu.CompilerParams(vmem_limit_bytes=limit),
        )(*parts).reshape(block)

    spec = P("gx", "gy", None)
    return jax.shard_map(local, mesh=mesh, in_specs=(spec,), out_specs=spec, check_vma=False)
```

```python
import functools

import jax
import jax.numpy as jnp
import ml_dtypes
import numpy as np
from jax import lax
from jax.experimental import pallas as pl
from jax.experimental.pallas import tpu as pltpu
from jax.sharding import PartitionSpec as P

LIFT_A, LIFT_B, LIFT_C, LIFT_D = -1.586134342, -0.05298011854, 0.8829110762, 0.4435068522
LIFT_K = 1.149604398
MESH = pl.DeviceIdType.MESH
F32, BF16 = jnp.float32, jnp.bfloat16

COUNT = {0: 20, 1: 8, 2: 2, -1: 8, -2: 2}
X_AT = {0: 0, 1: 18, 2: 24, -1: 25, -2: 31}
Y_AT = {0: 0, -1: 32, 1: 40, -2: 48, 2: 56}
ENTRIES, ROWS = 32, 64
PAIRS = [X_AT[o] + p for o, c in COUNT.items() for p in range(c // 2)]
LATE = (5, 7, 4)
EARLY = 15
Y_STATES = 10
X_STATES = {1: 22, -1: 29}
OFFSETS = (0, -1, 1, -2, 2)
GROUP = {dx: [(dx, dy) for dy in (-2, 2, -1, 1, 0) if (dx, dy) != (0, 0)] for dx in OFFSETS}


def pieces(dx, dy):
    if dx == 0:
        return [(False, (0, 18), (Y_AT[dy], 8))] if abs(dy) == 1 else [(False, (0, 10), (Y_AT[dy], 2))]
    if abs(dx) == 2:
        return [(False, (X_AT[dx], 1), (Y_AT[dy], 2 if abs(dy) == 2 else 4))]
    if dy == 0:
        return [(True, (X_STATES[dx], 2), (0, 32)), (False, (X_AT[dx], 4), (0, 20))]
    if abs(dy) == 1:
        return [(True, (X_STATES[dx], 1), (Y_AT[dy], 4)), (False, (X_AT[dx], 4), (Y_AT[dy], 7))]
    return [(False, (X_AT[dx], 2), (Y_AT[dy], 2))]


MOVES = [(dx, dy, *piece) for dx in OFFSETS for dx, dy in GROUP[dx] for piece in pieces(dx, dy)]


def counter(dx, is_states):
    return 0 if dx == 0 else 1 if dx > 0 else 2 if is_states else 3


COUNTERS = 4


def area(rows):
    return next((rows // r, r) for r in range(ROWS, 0, -1) if rows % r == 0 and rows // r <= ENTRIES)


def unsent():
    sent = {(e, r) for _, _, _, (e0, ne), (r0, nr) in MOVES for e in range(e0, e0 + ne) for r in range(r0, r0 + nr)}
    out = [(e, Y_AT[dy] + 4, 4) for e in X_STATES.values() for dy in (-1, 1)]
    for e in PAIRS:
        for tile in range(32 if e < X_AT[1] else 0, ROWS, 8):
            count = sum((e, r) in sent for r in range(tile, tile + 8))
            if count < 8 and tile != 24:
                out.append((e, tile + count, 8 - count))
    return out


def lift_1d(v):
    even, odd = v[0::2], v[1::2]
    odd = odd + LIFT_A * (even + np.roll(even, -1, 0))
    even = even + LIFT_B * (np.roll(odd, 1, 0) + odd)
    odd = odd + LIFT_C * (even + np.roll(even, -1, 0))
    even = even + LIFT_D * (np.roll(odd, 1, 0) + odd)
    return even / LIFT_K, odd * LIFT_K


def interleave(low, high):
    out = np.empty((2 * low.shape[0], low.shape[1]))
    out[0::2], out[1::2] = low, high
    return out


def row_space(parts, count):
    basis = np.zeros((0, parts[0].shape[1]))
    for part in parts:
        rest = part - part @ basis.T @ basis
        size, rows = np.linalg.svd(rest)[1:]
        basis = np.concatenate([basis, rows[:int((size > 1e-9).sum())]])
    return np.concatenate([basis, np.zeros((count - len(basis), basis.shape[1]))])


def thirds(matrix):
    out, rest = [], np.asarray(matrix, np.float64)
    for _ in range(3):
        out.append(rest.astype(ml_dtypes.bfloat16))
        rest = rest - out[-1].astype(np.float64)
    return out


def operators():
    n, blocks, mid = 32, 16, 8
    low, levels = np.eye(n * blocks), {}
    for level in range(1, 5):
        low, high = lift_1d(low)
        m = n >> level
        levels[level] = interleave(low[mid * m:(mid + 1) * m], high[mid * m:(mid + 1) * m])
    functional, combine = {}, {}
    for offset, count in COUNT.items():
        parts = [levels[level][:, (mid + offset) * n:(mid + offset + 1) * n] for level in (4, 3, 2)]
        functional[offset] = row_space(parts, count)
        combine[offset] = np.concatenate(parts[::-1])
    basis = np.stack(own_basis(np.eye(n)))
    inverse = np.linalg.pinv(basis)
    weights = np.concatenate([functional[o] @ inverse for o in COUNT if o])
    cx = [np.concatenate([(combine[o] @ (functional[o].T if o else inverse))[:, h::2] for o in COUNT], 1) for h in (0, 1)]
    late = [[[tuple(c[at + i, p] for c in cx) for p in range(EARLY, len(PAIRS))] for i in range(count)] for at, count in zip((0, 16, 24), LATE)]
    assert all(np.abs(c[at + count:end, EARLY:]).max(initial=0) < 1e-12 for c in cx for at, count, end in zip((0, 16, 24), LATE, (16, 24, 28)))
    early = np.stack([np.kron(c[:, :EARLY], np.eye(8)) for c in cx])
    high, mid_, low = thirds(early)
    early = np.stack([np.concatenate(m, 2) for m in ((high, high), (mid_, mid_), (low, high))])
    fy, cy = np.zeros((ROWS, 32)), np.zeros((28, ROWS))
    for offset, count in COUNT.items():
        at = Y_AT[offset]
        fy[at:at + count], cy[:, at:at + count] = functional[offset], combine[offset] @ functional[offset].T
    ty = np.zeros((32, ROWS))
    ty[0:8], ty[8:16], ty[16:24], ty[24:32:2] = cy[0:16:2], cy[1:16:2], cy[16:24], cy[24:28]
    high, mid_, low = thirds(fy)
    fy = np.concatenate([high, high, high, mid_, mid_, low], 1)
    high, mid_, low = thirds(ty)
    ty = np.stack([np.concatenate(m, 1) for m in ((high, high, high), (mid_, mid_, low))])
    low, high = lift_1d(np.eye(128))
    z1 = wide(interleave(low, high).T)
    zp = np.concatenate(thirds(np.kron(np.eye(2), low.T)), 1)
    low, zu = np.eye(64), np.zeros((3, 64, 128))
    for level in range(3):
        low, high = lift_1d(low)
        zu[level, :, ::2 << level] = interleave(low, high).T
    zu = np.stack([wide(np.concatenate([m, m])) for m in zu])
    return weights, late, [tiles(m) for m in (zp, fy, z1, ty, early, zu)]


def wide(matrix):
    high, mid, low = thirds(matrix)
    return np.concatenate([np.concatenate(m) for m in ((high, high), (mid, mid), (low, high))], 1)


def tiles(matrix):
    columns = -(-matrix.shape[-1] // 128) * 128
    padded = np.zeros((*matrix.shape[:-1], columns), matrix.dtype)
    padded[..., :matrix.shape[-1]] = matrix
    return np.moveaxis(padded.reshape(*matrix.shape[:-1], columns // 128, 128), -2, -3)


def whole(ref, *at, rows=slice(None), columns=None):
    count = ref.shape[len(at)]
    out = ref[(*at, 0, rows)] if count == 1 else jnp.concatenate([ref[(*at, i, rows)] for i in range(count)], 1)
    return out if columns is None else out[:, :columns]


def dot(a, b):
    return lax.dot_general(a, b, (((1,), (0,)), ((), ())), preferred_element_type=F32)


def split(v):
    high = v.astype(BF16)
    rest = v - high.astype(F32)
    mid = rest.astype(BF16)
    return high, mid, (rest - mid.astype(F32)).astype(BF16)


def stacked(v):
    high, mid, low = split(v)
    return jnp.concatenate([high, mid, low, high, mid, high], 0)


def wide_dot(v, ref, *at):
    high, mid, low = split(v)
    m = whole(ref, *at)
    n = m.shape[1] // 3
    v = dot(jnp.concatenate([high, mid], 1), m[:, :2 * n])
    return dot(jnp.concatenate([high, low], 1), m[:, 2 * n:]) + v[:, n:] + v[:, :n]


def states(s, side):
    if side < 0:
        return s(31) + LIFT_A * s(30), s(30) + LIFT_B * (s(29) + LIFT_A * (s(28) + s(30)))
    return s(0), s(0) + LIFT_B * (s(1) + LIFT_A * (s(0) + s(2)))


def own_basis(v):
    out, odd, even, odd3 = [], 0.0, 0.0, 0.0
    for i in range(17):
        if i < 16:
            after = v[2 * i + 2] if i < 15 else 0.0
            odd_now = v[2 * i + 1] + LIFT_A * (v[2 * i] + after)
            even_now = v[2 * i] + LIFT_B * (odd + odd_now)
        else:
            odd_now, even_now = None, LIFT_B * odd
        if i > 0:
            odd3_now = odd + LIFT_C * (even + even_now)
            out.append(even + LIFT_D * (odd3 + odd3_now))
            odd3 = odd3_now
        odd, even = odd_now, even_now
    return [*out, *states(lambda i: v[i], -1), *states(lambda i: v[i], 1)]


def prepare_states(dx, v_ref, vo_ref, xh):
    e = X_STATES[dx]
    for q, plane in enumerate(states(lambda x: v_ref[x], dx)):
        xh[q] = plane
        vo_ref[e + q, 0:32, :] = plane
    for dy in (-1, 1):
        at = Y_AT[dy]
        for p, rows in enumerate(states(lambda y: xh[:, y, :], dy)):
            vo_ref[e, at + 2 * p:at + 2 * p + 2, :] = rows
        vo_ref[e, at + 4:at + 8, :] = jnp.zeros((4, 128), F32)


def functional(f, values, weights):
    if f < 20:
        return values[f]
    terms = [w * value for w, value in zip(weights[f - 20], values) if abs(w) > 1e-14]
    while len(terms) > 1:
        terms = [sum(terms[k:k + 2][1:], terms[k]) for k in range(0, len(terms), 2)]
    return terms[0] if terms else jnp.zeros((8, 128), F32)


def prepare_pairs(first, sides, zp_ref, fy_ref, vo_ref):
    high, mid, low = split(jnp.concatenate(sides, 1))
    m = whole(zp_ref)
    packed = dot(high, m[:, :256]) + dot(mid, m[:, :256])
    packed = dot(low, m[:, :128]) + dot(high, m[:, 256:]) + packed[:, 128:] + packed[:, :128]
    count = packed.shape[0] // 32
    columns = [stacked(packed[32 * i:32 * i + 32]) for i in range(count)]
    for i in range(0, count, 2):
        rows = dot(whole(fy_ref, columns=192), jnp.concatenate(columns[i:i + 2], 1))
        for j in range(min(2, count - i)):
            vo_ref[PAIRS[first + i + j]] = rows[:, 128 * j:128 * j + 128]


def prepare_rows(vo_ref, zt):
    for dy in (-1, 1):
        for q, rows in enumerate(states(lambda y: zt[:, y, :], dy)):
            for t in range(4):
                vo_ref[Y_STATES + 4 * q + t, Y_AT[dy]:Y_AT[dy] + 8, :] = rows[8 * t:8 * t + 8]


def split_y(p, halo, first, last):
    a, b, c, d = halo
    p0, p1, p2, p3 = p

    def following(v, edge):
        return jnp.where(last, edge, pltpu.roll(v, 7, 0))

    def preceding(v, edge):
        return jnp.where(first, edge, pltpu.roll(v, 1, 0))

    o0 = p1 + LIFT_A * (p0 + p2)
    o1 = p3 + LIFT_A * (p2 + following(p0, c))
    before = a + LIFT_A * p0
    e0 = p0 + LIFT_B * (preceding(o1, before) + o0)
    e1 = p2 + LIFT_B * (o0 + o1)
    q0 = o0 + LIFT_C * (e0 + e1)
    q1 = o1 + LIFT_C * (e1 + following(e0, d + LIFT_B * o1))
    before = before + LIFT_C * (b + LIFT_B * before + e0)
    f0 = e0 + LIFT_D * (preceding(q1, before) + q0)
    f1 = e1 + LIFT_D * (q0 + q1)
    return f0 * (1 / LIFT_K), q0 * LIFT_K, f1 * (1 / LIFT_K), q1 * LIFT_K


def exchange(nx, ny, nz, weights, late, v_hbm, zp_hbm, fy_hbm, z1_hbm, ty_hbm, te_hbm, zu_hbm, done,
             v_ref, vo_ref, vi_ref, ys_ref, zp_ref, fy_ref, z1_ref, ty_ref, te_ref, zu_ref, te_in, tl_in, e2_ref, e34_ref,
             zt, basis, sides, xh, up, xz, send, recv, hello, sems):
    x, y = lax.axis_index("gx"), lax.axis_index("gy")
    z = lax.rem(x, nz)

    def device(dx, dy):
        return lax.rem(x + dx + nx, nx), lax.rem(y + dy + ny, ny)

    copies, arriving = [], [0] * COUNTERS
    for dx, dy, is_states, (e, ne), (r, nr) in MOVES:
        at, k = (pl.ds(e, ne), pl.ds(r, nr)), counter(dx, is_states)
        arriving[k] += ne * nr
        copies.append((dx, dy, is_states, pltpu.make_async_remote_copy(
            src_ref=vo_ref.at[at], dst_ref=vi_ref.at[at], send_sem=send, recv_sem=recv.at[k],
            device_id=device(-dx, -dy), device_id_type=MESH)))

    def wait_rows(sem, rows):
        n, r = area(rows)
        some = vi_ref.at[pl.ds(0, n), pl.ds(0, r)]
        pltpu.make_async_copy(some, some, sem).wait()

    def start(which, kinds=(True, False)):
        for dx, _, is_states, copy in copies:
            if dx == which and is_states in kinds:
                copy.start()

    def start_ahead(kinds, waits):
        for dx, dy, is_states, copy in copies:
            if dx == -1 and is_states in kinds:
                if dy in (0, 1):
                    pl.when(((x == nx - 1) & (y == dy)) == waits)(copy.start)
                elif not waits:
                    copy.start()

    def arrive(k):
        wait_rows(recv.at[k], arriving[k])

    barrier = pltpu.get_barrier_semaphore()

    def greet(dx):
        for o in GROUP[dx]:
            pl.semaphore_signal(barrier, inc=1, device_id=device(*o), device_id_type=MESH)

    def say_hello(dx, dys):
        for dy in dys:
            pl.semaphore_signal(hello.at[dx - 1], inc=1, device_id=device(dx, dy), device_id_type=MESH)

    loads = [pltpu.make_async_copy(a, b, sems.at[i]) for i, (a, b) in enumerate(
        (*((v_hbm.at[:, pl.ds(8 * t, 8)], v_ref.at[:, pl.ds(8 * t, 8)]) for t in range(4)),
         (zp_hbm, zp_ref), (fy_hbm, fy_ref), (z1_hbm, z1_ref), (ty_hbm, ty_ref), (te_hbm, te_ref), (zu_hbm, zu_ref)))]
    for load in loads[:4]:
        load.start()
    pl.when(z != nz - 1)(lambda: greet(-1))
    greet(-2)
    loads[4].start()
    loads[5].start()

    @pl.when(z >= nz - 2)
    def _():
        pl.semaphore_wait(barrier, jnp.where(z == nz - 2, 5, 10))
        pl.when(z == nz - 1)(lambda: say_hello(1, range(-2, 3)))
        say_hello(2, range(-2, 3))

    @pl.when(z < nz - 2)
    def _():
        greet(0)
        pl.when(z < nz - 3)(lambda: greet(1))
        pl.when(z < nz - 4)(lambda: greet(2))

    for e, r, count in unsent():
        vi_ref[e, r:r + count, :] = jnp.zeros((count, 128), F32)
    for t in range(4):
        loads[t].wait()
        values = own_basis([v_ref[x, 8 * t:8 * t + 8, :] for x in range(32)])
        for i, value in enumerate(values):
            basis[i, t] = value
        for i in range(EARLY, len(PAIRS)):
            for h in (0, 1):
                sides[h, 4 * (i - EARLY) + t] = functional(2 * i + h, values, weights)
    prepare_states(-1, v_ref, vo_ref, xh)
    pl.when(z == nz - 1)(lambda: start_ahead((True,), False))
    loads[4].wait()
    loads[5].wait()
    prepare_pairs(EARLY, [sides[h].reshape(32 * (len(PAIRS) - EARLY), 128) for h in (0, 1)], zp_ref, fy_ref, vo_ref)

    @pl.when(z >= nz - 2)
    def _():
        start(-2)
        pl.when(z == nz - 1)(lambda: start_ahead((False,), False))

    for load in loads[6:]:
        load.start()
    prepare_states(1, v_ref, vo_ref, xh)
    early = [[functional(2 * i + h, [basis[k, t] for k in range(20)], weights) for i in range(EARLY) for t in range(4)] for h in (0, 1)]
    prepare_pairs(0, [jnp.concatenate(side, 0) for side in early], zp_ref, fy_ref, vo_ref)
    loads[6].wait()
    for t in range(4):
        zt[:, 8 * t:8 * t + 8, :] = wide_dot(v_ref[:, 8 * t:8 * t + 8, :].reshape(256, 128), z1_ref).reshape(32, 8, 128)
    prepare_rows(vo_ref, zt)

    @pl.when(z < nz - 2)
    def _():
        pl.semaphore_wait(barrier, jnp.where(z == 0, 14, jnp.where(z == 1, 19, 24)))

        @pl.when(z == nz - 3)
        def _():
            say_hello(1, (0,))
            say_hello(2, (0,))

        start(-2)
        pl.when(z > 1)(lambda: start(2))
        start(-1)
        pl.when(z > 0)(lambda: start(1))
        start(0)

    @pl.when(z == nz - 2)
    def _():
        pl.semaphore_wait(hello.at[0], 1)
        start(-1)

    @pl.when(z == nz - 1)
    def _():
        pl.semaphore_wait(hello.at[1], 1)
        start_ahead((True, False), True)

    @pl.when(z >= nz - 2)
    def _():
        start(2)
        start(1)
        start(0)

    sub = lax.broadcasted_iota(jnp.int32, (8, 128), 0)
    first, last = sub == 0, sub == 7

    def row(ref, e, r):
        return jnp.broadcast_to(ref[e, pl.ds(r, 1), :], (8, 128))

    def plane(x):
        p = [zt[x, pl.ds(r, 8, 4), :] for r in range(4)]
        halo = [row(vi_ref, Y_STATES + 4 * (k % 2) + x // 8, Y_AT[-1 if k < 2 else 1] + x % 8) for k in range(4)]
        for r, v in enumerate(split_y(p, halo, first, last)):
            ys_ref[x + 2, r] = v

    def state_planes(dx):
        e, side = X_STATES[dx], (dx + 1) // 2
        xz[side] = wide_dot(jnp.concatenate([vi_ref[e, 0:32, :], vi_ref[e + 1, 0:32, :], vi_ref[e, 32:48, :]], 0), z1_ref)
        for q in (0, 1):
            p = [xz[side, pl.ds(32 * q + r, 8, 4), :] for r in range(4)]
            halo = [row(xz, side, 64 + 8 * (k // 2) + 2 * (k % 2) + q) for k in range(4)]
            for r, v in enumerate(split_y(p, halo, first, last)):
                ys_ref[34 * side + q, r] = v

    def upper(first_pair, count, out_ref):
        done = []
        for i in range(first_pair, first_pair + count):
            e = PAIRS[i]
            v = vi_ref[e]
            own = vo_ref[e, 0:32, :] if i < COUNT[0] // 2 else jnp.concatenate([v[0:24], jnp.zeros((8, 128), F32)], 0)
            done.append(jnp.concatenate([own, v[32:]], 0))
        for i in range(0, count, 2):
            high, mid, low = split(jnp.concatenate(done[i:i + 2], 1))
            r = (dot(whole(ty_ref, 1, columns=192), jnp.concatenate([high, mid, high], 0))
                 + dot(whole(ty_ref, 0, columns=192), jnp.concatenate([high, mid, low], 0)))
            for j in range(min(2, count - i)):
                for t in range(4):
                    out_ref[t // 2, first_pair % EARLY + i + j, :, 128 * (t % 2):128 * (t % 2) + 128] = r[8 * t:8 * t + 8, 128 * j:128 * j + 128]

    loads[7].wait()
    arrive(0)
    for x in range(32):
        plane(x)
    upper(0, 10, te_in)

    arrive(1)
    state_planes(1)
    upper(10, 5, te_in)
    loads[8].wait()
    for u, (ref, at, rows) in enumerate(((e2_ref, 0, 128), (e34_ref, 128, 96))):
        high, mid, low = split(te_in[u].reshape(8 * EARLY, 256))
        high_mid, high_low = [jnp.concatenate([high, w], 0) for w in (mid, low)]
        m = [[whole(te_ref, k, h, rows=slice(at, at + rows), columns=240) for k in range(3)] for h in (0, 1)]
        v = [dot(m[h][2], high_low) + dot(m[h][1], high_mid) + dot(m[h][0], high_mid) for h in (0, 1)]
        ref[...] = jnp.where(lax.broadcasted_iota(jnp.int32, (rows, 256), 1) % 128 < 64, v[0], v[1])

    loads[9].wait()
    l2 = wide_dot(jnp.concatenate([e2_ref[:, :128], e2_ref[:, 128:]], 0), zu_ref, 0).reshape(2, 16, 8, 128)
    l3 = wide_dot(e34_ref[:64, :128], zu_ref, 1).reshape(8, 8, 128)
    l4 = wide_dot(e34_ref[64:, 128:], zu_ref, 2).reshape(4, 8, 128)
    for i in range(2, 16):
        for t in (0, 1):
            up[i, t] = merge(i, t, l2[t, i], l3, l4)
    lift_x(ys_ref, up, done)

    @pl.when(z < 2)
    def _():
        pl.semaphore_wait(hello.at[1], 5)
        start(2)

    @pl.when(z == 0)
    def _():
        pl.semaphore_wait(hello.at[0], 5)
        start(1)

    arrive(2)
    state_planes(-1)
    first_x(ys_ref, done)
    arrive(3)
    upper(15, 5, tl_in)

    half = lax.broadcasted_iota(jnp.int32, (8, 128), 1) < 64

    def changed(level, u, lanes, early):
        rows = []
        for i, pairs in enumerate(late[level]):
            terms = [jnp.where(half, *pair) * tl_in[u, p, :, lanes:lanes + 128] for p, pair in enumerate(pairs) if max(map(abs, pair)) > 1e-14]
            while len(terms) > 1:
                terms = [sum(terms[k:k + 2][1:], terms[k]) for k in range(0, len(terms), 2)]
            rows.append(early(8 * i) + terms[0])
        return rows

    l2 = [changed(0, 0, 128 * t, lambda r: e2_ref[r:r + 8, 128 * t:128 * t + 128]) for t in (0, 1)]
    l2 = wide_dot(jnp.concatenate(l2[0] + l2[1], 0), zu_ref, 0).reshape(2, LATE[0], 8, 128)
    l3 = wide_dot(jnp.concatenate(changed(1, 1, 0, lambda r: e34_ref[r:r + 8, :128]), 0), zu_ref, 1).reshape(LATE[1], 8, 128)
    l4 = wide_dot(jnp.concatenate(changed(2, 1, 128, lambda r: e34_ref[64 + r:72 + r, 128:]), 0), zu_ref, 2).reshape(LATE[2], 8, 128)
    odd_lane = lax.broadcasted_iota(jnp.int32, (8, 128), 1) % 2 == 1
    for i in range(2 * LATE[1]):
        for t in (0, 1):
            at = (i, 0, pl.ds(2 * t, 8, 4), slice(None))
            if i < LATE[0]:
                done[at] = jnp.where(odd_lane, done[at], merge(i, t, l2[t, i], l3, l4))
            elif i % 2 == 0 and t == 0:
                done[at] = merge(i, t, done[at], l3, l4)
    wait_rows(send, sum(arriving))


def merge(i, t, v, l3, l4):
    sub = lax.broadcasted_iota(jnp.int32, (8, 128), 0)
    lane = lax.broadcasted_iota(jnp.int32, (8, 128), 1)
    if i % 2 or t:
        return v
    w = l3[i // 2]
    if i % 4 == 0:
        w = jnp.where((lane % 8 == 0) & (sub % 2 == 0), l4[i // 4], w)
    return jnp.where(lane % 4 == 0, w, v)


def lift_x(ys, up, done):
    odd_lane = lax.broadcasted_iota(jnp.int32, (8, 128), 1) % 2 == 1
    state = {}
    for r in range(4):
        state[r] = (ys[3, r] + LIFT_A * (ys[2, r] + ys[4, r]), None, None)
    for i in range(1, 17):
        for r in range(4):
            o, e, q = state[r]
            if i < 16:
                p = ys[2 + 2 * i, r]
                o_now = ys[3 + 2 * i, r] + LIFT_A * (p + ys[4 + 2 * i, r])
                e_now = p + LIFT_B * (o + o_now)
            else:
                o_now, e_now = None, ys[35, r] + LIFT_B * o
            q_now = None
            if i > 1:
                q_now = o + LIFT_C * (e + e_now)
                done[i - 1, 1, pl.ds(r, 8, 4), :] = q_now * LIFT_K
            if i > 2:
                low = (e + LIFT_D * (q + q_now)) * (1 / LIFT_K)
                done[i - 1, 0, pl.ds(r, 8, 4), :] = low if r % 2 else jnp.where(odd_lane, low, up[i - 1, r // 2])
            state[r] = (o_now, e_now, q_now)


def first_x(ys, done):
    for r in range(4):
        o = [ys[0, r] + LIFT_A * ys[2, r], *(ys[3 + 2 * i, r] + LIFT_A * (ys[2 + 2 * i, r] + ys[4 + 2 * i, r]) for i in range(3))]
        e = [ys[1, r] + LIFT_B * o[0], *(ys[2 + 2 * i, r] + LIFT_B * (o[i] + o[i + 1]) for i in range(3))]
        q = [o[i] + LIFT_C * (e[i] + e[i + 1]) for i in range(3)]
        for i in range(2):
            done[i, 0, pl.ds(r, 8, 4), :] = (e[i + 1] + LIFT_D * (q[i] + q[i + 1])) * (1 / LIFT_K)
        done[0, 1, pl.ds(r, 8, 4), :] = q[1] * LIFT_K


def finish(done, out_ref, sem):
    for i in range(0, 16, 4):
        pltpu.make_async_copy(done.at[pl.ds(i, 4)], out_ref.at[pl.ds(i, 4)], sem).start()
    pltpu.make_async_copy(done, out_ref, sem).wait()


def solution(mesh):
    nx, ny = mesh.shape["gx"], mesh.shape["gy"]
    weights, late, (zp, fy, z1, ty, te, zu) = operators()
    vmem, hbm = pl.BlockSpec(memory_space=pltpu.VMEM), pl.BlockSpec(memory_space=pltpu.HBM)
    limit = 24 * 1024 * 1024
    block, pairs = (32, 32, 128), (16, 2, 32, 128)

    def kept(*ms):
        return [pltpu.with_memory_space_constraint(jnp.asarray(m), pltpu.HBM) for m in ms]

    def local(v):
        done = pl.pallas_call(
            functools.partial(exchange, nx, ny, 8, weights.tolist(), late),
            out_shape=pltpu.VMEM(pairs, F32),
            in_specs=[hbm] * 7, out_specs=vmem,
            scratch_shapes=[*(pltpu.VMEM(s, F32) for s in (block, (ENTRIES, ROWS, 128), (ENTRIES, ROWS, 128), (36, 4, 8, 128))),
                            *(pltpu.VMEM(m.shape, BF16) for m in (zp, fy, z1, ty, te, zu)),
                            *(pltpu.VMEM(s, F32) for s in ((2, EARLY, 8, 256), (2, len(PAIRS) - EARLY, 8, 256), (128, 256), (96, 256),
                                                           block, (20, 4, 8, 128), (2, 4 * (len(PAIRS) - EARLY), 8, 128), (2, 32, 128), (16, 2, 8, 128), (2, 80, 128))),
                            pltpu.SemaphoreType.DMA, pltpu.SemaphoreType.DMA((COUNTERS,)), pltpu.SemaphoreType.REGULAR((2,)), pltpu.SemaphoreType.DMA((10,))],
            compiler_params=pltpu.CompilerParams(collective_id=0, has_side_effects=True, vmem_limit_bytes=limit),
        )(*kept(v, zp, fy, z1, ty, te, zu))
        return pl.pallas_call(
            finish,
            out_shape=jax.ShapeDtypeStruct(pairs, F32),
            in_specs=[vmem], out_specs=pl.BlockSpec(memory_space=pl.ANY),
            scratch_shapes=[pltpu.SemaphoreType.DMA],
            compiler_params=pltpu.CompilerParams(vmem_limit_bytes=limit),
        )(done).reshape(block)

    spec = P("gx", "gy", None)
    return jax.shard_map(local, mesh=mesh, in_specs=(spec,), out_specs=spec, check_vma=False)
```

```python
import functools

import jax
import jax.numpy as jnp
import ml_dtypes
import numpy as np
from jax import lax
from jax.experimental import pallas as pl
from jax.experimental.pallas import tpu as pltpu
from jax.sharding import PartitionSpec as P

LIFT_A, LIFT_B, LIFT_C, LIFT_D = -1.586134342, -0.05298011854, 0.8829110762, 0.4435068522
LIFT_K = 1.149604398
MESH = pl.DeviceIdType.MESH
F32, BF16 = jnp.float32, jnp.bfloat16

COUNT = {0: 20, 1: 8, 2: 2, -1: 8, -2: 2}
X_AT = {0: 0, 1: 18, 2: 24, -1: 25, -2: 31}
Y_AT = {0: 0, -1: 32, 1: 40, -2: 48, 2: 56}
ENTRIES, ROWS = 32, 64
PAIRS = [X_AT[o] + p for o, c in COUNT.items() for p in range(c // 2)]
LATE = (5, 7, 4)
EARLY = 15
Y_STATES = 10
X_STATES = {1: 22, -1: 29}
OFFSETS = (0, -1, 1, -2, 2)
GROUP = {dx: [(dx, dy) for dy in (-2, 2, -1, 1, 0) if (dx, dy) != (0, 0)] for dx in OFFSETS}


def pieces(dx, dy):
    if dx == 0:
        return [(False, (0, 18), (Y_AT[dy], 8))] if abs(dy) == 1 else [(False, (0, 10), (Y_AT[dy], 2))]
    if abs(dx) == 2:
        return [(False, (X_AT[dx], 1), (Y_AT[dy], 2 if abs(dy) == 2 else 4))]
    if dy == 0:
        return [(True, (X_STATES[dx], 2), (0, 32)), (False, (X_AT[dx], 4), (0, 20))]
    if abs(dy) == 1:
        return [(True, (X_STATES[dx], 1), (Y_AT[dy], 4)), (False, (X_AT[dx], 4), (Y_AT[dy], 7))]
    return [(False, (X_AT[dx], 2), (Y_AT[dy], 2))]


MOVES = [(dx, dy, *piece) for dx in OFFSETS for dx, dy in GROUP[dx] for piece in pieces(dx, dy)]


def counter(dx, is_states):
    return 0 if dx == 0 else 1 if dx > 0 else 2 if is_states else 3


COUNTERS = 4


def area(rows):
    return next((rows // r, r) for r in range(ROWS, 0, -1) if rows % r == 0 and rows // r <= ENTRIES)


def unsent():
    sent = {(e, r) for _, _, _, (e0, ne), (r0, nr) in MOVES for e in range(e0, e0 + ne) for r in range(r0, r0 + nr)}
    out = [(e, Y_AT[dy] + 4, 4) for e in X_STATES.values() for dy in (-1, 1)]
    for e in PAIRS:
        for tile in range(32 if e < X_AT[1] else 0, ROWS, 8):
            count = sum((e, r) in sent for r in range(tile, tile + 8))
            if count < 8 and tile != 24:
                out.append((e, tile + count, 8 - count))
    return out


def lift_1d(v):
    even, odd = v[0::2], v[1::2]
    odd = odd + LIFT_A * (even + np.roll(even, -1, 0))
    even = even + LIFT_B * (np.roll(odd, 1, 0) + odd)
    odd = odd + LIFT_C * (even + np.roll(even, -1, 0))
    even = even + LIFT_D * (np.roll(odd, 1, 0) + odd)
    return even / LIFT_K, odd * LIFT_K


def interleave(low, high):
    out = np.empty((2 * low.shape[0], low.shape[1]))
    out[0::2], out[1::2] = low, high
    return out


def row_space(parts, count):
    basis = np.zeros((0, parts[0].shape[1]))
    for part in parts:
        rest = part - part @ basis.T @ basis
        size, rows = np.linalg.svd(rest)[1:]
        basis = np.concatenate([basis, rows[:int((size > 1e-9).sum())]])
    return np.concatenate([basis, np.zeros((count - len(basis), basis.shape[1]))])


def thirds(matrix):
    out, rest = [], np.asarray(matrix, np.float64)
    for _ in range(3):
        out.append(rest.astype(ml_dtypes.bfloat16))
        rest = rest - out[-1].astype(np.float64)
    return out


def operators():
    n, blocks, mid = 32, 16, 8
    low, levels = np.eye(n * blocks), {}
    for level in range(1, 5):
        low, high = lift_1d(low)
        m = n >> level
        levels[level] = interleave(low[mid * m:(mid + 1) * m], high[mid * m:(mid + 1) * m])
    functional, combine = {}, {}
    for offset, count in COUNT.items():
        parts = [levels[level][:, (mid + offset) * n:(mid + offset + 1) * n] for level in (4, 3, 2)]
        functional[offset] = row_space(parts, count)
        combine[offset] = np.concatenate(parts[::-1])
    basis = np.stack(own_basis(np.eye(n)))
    inverse = np.linalg.pinv(basis)
    weights = np.concatenate([functional[o] @ inverse for o in COUNT if o])
    cx = [np.concatenate([(combine[o] @ (functional[o].T if o else inverse))[:, h::2] for o in COUNT], 1) for h in (0, 1)]
    late = [[[tuple(c[at + i, p] for c in cx) for p in range(EARLY, len(PAIRS))] for i in range(count)] for at, count in zip((0, 16, 24), LATE)]
    assert all(np.abs(c[at + count:end, EARLY:]).max(initial=0) < 1e-12 for c in cx for at, count, end in zip((0, 16, 24), LATE, (16, 24, 28)))
    early = np.stack([np.kron(c[:, :EARLY], np.eye(8)) for c in cx])
    high, mid_, low = thirds(early)
    early = np.stack([np.concatenate(m, 2) for m in ((high, high), (mid_, mid_), (low, high))])
    fy, cy = np.zeros((ROWS, 32)), np.zeros((28, ROWS))
    for offset, count in COUNT.items():
        at = Y_AT[offset]
        fy[at:at + count], cy[:, at:at + count] = functional[offset], combine[offset] @ functional[offset].T
    ty = np.zeros((32, ROWS))
    ty[0:8], ty[8:16], ty[16:24], ty[24:32:2] = cy[0:16:2], cy[1:16:2], cy[16:24], cy[24:28]
    high, mid_, low = thirds(fy)
    fy = np.concatenate([high, high, high, mid_, mid_, low], 1)
    high, mid_, low = thirds(ty)
    ty = np.stack([np.concatenate(m, 1) for m in ((high, high, high), (mid_, mid_, low))])
    low, high = lift_1d(np.eye(128))
    z1 = wide(interleave(low, high).T)
    zp = np.concatenate(thirds(np.kron(np.eye(2), low.T)), 1)
    low, zu = np.eye(64), np.zeros((3, 64, 128))
    for level in range(3):
        low, high = lift_1d(low)
        zu[level, :, ::2 << level] = interleave(low, high).T
    zu = np.stack([wide(np.concatenate([m, m])) for m in zu])
    return weights, late, [tiles(m) for m in (zp, fy, z1, ty, early, zu)]


def wide(matrix):
    high, mid, low = thirds(matrix)
    return np.concatenate([np.concatenate(m) for m in ((high, high), (mid, mid), (low, high))], 1)


def tiles(matrix):
    columns = -(-matrix.shape[-1] // 128) * 128
    padded = np.zeros((*matrix.shape[:-1], columns), matrix.dtype)
    padded[..., :matrix.shape[-1]] = matrix
    return np.moveaxis(padded.reshape(*matrix.shape[:-1], columns // 128, 128), -2, -3)


def whole(ref, *at, rows=slice(None), columns=None):
    count = ref.shape[len(at)]
    out = ref[(*at, 0, rows)] if count == 1 else jnp.concatenate([ref[(*at, i, rows)] for i in range(count)], 1)
    return out if columns is None else out[:, :columns]


def dot(a, b):
    return lax.dot_general(a, b, (((1,), (0,)), ((), ())), preferred_element_type=F32)


def split(v):
    high = v.astype(BF16)
    rest = v - high.astype(F32)
    mid = rest.astype(BF16)
    return high, mid, (rest - mid.astype(F32)).astype(BF16)


def stacked(v):
    high, mid, low = split(v)
    return jnp.concatenate([high, mid, low, high, mid, high], 0)


def wide_dot(v, ref, *at):
    high, mid, low = split(v)
    m = whole(ref, *at)
    n = m.shape[1] // 3
    v = dot(jnp.concatenate([high, mid], 1), m[:, :2 * n])
    return dot(jnp.concatenate([high, low], 1), m[:, 2 * n:]) + v[:, n:] + v[:, :n]


def states(s, side):
    if side < 0:
        return s(31) + LIFT_A * s(30), s(30) + LIFT_B * (s(29) + LIFT_A * (s(28) + s(30)))
    return s(0), s(0) + LIFT_B * (s(1) + LIFT_A * (s(0) + s(2)))


def own_basis(v):
    out, odd, even, odd3 = [], 0.0, 0.0, 0.0
    for i in range(17):
        if i < 16:
            after = v[2 * i + 2] if i < 15 else 0.0
            odd_now = v[2 * i + 1] + LIFT_A * (v[2 * i] + after)
            even_now = v[2 * i] + LIFT_B * (odd + odd_now)
        else:
            odd_now, even_now = None, LIFT_B * odd
        if i > 0:
            odd3_now = odd + LIFT_C * (even + even_now)
            out.append(even + LIFT_D * (odd3 + odd3_now))
            odd3 = odd3_now
        odd, even = odd_now, even_now
    return [*out, *states(lambda i: v[i], -1), *states(lambda i: v[i], 1)]


def prepare_states(dx, v_ref, vo_ref, xh):
    e = X_STATES[dx]
    for q, plane in enumerate(states(lambda x: v_ref[x], dx)):
        xh[q] = plane
        vo_ref[e + q, 0:32, :] = plane
    for dy in (-1, 1):
        at = Y_AT[dy]
        for p, rows in enumerate(states(lambda y: xh[:, y, :], dy)):
            vo_ref[e, at + 2 * p:at + 2 * p + 2, :] = rows
        vo_ref[e, at + 4:at + 8, :] = jnp.zeros((4, 128), F32)


def functional(f, values, weights):
    if f < 20:
        return values[f]
    terms = [w * value for w, value in zip(weights[f - 20], values) if abs(w) > 1e-14]
    while len(terms) > 1:
        terms = [sum(terms[k:k + 2][1:], terms[k]) for k in range(0, len(terms), 2)]
    return terms[0] if terms else jnp.zeros((8, 128), F32)


def prepare_pairs(first, sides, zp_ref, fy_ref, vo_ref):
    high, mid, low = split(jnp.concatenate(sides, 1))
    m = whole(zp_ref)
    packed = dot(high, m[:, :256]) + dot(mid, m[:, :256])
    packed = dot(low, m[:, :128]) + dot(high, m[:, 256:]) + packed[:, 128:] + packed[:, :128]
    count = packed.shape[0] // 32
    columns = [stacked(packed[32 * i:32 * i + 32]) for i in range(count)]
    for i in range(0, count, 2):
        rows = dot(whole(fy_ref, columns=192), jnp.concatenate(columns[i:i + 2], 1))
        for j in range(min(2, count - i)):
            vo_ref[PAIRS[first + i + j]] = rows[:, 128 * j:128 * j + 128]


def prepare_rows(vo_ref, zt):
    for dy in (-1, 1):
        for q, rows in enumerate(states(lambda y: zt[:, y, :], dy)):
            for t in range(4):
                vo_ref[Y_STATES + 4 * q + t, Y_AT[dy]:Y_AT[dy] + 8, :] = rows[8 * t:8 * t + 8]


def split_y(p, halo, first, last):
    a, b, c, d = halo
    p0, p1, p2, p3 = p

    def following(v, edge):
        return jnp.where(last, edge, pltpu.roll(v, 7, 0))

    def preceding(v, edge):
        return jnp.where(first, edge, pltpu.roll(v, 1, 0))

    o0 = p1 + LIFT_A * (p0 + p2)
    o1 = p3 + LIFT_A * (p2 + following(p0, c))
    before = a + LIFT_A * p0
    e0 = p0 + LIFT_B * (preceding(o1, before) + o0)
    e1 = p2 + LIFT_B * (o0 + o1)
    q0 = o0 + LIFT_C * (e0 + e1)
    q1 = o1 + LIFT_C * (e1 + following(e0, d + LIFT_B * o1))
    before = before + LIFT_C * (b + LIFT_B * before + e0)
    f0 = e0 + LIFT_D * (preceding(q1, before) + q0)
    f1 = e1 + LIFT_D * (q0 + q1)
    return f0 * (1 / LIFT_K), q0 * LIFT_K, f1 * (1 / LIFT_K), q1 * LIFT_K


def exchange(nx, ny, nz, weights, late, v_hbm, zp_hbm, fy_hbm, z1_hbm, ty_hbm, te_hbm, zu_hbm, done,
             v_ref, vo_ref, vi_ref, ys_ref, zp_ref, fy_ref, z1_ref, ty_ref, te_ref, zu_ref, te_in, tl_in, e2_ref, e34_ref,
             zt, basis, sides, xh, up, xz, send, recv, hello, sems):
    x, y = lax.axis_index("gx"), lax.axis_index("gy")
    z = lax.rem(x, nz)

    def device(dx, dy):
        return lax.rem(x + dx + nx, nx), lax.rem(y + dy + ny, ny)

    copies, arriving = [], [0] * COUNTERS
    for dx, dy, is_states, (e, ne), (r, nr) in MOVES:
        at, k = (pl.ds(e, ne), pl.ds(r, nr)), counter(dx, is_states)
        arriving[k] += ne * nr
        copies.append((dx, dy, is_states, pltpu.make_async_remote_copy(
            src_ref=vo_ref.at[at], dst_ref=vi_ref.at[at], send_sem=send, recv_sem=recv.at[k],
            device_id=device(-dx, -dy), device_id_type=MESH)))

    def wait_rows(sem, rows):
        n, r = area(rows)
        some = vi_ref.at[pl.ds(0, n), pl.ds(0, r)]
        pltpu.make_async_copy(some, some, sem).wait()

    def start(which, kinds=(True, False)):
        for dx, _, is_states, copy in copies:
            if dx == which and is_states in kinds:
                copy.start()

    def start_ahead(kinds, waits):
        for dx, dy, is_states, copy in copies:
            if dx == -1 and is_states in kinds:
                if dy in (0, 1):
                    pl.when(((x == nx - 1) & (y == dy)) == waits)(copy.start)
                elif not waits:
                    copy.start()

    def arrive(k):
        wait_rows(recv.at[k], arriving[k])

    barrier = pltpu.get_barrier_semaphore()

    def greet(dx):
        for o in GROUP[dx]:
            pl.semaphore_signal(barrier, inc=1, device_id=device(*o), device_id_type=MESH)

    def say_hello(dx, dys):
        for dy in dys:
            pl.semaphore_signal(hello.at[dx - 1], inc=1, device_id=device(dx, dy), device_id_type=MESH)

    loads = [pltpu.make_async_copy(a, b, sems.at[(0, 1, 2, 3, 4, 4, 5, 5, 6, 7)[i]]) for i, (a, b) in enumerate(
        (*((v_hbm.at[:, pl.ds(8 * t, 8)], v_ref.at[:, pl.ds(8 * t, 8)]) for t in range(4)),
         (zp_hbm, zp_ref), (fy_hbm, fy_ref), (z1_hbm, z1_ref), (ty_hbm, ty_ref), (te_hbm, te_ref), (zu_hbm, zu_ref)))]
    for load in loads[:4]:
        load.start()
    pl.when(z != nz - 1)(lambda: greet(-1))
    greet(-2)
    loads[4].start()
    loads[5].start()

    @pl.when(z >= nz - 2)
    def _():
        pl.semaphore_wait(barrier, jnp.where(z == nz - 2, 5, 10))
        pl.when(z == nz - 1)(lambda: say_hello(1, range(-2, 3)))
        say_hello(2, range(-2, 3))

    @pl.when(z < nz - 2)
    def _():
        greet(0)
        pl.when(z < nz - 3)(lambda: greet(1))
        pl.when(z < nz - 4)(lambda: greet(2))

    for e, r, count in unsent():
        vi_ref[e, r:r + count, :] = jnp.zeros((count, 128), F32)
    for t in range(4):
        loads[t].wait()
        values = own_basis([v_ref[x, 8 * t:8 * t + 8, :] for x in range(32)])
        for i, value in enumerate(values):
            basis[i, t] = value
        for i in range(EARLY, len(PAIRS)):
            for h in (0, 1):
                sides[h, 4 * (i - EARLY) + t] = functional(2 * i + h, values, weights)
    prepare_states(-1, v_ref, vo_ref, xh)
    pl.when(z == nz - 1)(lambda: start_ahead((True,), False))
    wait_rows(sems.at[4], (zp_ref.size + fy_ref.size) // 256)
    prepare_pairs(EARLY, [sides[h].reshape(32 * (len(PAIRS) - EARLY), 128) for h in (0, 1)], zp_ref, fy_ref, vo_ref)

    @pl.when(z >= nz - 2)
    def _():
        start(-2)
        pl.when(z == nz - 1)(lambda: start_ahead((False,), False))

    for load in loads[6:]:
        load.start()
    prepare_states(1, v_ref, vo_ref, xh)
    early = [[functional(2 * i + h, [basis[k, t] for k in range(20)], weights) for i in range(EARLY) for t in range(4)] for h in (0, 1)]
    prepare_pairs(0, [jnp.concatenate(side, 0) for side in early], zp_ref, fy_ref, vo_ref)
    wait_rows(sems.at[5], (z1_ref.size + ty_ref.size) // 256)
    for t in range(4):
        zt[:, 8 * t:8 * t + 8, :] = wide_dot(v_ref[:, 8 * t:8 * t + 8, :].reshape(256, 128), z1_ref).reshape(32, 8, 128)
    prepare_rows(vo_ref, zt)

    @pl.when(z < nz - 2)
    def _():
        pl.semaphore_wait(barrier, jnp.where(z == 0, 14, jnp.where(z == 1, 19, 24)))

        @pl.when(z == nz - 3)
        def _():
            say_hello(1, (0,))
            say_hello(2, (0,))

        start(-2)
        pl.when(z > 1)(lambda: start(2))
        start(-1)
        pl.when(z > 0)(lambda: start(1))
        start(0)

    @pl.when(z == nz - 2)
    def _():
        pl.semaphore_wait(hello.at[0], 1)
        start(-1)

    @pl.when(z == nz - 1)
    def _():
        pl.semaphore_wait(hello.at[1], 1)
        start_ahead((True, False), True)

    @pl.when(z >= nz - 2)
    def _():
        start(2)
        start(1)
        start(0)

    sub = lax.broadcasted_iota(jnp.int32, (8, 128), 0)
    first, last = sub == 0, sub == 7

    def row(ref, e, r):
        return jnp.broadcast_to(ref[e, pl.ds(r, 1), :], (8, 128))

    def plane(x):
        p = [zt[x, pl.ds(r, 8, 4), :] for r in range(4)]
        halo = [row(vi_ref, Y_STATES + 4 * (k % 2) + x // 8, Y_AT[-1 if k < 2 else 1] + x % 8) for k in range(4)]
        for r, v in enumerate(split_y(p, halo, first, last)):
            ys_ref[x + 2, r] = v

    def state_planes(dx):
        e, side = X_STATES[dx], (dx + 1) // 2
        xz[side] = wide_dot(jnp.concatenate([vi_ref[e, 0:32, :], vi_ref[e + 1, 0:32, :], vi_ref[e, 32:48, :]], 0), z1_ref)
        for q in (0, 1):
            p = [xz[side, pl.ds(32 * q + r, 8, 4), :] for r in range(4)]
            halo = [row(xz, side, 64 + 8 * (k // 2) + 2 * (k % 2) + q) for k in range(4)]
            for r, v in enumerate(split_y(p, halo, first, last)):
                ys_ref[34 * side + q, r] = v

    def upper(first_pair, count, out_ref):
        done = []
        for i in range(first_pair, first_pair + count):
            e = PAIRS[i]
            v = vi_ref[e]
            own = vo_ref[e, 0:32, :] if i < COUNT[0] // 2 else jnp.concatenate([v[0:24], jnp.zeros((8, 128), F32)], 0)
            done.append(jnp.concatenate([own, v[32:]], 0))
        for i in range(0, count, 2):
            high, mid, low = split(jnp.concatenate(done[i:i + 2], 1))
            r = (dot(whole(ty_ref, 1, columns=192), jnp.concatenate([high, mid, high], 0))
                 + dot(whole(ty_ref, 0, columns=192), jnp.concatenate([high, mid, low], 0)))
            for j in range(min(2, count - i)):
                for t in range(4):
                    out_ref[t // 2, first_pair % EARLY + i + j, :, 128 * (t % 2):128 * (t % 2) + 128] = r[8 * t:8 * t + 8, 128 * j:128 * j + 128]

    arrive(0)
    for x in range(32):
        plane(x)
    upper(0, 10, te_in)

    arrive(1)
    state_planes(1)
    upper(10, 5, te_in)
    loads[8].wait()
    for u, (ref, at, rows) in enumerate(((e2_ref, 0, 128), (e34_ref, 128, 96))):
        high, mid, low = split(te_in[u].reshape(8 * EARLY, 256))
        high_mid, high_low = [jnp.concatenate([high, w], 0) for w in (mid, low)]
        m = [[whole(te_ref, k, h, rows=slice(at, at + rows), columns=240) for k in range(3)] for h in (0, 1)]
        v = [dot(m[h][2], high_low) + dot(m[h][1], high_mid) + dot(m[h][0], high_mid) for h in (0, 1)]
        ref[...] = jnp.where(lax.broadcasted_iota(jnp.int32, (rows, 256), 1) % 128 < 64, v[0], v[1])

    loads[9].wait()
    l2 = wide_dot(jnp.concatenate([e2_ref[:, :128], e2_ref[:, 128:]], 0), zu_ref, 0).reshape(2, 16, 8, 128)
    l3 = wide_dot(e34_ref[:64, :128], zu_ref, 1).reshape(8, 8, 128)
    l4 = wide_dot(e34_ref[64:, 128:], zu_ref, 2).reshape(4, 8, 128)
    for i in range(2, 16):
        for t in (0, 1):
            up[i, t] = merge(i, t, l2[t, i], l3, l4)
    lift_x(ys_ref, up, done)

    @pl.when(z < 2)
    def _():
        pl.semaphore_wait(hello.at[1], 5)
        start(2)

    @pl.when(z == 0)
    def _():
        pl.semaphore_wait(hello.at[0], 5)
        start(1)

    arrive(2)
    state_planes(-1)
    first_x(ys_ref, done)
    arrive(3)
    upper(15, 5, tl_in)

    half = lax.broadcasted_iota(jnp.int32, (8, 128), 1) < 64

    def changed(level, u, lanes, early):
        rows = []
        for i, pairs in enumerate(late[level]):
            terms = [jnp.where(half, *pair) * tl_in[u, p, :, lanes:lanes + 128] for p, pair in enumerate(pairs) if max(map(abs, pair)) > 1e-14]
            while len(terms) > 1:
                terms = [sum(terms[k:k + 2][1:], terms[k]) for k in range(0, len(terms), 2)]
            rows.append(early(8 * i) + terms[0])
        return rows

    l2 = [changed(0, 0, 128 * t, lambda r: e2_ref[r:r + 8, 128 * t:128 * t + 128]) for t in (0, 1)]
    l2 = wide_dot(jnp.concatenate(l2[0] + l2[1], 0), zu_ref, 0).reshape(2, LATE[0], 8, 128)
    l3 = wide_dot(jnp.concatenate(changed(1, 1, 0, lambda r: e34_ref[r:r + 8, :128]), 0), zu_ref, 1).reshape(LATE[1], 8, 128)
    l4 = wide_dot(jnp.concatenate(changed(2, 1, 128, lambda r: e34_ref[64 + r:72 + r, 128:]), 0), zu_ref, 2).reshape(LATE[2], 8, 128)
    odd_lane = lax.broadcasted_iota(jnp.int32, (8, 128), 1) % 2 == 1
    for i in range(2 * LATE[1]):
        for t in (0, 1):
            at = (i, 0, pl.ds(2 * t, 8, 4), slice(None))
            if i < LATE[0]:
                done[at] = jnp.where(odd_lane, done[at], merge(i, t, l2[t, i], l3, l4))
            elif i % 2 == 0 and t == 0:
                done[at] = merge(i, t, done[at], l3, l4)
    wait_rows(send, sum(arriving))


def merge(i, t, v, l3, l4):
    sub = lax.broadcasted_iota(jnp.int32, (8, 128), 0)
    lane = lax.broadcasted_iota(jnp.int32, (8, 128), 1)
    if i % 2 or t:
        return v
    w = l3[i // 2]
    if i % 4 == 0:
        w = jnp.where((lane % 8 == 0) & (sub % 2 == 0), l4[i // 4], w)
    return jnp.where(lane % 4 == 0, w, v)


def lift_x(ys, up, done):
    odd_lane = lax.broadcasted_iota(jnp.int32, (8, 128), 1) % 2 == 1
    state = {}
    for r in range(4):
        state[r] = (ys[3, r] + LIFT_A * (ys[2, r] + ys[4, r]), None, None)
    for i in range(1, 17):
        for r in range(4):
            o, e, q = state[r]
            if i < 16:
                p = ys[2 + 2 * i, r]
                o_now = ys[3 + 2 * i, r] + LIFT_A * (p + ys[4 + 2 * i, r])
                e_now = p + LIFT_B * (o + o_now)
            else:
                o_now, e_now = None, ys[35, r] + LIFT_B * o
            q_now = None
            if i > 1:
                q_now = o + LIFT_C * (e + e_now)
                done[i - 1, 1, pl.ds(r, 8, 4), :] = q_now * LIFT_K
            if i > 2:
                low = (e + LIFT_D * (q + q_now)) * (1 / LIFT_K)
                done[i - 1, 0, pl.ds(r, 8, 4), :] = low if r % 2 else jnp.where(odd_lane, low, up[i - 1, r // 2])
            state[r] = (o_now, e_now, q_now)


def first_x(ys, done):
    for r in range(4):
        o = [ys[0, r] + LIFT_A * ys[2, r], *(ys[3 + 2 * i, r] + LIFT_A * (ys[2 + 2 * i, r] + ys[4 + 2 * i, r]) for i in range(3))]
        e = [ys[1, r] + LIFT_B * o[0], *(ys[2 + 2 * i, r] + LIFT_B * (o[i] + o[i + 1]) for i in range(3))]
        q = [o[i] + LIFT_C * (e[i] + e[i + 1]) for i in range(3)]
        for i in range(2):
            done[i, 0, pl.ds(r, 8, 4), :] = (e[i + 1] + LIFT_D * (q[i] + q[i + 1])) * (1 / LIFT_K)
        done[0, 1, pl.ds(r, 8, 4), :] = q[1] * LIFT_K


def finish(done, out_ref, sem):
    for i in range(0, 16, 4):
        pltpu.make_async_copy(done.at[pl.ds(i, 4)], out_ref.at[pl.ds(i, 4)], sem).start()
    pltpu.make_async_copy(done, out_ref, sem).wait()


def solution(mesh):
    nx, ny = mesh.shape["gx"], mesh.shape["gy"]
    weights, late, (zp, fy, z1, ty, te, zu) = operators()
    vmem, hbm = pl.BlockSpec(memory_space=pltpu.VMEM), pl.BlockSpec(memory_space=pltpu.HBM)
    limit = 24 * 1024 * 1024
    block, pairs = (32, 32, 128), (16, 2, 32, 128)

    def kept(*ms):
        return [pltpu.with_memory_space_constraint(jnp.asarray(m), pltpu.HBM) for m in ms]

    def local(v):
        done = pl.pallas_call(
            functools.partial(exchange, nx, ny, 8, weights.tolist(), late),
            out_shape=pltpu.VMEM(pairs, F32),
            in_specs=[hbm] * 7, out_specs=vmem,
            scratch_shapes=[*(pltpu.VMEM(s, F32) for s in (block, (ENTRIES, ROWS, 128), (ENTRIES, ROWS, 128), (36, 4, 8, 128))),
                            *(pltpu.VMEM(m.shape, BF16) for m in (zp, fy, z1, ty, te, zu)),
                            *(pltpu.VMEM(s, F32) for s in ((2, EARLY, 8, 256), (2, len(PAIRS) - EARLY, 8, 256), (128, 256), (96, 256),
                                                           block, (20, 4, 8, 128), (2, 4 * (len(PAIRS) - EARLY), 8, 128), (2, 32, 128), (16, 2, 8, 128), (2, 80, 128))),
                            pltpu.SemaphoreType.DMA, pltpu.SemaphoreType.DMA((COUNTERS,)), pltpu.SemaphoreType.REGULAR((2,)), pltpu.SemaphoreType.DMA((8,))],
            compiler_params=pltpu.CompilerParams(collective_id=0, has_side_effects=True, vmem_limit_bytes=limit),
        )(*kept(v, zp, fy, z1, ty, te, zu))
        return pl.pallas_call(
            finish,
            out_shape=jax.ShapeDtypeStruct(pairs, F32),
            in_specs=[vmem], out_specs=pl.BlockSpec(memory_space=pl.ANY),
            scratch_shapes=[pltpu.SemaphoreType.DMA],
            compiler_params=pltpu.CompilerParams(vmem_limit_bytes=limit),
        )(done).reshape(block)

    spec = P("gx", "gy", None)
    return jax.shard_map(local, mesh=mesh, in_specs=(spec,), out_specs=spec, check_vma=False)
```

```python
import functools

import jax
import jax.numpy as jnp
import ml_dtypes
import numpy as np
from jax import lax
from jax.experimental import pallas as pl
from jax.experimental.pallas import tpu as pltpu
from jax.sharding import PartitionSpec as P

LIFT_A, LIFT_B, LIFT_C, LIFT_D = -1.586134342, -0.05298011854, 0.8829110762, 0.4435068522
LIFT_K = 1.149604398
MESH = pl.DeviceIdType.MESH
F32, BF16 = jnp.float32, jnp.bfloat16

COUNT = {0: 20, 1: 8, 2: 2, -1: 8, -2: 2}
X_AT = {0: 0, 1: 18, 2: 24, -1: 25, -2: 31}
Y_AT = {0: 0, -1: 32, 1: 40, -2: 48, 2: 56}
ENTRIES, ROWS = 32, 64
PAIRS = [X_AT[o] + p for o, c in COUNT.items() for p in range(c // 2)]
LATE = (5, 7, 4)
EARLY = 15
Y_STATES = 10
X_STATES = {1: 22, -1: 29}
OFFSETS = (0, -1, 1, -2, 2)
GROUP = {dx: [(dx, dy) for dy in (-2, 2, -1, 1, 0) if (dx, dy) != (0, 0)] for dx in OFFSETS}


def pieces(dx, dy):
    if dx == 0:
        return [(False, (0, 18), (Y_AT[dy], 8))] if abs(dy) == 1 else [(False, (0, 10), (Y_AT[dy], 2))]
    if abs(dx) == 2:
        return [(False, (X_AT[dx], 1), (Y_AT[dy], 2 if abs(dy) == 2 else 4))]
    if dy == 0:
        return [(True, (X_STATES[dx], 2), (0, 32)), (False, (X_AT[dx], 4), (0, 20))]
    if abs(dy) == 1:
        return [(True, (X_STATES[dx], 1), (Y_AT[dy], 4)), (False, (X_AT[dx], 4), (Y_AT[dy], 7))]
    return [(False, (X_AT[dx], 2), (Y_AT[dy], 2))]


MOVES = [(dx, dy, *piece) for dx in OFFSETS for dx, dy in GROUP[dx] for piece in pieces(dx, dy)]


def counter(dx, is_states):
    return 0 if dx == 0 else 1 if dx > 0 else 2 if is_states else 3


COUNTERS = 4


def area(rows):
    return next((rows // r, r) for r in range(ROWS, 0, -1) if rows % r == 0 and rows // r <= ENTRIES)


def unsent():
    sent = {(e, r) for _, _, _, (e0, ne), (r0, nr) in MOVES for e in range(e0, e0 + ne) for r in range(r0, r0 + nr)}
    out = [(e, Y_AT[dy] + 4, 4) for e in X_STATES.values() for dy in (-1, 1)]
    for e in PAIRS:
        for tile in range(32 if e < X_AT[1] else 0, ROWS, 8):
            count = sum((e, r) in sent for r in range(tile, tile + 8))
            if count < 8 and tile != 24:
                out.append((e, tile + count, 8 - count))
    return out


def lift_1d(v):
    even, odd = v[0::2], v[1::2]
    odd = odd + LIFT_A * (even + np.roll(even, -1, 0))
    even = even + LIFT_B * (np.roll(odd, 1, 0) + odd)
    odd = odd + LIFT_C * (even + np.roll(even, -1, 0))
    even = even + LIFT_D * (np.roll(odd, 1, 0) + odd)
    return even / LIFT_K, odd * LIFT_K


def interleave(low, high):
    out = np.empty((2 * low.shape[0], low.shape[1]))
    out[0::2], out[1::2] = low, high
    return out


def row_space(parts, count):
    basis = np.zeros((0, parts[0].shape[1]))
    for part in parts:
        rest = part - part @ basis.T @ basis
        size, rows = np.linalg.svd(rest)[1:]
        basis = np.concatenate([basis, rows[:int((size > 1e-9).sum())]])
    return np.concatenate([basis, np.zeros((count - len(basis), basis.shape[1]))])


def thirds(matrix):
    out, rest = [], np.asarray(matrix, np.float64)
    for _ in range(3):
        out.append(rest.astype(ml_dtypes.bfloat16))
        rest = rest - out[-1].astype(np.float64)
    return out


def operators():
    n, blocks, mid = 32, 16, 8
    low, levels = np.eye(n * blocks), {}
    for level in range(1, 5):
        low, high = lift_1d(low)
        m = n >> level
        levels[level] = interleave(low[mid * m:(mid + 1) * m], high[mid * m:(mid + 1) * m])
    functional, combine = {}, {}
    for offset, count in COUNT.items():
        parts = [levels[level][:, (mid + offset) * n:(mid + offset + 1) * n] for level in (4, 3, 2)]
        functional[offset] = row_space(parts, count)
        combine[offset] = np.concatenate(parts[::-1])
    basis = np.stack(own_basis(np.eye(n)))
    inverse = np.linalg.pinv(basis)
    weights = np.concatenate([functional[o] @ inverse for o in COUNT if o])
    cx = [np.concatenate([(combine[o] @ (functional[o].T if o else inverse))[:, h::2] for o in COUNT], 1) for h in (0, 1)]
    late = [[[tuple(c[at + i, p] for c in cx) for p in range(EARLY, len(PAIRS))] for i in range(count)] for at, count in zip((0, 16, 24), LATE)]
    assert all(np.abs(c[at + count:end, EARLY:]).max(initial=0) < 1e-12 for c in cx for at, count, end in zip((0, 16, 24), LATE, (16, 24, 28)))
    early = np.stack([np.kron(c[:, :EARLY], np.eye(8)) for c in cx])
    high, mid_, low = thirds(early)
    early = np.stack([np.concatenate(m, 2) for m in ((high, high), (mid_, mid_), (low, high))])
    fy, cy = np.zeros((ROWS, 32)), np.zeros((28, ROWS))
    for offset, count in COUNT.items():
        at = Y_AT[offset]
        fy[at:at + count], cy[:, at:at + count] = functional[offset], combine[offset] @ functional[offset].T
    ty = np.zeros((32, ROWS))
    ty[0:8], ty[8:16], ty[16:24], ty[24:32:2] = cy[0:16:2], cy[1:16:2], cy[16:24], cy[24:28]
    high, mid_, low = thirds(fy)
    fy = np.concatenate([high, high, high, mid_, mid_, low], 1)
    high, mid_, low = thirds(ty)
    ty = np.stack([np.concatenate(m, 1) for m in ((high, high, high), (mid_, mid_, low))])
    low, high = lift_1d(np.eye(128))
    z1 = wide(interleave(low, high).T)
    zp = np.concatenate(thirds(np.kron(np.eye(2), low.T)), 1)
    low, zu = np.eye(64), np.zeros((3, 64, 128))
    for level in range(3):
        low, high = lift_1d(low)
        zu[level, :, ::2 << level] = interleave(low, high).T
    zu = np.stack([wide(np.concatenate([m, m])) for m in zu])
    return weights, late, [tiles(m) for m in (zp, fy, z1, ty, early, zu)]


def wide(matrix):
    high, mid, low = thirds(matrix)
    return np.concatenate([np.concatenate(m) for m in ((high, high), (mid, mid), (low, high))], 1)


def tiles(matrix):
    columns = -(-matrix.shape[-1] // 128) * 128
    padded = np.zeros((*matrix.shape[:-1], columns), matrix.dtype)
    padded[..., :matrix.shape[-1]] = matrix
    return np.moveaxis(padded.reshape(*matrix.shape[:-1], columns // 128, 128), -2, -3)


def whole(ref, *at, rows=slice(None), columns=None):
    count = ref.shape[len(at)]
    out = ref[(*at, 0, rows)] if count == 1 else jnp.concatenate([ref[(*at, i, rows)] for i in range(count)], 1)
    return out if columns is None else out[:, :columns]


def dot(a, b):
    return lax.dot_general(a, b, (((1,), (0,)), ((), ())), preferred_element_type=F32)


def split(v):
    high = v.astype(BF16)
    rest = v - high.astype(F32)
    mid = rest.astype(BF16)
    return high, mid, (rest - mid.astype(F32)).astype(BF16)


def stacked(v):
    high, mid, low = split(v)
    return jnp.concatenate([high, mid, low, high, mid, high], 0)


def wide_dot(v, ref, *at):
    high, mid, low = split(v)
    m = whole(ref, *at)
    n = m.shape[1] // 3
    v = dot(jnp.concatenate([high, mid], 1), m[:, :2 * n])
    return dot(jnp.concatenate([high, low], 1), m[:, 2 * n:]) + v[:, n:] + v[:, :n]


def states(s, side):
    if side < 0:
        return s(31) + LIFT_A * s(30), s(30) + LIFT_B * (s(29) + LIFT_A * (s(28) + s(30)))
    return s(0), s(0) + LIFT_B * (s(1) + LIFT_A * (s(0) + s(2)))


def own_basis(v):
    out, odd, even, odd3 = [], 0.0, 0.0, 0.0
    for i in range(17):
        if i < 16:
            after = v[2 * i + 2] if i < 15 else 0.0
            odd_now = v[2 * i + 1] + LIFT_A * (v[2 * i] + after)
            even_now = v[2 * i] + LIFT_B * (odd + odd_now)
        else:
            odd_now, even_now = None, LIFT_B * odd
        if i > 0:
            odd3_now = odd + LIFT_C * (even + even_now)
            out.append(even + LIFT_D * (odd3 + odd3_now))
            odd3 = odd3_now
        odd, even = odd_now, even_now
    return [*out, *states(lambda i: v[i], -1), *states(lambda i: v[i], 1)]


def prepare_states(dx, v_ref, vo_ref, xh):
    e = X_STATES[dx]
    for q, plane in enumerate(states(lambda x: v_ref[x], dx)):
        xh[q] = plane
        vo_ref[e + q, 0:32, :] = plane
    for dy in (-1, 1):
        at = Y_AT[dy]
        for p, rows in enumerate(states(lambda y: xh[:, y, :], dy)):
            vo_ref[e, at + 2 * p:at + 2 * p + 2, :] = rows
        vo_ref[e, at + 4:at + 8, :] = jnp.zeros((4, 128), F32)


def functional(f, values, weights):
    if f < 20:
        return values[f]
    terms = [w * value for w, value in zip(weights[f - 20], values) if abs(w) > 1e-14]
    while len(terms) > 1:
        terms = [sum(terms[k:k + 2][1:], terms[k]) for k in range(0, len(terms), 2)]
    return terms[0] if terms else jnp.zeros((8, 128), F32)


def prepare_pairs(first, sides, zp_ref, fy_ref, vo_ref):
    high, mid, low = split(jnp.concatenate(sides, 1))
    m = whole(zp_ref)
    packed = dot(high, m[:, :256]) + dot(mid, m[:, :256])
    packed = dot(low, m[:, :128]) + dot(high, m[:, 256:]) + packed[:, 128:] + packed[:, :128]
    count = packed.shape[0] // 32
    columns = [stacked(packed[32 * i:32 * i + 32]) for i in range(count)]
    for i in range(0, count, 2):
        rows = dot(whole(fy_ref, columns=192), jnp.concatenate(columns[i:i + 2], 1))
        for j in range(min(2, count - i)):
            vo_ref[PAIRS[first + i + j]] = rows[:, 128 * j:128 * j + 128]


def prepare_rows(vo_ref, zt):
    for dy in (-1, 1):
        for q, rows in enumerate(states(lambda y: zt[:, y, :], dy)):
            for t in range(4):
                vo_ref[Y_STATES + 4 * q + t, Y_AT[dy]:Y_AT[dy] + 8, :] = rows[8 * t:8 * t + 8]


def split_y(p, halo, first, last):
    a, b, c, d = halo
    p0, p1, p2, p3 = p

    def following(v, edge):
        return jnp.where(last, edge, pltpu.roll(v, 7, 0))

    def preceding(v, edge):
        return jnp.where(first, edge, pltpu.roll(v, 1, 0))

    o0 = p1 + LIFT_A * (p0 + p2)
    o1 = p3 + LIFT_A * (p2 + following(p0, c))
    before = a + LIFT_A * p0
    e0 = p0 + LIFT_B * (preceding(o1, before) + o0)
    e1 = p2 + LIFT_B * (o0 + o1)
    q0 = o0 + LIFT_C * (e0 + e1)
    q1 = o1 + LIFT_C * (e1 + following(e0, d + LIFT_B * o1))
    before = before + LIFT_C * (b + LIFT_B * before + e0)
    f0 = e0 + LIFT_D * (preceding(q1, before) + q0)
    f1 = e1 + LIFT_D * (q0 + q1)
    return f0 * (1 / LIFT_K), q0 * LIFT_K, f1 * (1 / LIFT_K), q1 * LIFT_K


def exchange(nx, ny, nz, weights, late, v_hbm, zp_hbm, fy_hbm, z1_hbm, ty_hbm, te_hbm, zu_hbm, done,
             v_ref, vo_ref, vi_ref, ys_ref, zp_ref, fy_ref, z1_ref, ty_ref, te_ref, zu_ref, te_in, tl_in, e2_ref, e34_ref,
             zt, basis, sides, xh, up, xz, send, recv, hello, sems):
    x, y = lax.axis_index("gx"), lax.axis_index("gy")
    z = lax.rem(x, nz)

    def device(dx, dy):
        return lax.rem(x + dx + nx, nx), lax.rem(y + dy + ny, ny)

    copies, arriving = [], [0] * COUNTERS
    for dx, dy, is_states, (e, ne), (r, nr) in MOVES:
        at, k = (pl.ds(e, ne), pl.ds(r, nr)), counter(dx, is_states)
        arriving[k] += ne * nr
        copies.append((dx, dy, is_states, pltpu.make_async_remote_copy(
            src_ref=vo_ref.at[at], dst_ref=vi_ref.at[at], send_sem=send, recv_sem=recv.at[k],
            device_id=device(-dx, -dy), device_id_type=MESH)))

    def wait_rows(sem, rows):
        n, r = area(rows)
        some = vi_ref.at[pl.ds(0, n), pl.ds(0, r)]
        pltpu.make_async_copy(some, some, sem).wait()

    def start(which, kinds=(True, False)):
        for dx, _, is_states, copy in copies:
            if dx == which and is_states in kinds:
                copy.start()

    def start_ahead(kinds, waits):
        for dx, dy, is_states, copy in copies:
            if dx == -1 and is_states in kinds:
                if dy in (0, 1):
                    pl.when(((x == nx - 1) & (y == dy)) == waits)(copy.start)
                elif not waits:
                    copy.start()

    def arrive(k):
        wait_rows(recv.at[k], arriving[k])

    barrier = pltpu.get_barrier_semaphore()

    def greet(dx):
        for o in GROUP[dx]:
            pl.semaphore_signal(barrier, inc=1, device_id=device(*o), device_id_type=MESH)

    def say_hello(dx, dys):
        for dy in dys:
            pl.semaphore_signal(hello, inc=1, device_id=device(dx, dy), device_id_type=MESH)

    loads = [pltpu.make_async_copy(a, b, sems.at[(0, 1, 2, 3, 4, 4, 5, 5, 6, 7)[i]]) for i, (a, b) in enumerate(
        (*((v_hbm.at[:, pl.ds(8 * t, 8)], v_ref.at[:, pl.ds(8 * t, 8)]) for t in range(4)),
         (zp_hbm, zp_ref), (fy_hbm, fy_ref), (z1_hbm, z1_ref), (ty_hbm, ty_ref), (te_hbm, te_ref), (zu_hbm, zu_ref)))]
    for load in loads[:4]:
        load.start()
    pl.when(z != nz - 1)(lambda: greet(-1))
    greet(-2)
    loads[4].start()
    loads[5].start()

    @pl.when(z >= nz - 2)
    def _():
        pl.semaphore_wait(barrier, jnp.where(z == nz - 2, 5, 10))
        pl.when(z == nz - 1)(lambda: say_hello(1, range(-2, 3)))
        say_hello(2, range(-2, 3))

    @pl.when(z < nz - 2)
    def _():
        greet(0)
        pl.when(z < nz - 3)(lambda: greet(1))
        pl.when(z < nz - 4)(lambda: greet(2))

    for e, r, count in unsent():
        vi_ref[e, r:r + count, :] = jnp.zeros((count, 128), F32)
    for t in range(4):
        loads[t].wait()
        values = own_basis([v_ref[x, 8 * t:8 * t + 8, :] for x in range(32)])
        for i, value in enumerate(values):
            basis[i, t] = value
        for i in range(EARLY, len(PAIRS)):
            for h in (0, 1):
                sides[h, 4 * (i - EARLY) + t] = functional(2 * i + h, values, weights)
    prepare_states(-1, v_ref, vo_ref, xh)
    pl.when(z == nz - 1)(lambda: start_ahead((True,), False))
    wait_rows(sems.at[4], (zp_ref.size + fy_ref.size) // 256)
    prepare_pairs(EARLY, [sides[h].reshape(32 * (len(PAIRS) - EARLY), 128) for h in (0, 1)], zp_ref, fy_ref, vo_ref)

    @pl.when(z >= nz - 2)
    def _():
        start(-2)
        pl.when(z == nz - 1)(lambda: start_ahead((False,), False))

    for load in loads[6:]:
        load.start()
    prepare_states(1, v_ref, vo_ref, xh)
    early = [[functional(2 * i + h, [basis[k, t] for k in range(20)], weights) for i in range(EARLY) for t in range(4)] for h in (0, 1)]
    prepare_pairs(0, [jnp.concatenate(side, 0) for side in early], zp_ref, fy_ref, vo_ref)
    wait_rows(sems.at[5], (z1_ref.size + ty_ref.size) // 256)
    for t in range(4):
        zt[:, 8 * t:8 * t + 8, :] = wide_dot(v_ref[:, 8 * t:8 * t + 8, :].reshape(256, 128), z1_ref).reshape(32, 8, 128)
    prepare_rows(vo_ref, zt)

    @pl.when(z < nz - 2)
    def _():
        pl.semaphore_wait(barrier, jnp.where(z == 0, 14, jnp.where(z == 1, 19, 24)))

        @pl.when(z == nz - 3)
        def _():
            say_hello(1, (0,))
            say_hello(2, (0,))

        start(-2)
        pl.when(z > 1)(lambda: start(2))
        start(-1)
        pl.when(z > 0)(lambda: start(1))
        start(0)

    @pl.when(z == nz - 2)
    def _():
        pl.semaphore_wait(hello, 1)
        start(-1)

    @pl.when(z == nz - 1)
    def _():
        pl.semaphore_wait(hello, 1)
        start_ahead((True, False), True)

    @pl.when(z >= nz - 2)
    def _():
        start(2)
        start(1)
        start(0)

    sub = lax.broadcasted_iota(jnp.int32, (8, 128), 0)
    first, last = sub == 0, sub == 7

    def row(ref, e, r):
        return jnp.broadcast_to(ref[e, pl.ds(r, 1), :], (8, 128))

    def plane(x):
        p = [zt[x, pl.ds(r, 8, 4), :] for r in range(4)]
        halo = [row(vi_ref, Y_STATES + 4 * (k % 2) + x // 8, Y_AT[-1 if k < 2 else 1] + x % 8) for k in range(4)]
        for r, v in enumerate(split_y(p, halo, first, last)):
            ys_ref[x + 2, r] = v

    def state_planes(dx):
        e, side = X_STATES[dx], (dx + 1) // 2
        xz[side] = wide_dot(jnp.concatenate([vi_ref[e, 0:32, :], vi_ref[e + 1, 0:32, :], vi_ref[e, 32:48, :]], 0), z1_ref)
        for q in (0, 1):
            p = [xz[side, pl.ds(32 * q + r, 8, 4), :] for r in range(4)]
            halo = [row(xz, side, 64 + 8 * (k // 2) + 2 * (k % 2) + q) for k in range(4)]
            for r, v in enumerate(split_y(p, halo, first, last)):
                ys_ref[34 * side + q, r] = v

    def upper(first_pair, count, out_ref):
        done = []
        for i in range(first_pair, first_pair + count):
            e = PAIRS[i]
            v = vi_ref[e]
            own = vo_ref[e, 0:32, :] if i < COUNT[0] // 2 else jnp.concatenate([v[0:24], jnp.zeros((8, 128), F32)], 0)
            done.append(jnp.concatenate([own, v[32:]], 0))
        for i in range(0, count, 2):
            high, mid, low = split(jnp.concatenate(done[i:i + 2], 1))
            r = (dot(whole(ty_ref, 1, columns=192), jnp.concatenate([high, mid, high], 0))
                 + dot(whole(ty_ref, 0, columns=192), jnp.concatenate([high, mid, low], 0)))
            for j in range(min(2, count - i)):
                for t in range(4):
                    out_ref[t // 2, first_pair % EARLY + i + j, :, 128 * (t % 2):128 * (t % 2) + 128] = r[8 * t:8 * t + 8, 128 * j:128 * j + 128]

    arrive(0)
    for x in range(32):
        plane(x)
    upper(0, 10, te_in)

    arrive(1)
    state_planes(1)
    upper(10, 5, te_in)
    loads[8].wait()
    for u, (ref, at, rows) in enumerate(((e2_ref, 0, 128), (e34_ref, 128, 96))):
        high, mid, low = split(te_in[u].reshape(8 * EARLY, 256))
        high_mid, high_low = [jnp.concatenate([high, w], 0) for w in (mid, low)]
        m = [[whole(te_ref, k, h, rows=slice(at, at + rows), columns=240) for k in range(3)] for h in (0, 1)]
        v = [dot(m[h][2], high_low) + dot(m[h][1], high_mid) + dot(m[h][0], high_mid) for h in (0, 1)]
        ref[...] = jnp.where(lax.broadcasted_iota(jnp.int32, (rows, 256), 1) % 128 < 64, v[0], v[1])

    loads[9].wait()
    l2 = wide_dot(jnp.concatenate([e2_ref[:, :128], e2_ref[:, 128:]], 0), zu_ref, 0).reshape(2, 16, 8, 128)
    l3 = wide_dot(e34_ref[:64, :128], zu_ref, 1).reshape(8, 8, 128)
    l4 = wide_dot(e34_ref[64:, 128:], zu_ref, 2).reshape(4, 8, 128)
    for i in range(2, 16):
        for t in (0, 1):
            up[i, t] = merge(i, t, l2[t, i], l3, l4)
    lift_x(ys_ref, up, done)

    @pl.when(z < 2)
    def _():
        pl.semaphore_wait(hello, jnp.where(z == 0, 10, 5))
        start(2)
        pl.when(z == 0)(lambda: start(1))

    arrive(2)
    state_planes(-1)
    first_x(ys_ref, done)
    arrive(3)
    upper(15, 5, tl_in)

    half = lax.broadcasted_iota(jnp.int32, (8, 128), 1) < 64

    def changed(level, u, lanes, early):
        rows = []
        for i, pairs in enumerate(late[level]):
            terms = [jnp.where(half, *pair) * tl_in[u, p, :, lanes:lanes + 128] for p, pair in enumerate(pairs) if max(map(abs, pair)) > 1e-14]
            while len(terms) > 1:
                terms = [sum(terms[k:k + 2][1:], terms[k]) for k in range(0, len(terms), 2)]
            rows.append(early(8 * i) + terms[0])
        return rows

    l2 = [changed(0, 0, 128 * t, lambda r: e2_ref[r:r + 8, 128 * t:128 * t + 128]) for t in (0, 1)]
    l2 = wide_dot(jnp.concatenate(l2[0] + l2[1], 0), zu_ref, 0).reshape(2, LATE[0], 8, 128)
    l3 = wide_dot(jnp.concatenate(changed(1, 1, 0, lambda r: e34_ref[r:r + 8, :128]), 0), zu_ref, 1).reshape(LATE[1], 8, 128)
    l4 = wide_dot(jnp.concatenate(changed(2, 1, 128, lambda r: e34_ref[64 + r:72 + r, 128:]), 0), zu_ref, 2).reshape(LATE[2], 8, 128)
    odd_lane = lax.broadcasted_iota(jnp.int32, (8, 128), 1) % 2 == 1
    for i in range(2 * LATE[1]):
        for t in (0, 1):
            at = (i, 0, pl.ds(2 * t, 8, 4), slice(None))
            if i < LATE[0]:
                done[at] = jnp.where(odd_lane, done[at], merge(i, t, l2[t, i], l3, l4))
            elif i % 2 == 0 and t == 0:
                done[at] = merge(i, t, done[at], l3, l4)
    wait_rows(send, sum(arriving))


def merge(i, t, v, l3, l4):
    sub = lax.broadcasted_iota(jnp.int32, (8, 128), 0)
    lane = lax.broadcasted_iota(jnp.int32, (8, 128), 1)
    if i % 2 or t:
        return v
    w = l3[i // 2]
    if i % 4 == 0:
        w = jnp.where((lane % 8 == 0) & (sub % 2 == 0), l4[i // 4], w)
    return jnp.where(lane % 4 == 0, w, v)


def lift_x(ys, up, done):
    odd_lane = lax.broadcasted_iota(jnp.int32, (8, 128), 1) % 2 == 1
    state = {}
    for r in range(4):
        state[r] = (ys[3, r] + LIFT_A * (ys[2, r] + ys[4, r]), None, None)
    for i in range(1, 17):
        for r in range(4):
            o, e, q = state[r]
            if i < 16:
                p = ys[2 + 2 * i, r]
                o_now = ys[3 + 2 * i, r] + LIFT_A * (p + ys[4 + 2 * i, r])
                e_now = p + LIFT_B * (o + o_now)
            else:
                o_now, e_now = None, ys[35, r] + LIFT_B * o
            q_now = None
            if i > 1:
                q_now = o + LIFT_C * (e + e_now)
                done[i - 1, 1, pl.ds(r, 8, 4), :] = q_now * LIFT_K
            if i > 2:
                low = (e + LIFT_D * (q + q_now)) * (1 / LIFT_K)
                done[i - 1, 0, pl.ds(r, 8, 4), :] = low if r % 2 else jnp.where(odd_lane, low, up[i - 1, r // 2])
            state[r] = (o_now, e_now, q_now)


def first_x(ys, done):
    for r in range(4):
        o = [ys[0, r] + LIFT_A * ys[2, r], *(ys[3 + 2 * i, r] + LIFT_A * (ys[2 + 2 * i, r] + ys[4 + 2 * i, r]) for i in range(3))]
        e = [ys[1, r] + LIFT_B * o[0], *(ys[2 + 2 * i, r] + LIFT_B * (o[i] + o[i + 1]) for i in range(3))]
        q = [o[i] + LIFT_C * (e[i] + e[i + 1]) for i in range(3)]
        for i in range(2):
            done[i, 0, pl.ds(r, 8, 4), :] = (e[i + 1] + LIFT_D * (q[i] + q[i + 1])) * (1 / LIFT_K)
        done[0, 1, pl.ds(r, 8, 4), :] = q[1] * LIFT_K


def finish(done, out_ref, sem):
    for i in range(0, 16, 4):
        pltpu.make_async_copy(done.at[pl.ds(i, 4)], out_ref.at[pl.ds(i, 4)], sem).start()
    pltpu.make_async_copy(done, out_ref, sem).wait()


def solution(mesh):
    nx, ny = mesh.shape["gx"], mesh.shape["gy"]
    weights, late, (zp, fy, z1, ty, te, zu) = operators()
    vmem, hbm = pl.BlockSpec(memory_space=pltpu.VMEM), pl.BlockSpec(memory_space=pltpu.HBM)
    limit = 24 * 1024 * 1024
    block, pairs = (32, 32, 128), (16, 2, 32, 128)

    def kept(*ms):
        return [pltpu.with_memory_space_constraint(jnp.asarray(m), pltpu.HBM) for m in ms]

    def local(v):
        done = pl.pallas_call(
            functools.partial(exchange, nx, ny, 8, weights.tolist(), late),
            out_shape=pltpu.VMEM(pairs, F32),
            in_specs=[hbm] * 7, out_specs=vmem,
            scratch_shapes=[*(pltpu.VMEM(s, F32) for s in (block, (ENTRIES, ROWS, 128), (ENTRIES, ROWS, 128), (36, 4, 8, 128))),
                            *(pltpu.VMEM(m.shape, BF16) for m in (zp, fy, z1, ty, te, zu)),
                            *(pltpu.VMEM(s, F32) for s in ((2, EARLY, 8, 256), (2, len(PAIRS) - EARLY, 8, 256), (128, 256), (96, 256),
                                                           block, (20, 4, 8, 128), (2, 4 * (len(PAIRS) - EARLY), 8, 128), (2, 32, 128), (16, 2, 8, 128), (2, 80, 128))),
                            pltpu.SemaphoreType.DMA, pltpu.SemaphoreType.DMA((COUNTERS,)), pltpu.SemaphoreType.REGULAR, pltpu.SemaphoreType.DMA((8,))],
            compiler_params=pltpu.CompilerParams(collective_id=0, has_side_effects=True, vmem_limit_bytes=limit),
        )(*kept(v, zp, fy, z1, ty, te, zu))
        return pl.pallas_call(
            finish,
            out_shape=jax.ShapeDtypeStruct(pairs, F32),
            in_specs=[vmem], out_specs=pl.BlockSpec(memory_space=pl.ANY),
            scratch_shapes=[pltpu.SemaphoreType.DMA],
            compiler_params=pltpu.CompilerParams(vmem_limit_bytes=limit),
        )(done).reshape(block)

    spec = P("gx", "gy", None)
    return jax.shard_map(local, mesh=mesh, in_specs=(spec,), out_specs=spec, check_vma=False)
```
